32 devices in a mesh: enc: 8 (over y, x, core), rep: 4 (over z).
Axes of the slice: x: 2, y: 2, z: 4, core: 2. Of those that a mesh axis runs over, the one named last changes fastest.
Arguments:
- pixels: bfloat16 [4096, 1280], P(('enc', 'rep')), may hold values from -6 to 6
- window_owner: int32 [256], P(('enc', 'rep')), may hold values from 0 to 7, as said below
- window_len: int32 [256], P(('enc', 'rep')), may hold values from 4 to 16, as said below
- slot_token: int32 [5120], P(('enc', 'rep')), may hold values from -1 to 31, as said below
- cotangent: bfloat16 [5120, 5120], P(('enc', 'rep')), may hold values from -6 to 6
- w_qkv: bfloat16 [1280, 1920], replicated
- w_out: bfloat16 [640, 1280], replicated, may hold values from -0.25 to 0.25
- gain: float32 [1280], replicated, may hold values from 0.1 to 1.9
Outputs:
- embeddings: bfloat16 [5120, 5120], P(('enc', 'rep'))
- grad_w_out: float32 [640, 1280], P('enc')
The draws below stay inside these ranges and needn't reach their ends.
Inputs may be any that keep to these rules, and one draw needn't show every extreme that they name: `window_owner`: the 8 windows of one device name distinct owners, taken in the device's own rep group; in each rep group one owner is named by a window of every device. `window_len`: A multiple of 4. `slot_token`: on the device of enc index o and rep index r, the value 4 * s + m names merged token m of the window that the device of enc index s and rep index r sends to o. Each such value appears exactly once, for every m < window_len / 4 of that window and for no other m; -1 marks other tokens. The merged tokens of one window stand in consecutive rows in order, wrapping around at the end of the device's rows.
All inputs are finite; a program needn't handle non-finite values.
Results may differ from the reference program's by a relative error of at most 0.012.
The reference program's roundings to bfloat16 on the way count: a program that leaves them out, or rounds other values in their place, can miss the bound.
Values may be sent and summed in bfloat16 or wider, within the bound.
No kernel may reach another device: no remote copies, remote signals or barrier semaphores. Data moves between devices by JAX's collectives and lax.ppermute only.
A program may use at most 64 MiB of HBM per device.

```python
import math
import jax
import jax.numpy as jnp
from jax import lax

D = 1280
HD = 80
HEADS = 8
WIN = 16
MERGE = 4
LW = 8
TOK_DEV = 160
HW = 640
TPW = 4
OWNERS = 8
REPLICAS = 4
PATCHES = 4096
TOKENS = 5120


def routing_plan(key):
    base_key = jax.random.fold_in(key, 7331)
    key_hot, key_own, key_len, key_order, key_offset = jax.random.split(base_key, 5)
    hottest = jax.random.randint(key_hot, (REPLICAS,), 0, OWNERS).astype(jnp.int32)
    loader_keys = jax.random.split(key_own, OWNERS * REPLICAS)

    def pick_owners(loader_key, hot_owner):
        first_key, second_key = jax.random.split(loader_key)
        others = jax.random.permutation(first_key, OWNERS - 1).astype(jnp.int32)
        others = others + (others >= hot_owner).astype(jnp.int32)
        chosen = jnp.concatenate([hot_owner[None], others[:LW - 1]])
        shuffle = jax.random.permutation(second_key, LW)
        return chosen[shuffle]
    hot_each = jnp.broadcast_to(hottest[None, :], (OWNERS, REPLICAS)).reshape(-1)
    owners = jax.vmap(pick_owners)(loader_keys, hot_each).reshape(OWNERS, REPLICAS, LW)
    lengths = jax.random.randint(key_len, (OWNERS, REPLICAS, LW), 1, TPW + 1).astype(jnp.int32) * MERGE
    owner_ids = jnp.arange(OWNERS, dtype=jnp.int32)
    matches = (owners[None, :, :, :] == owner_ids[:, None, None, None]).astype(jnp.int32)
    length_at = jnp.transpose(jnp.sum(matches * lengths[None], axis=-1), (0, 2, 1))
    order_keys = jax.random.split(key_order, OWNERS * REPLICAS)
    segment_order = jax.vmap(lambda order_key: jax.random.permutation(order_key, OWNERS))(order_keys)
    segment_order = segment_order.reshape(OWNERS, REPLICAS, OWNERS).astype(jnp.int32)
    offset = jax.random.randint(key_offset, (OWNERS, REPLICAS, 1), 0, TOK_DEV).astype(jnp.int32)
    rows_here = jnp.arange(TOK_DEV, dtype=jnp.int32)[None, None, :]
    shifted = (rows_here - offset) % TOK_DEV
    inside = shifted < TPW * OWNERS
    segment = jnp.minimum(shifted // TPW, OWNERS - 1)
    source = jnp.take_along_axis(segment_order, segment, axis=2)
    token_part = shifted % TPW
    live_length = jnp.take_along_axis(length_at, source, axis=2)
    alive = jnp.logical_and(inside, token_part * MERGE < live_length)
    slot_table = jnp.where(alive, TPW * source + token_part, -1).astype(jnp.int32)
    return (owners, lengths, slot_table)


def draw_window_owner(key, part):
    return routing_plan(key)[0].reshape(-1)


def draw_window_len(key, part):
    return routing_plan(key)[1].reshape(-1)


def draw_slot_token(key, part):
    return routing_plan(key)[2].reshape(-1)


def draw_w_qkv(key, part):
    first_key = jax.random.fold_in(jax.random.fold_in(key, 911), 0)
    matrix = jax.random.normal(first_key, (D, 3 * HW), jnp.float32) / jnp.sqrt(jnp.float32(D))
    return matrix.astype(jnp.bfloat16)


def block_levels(rng, dims, cuts, low, largest):
    def one(dim, blocks):
        draws = jax.random.uniform(jax.random.fold_in(jax.random.fold_in(rng, 6), dim), (blocks,), jnp.float32, low / len(cuts), largest / len(cuts))
        return jnp.repeat(jnp.exp(draws), dims[dim] // blocks).reshape((-1,) + (1,) * (len(dims) - dim - 1))

    level = one(*cuts[0])
    for cut in cuts[1:]:
        level = level * one(*cut)
    return level


def centred(rng, shape, deviation, bound, pieces=(), kind=jnp.bfloat16):
    level = block_levels(rng, shape, pieces, -0.22, 0.18) if pieces else 1.0
    result = jax.random.normal(rng, shape, jnp.float32) * deviation * level
    return jnp.minimum(jnp.maximum(result, -bound), bound).astype(kind)


def setup_inputs(seed: int = 0) -> dict:
    seeds = jax.random.split(jax.random.key(seed), 9)
    pixels = centred(seeds[0], (PATCHES, D), 1.0, 6.0, ((0, 32),))
    window_owner = draw_window_owner(jax.random.fold_in(seeds[8], 71), 0)
    window_len = draw_window_len(jax.random.fold_in(seeds[8], 71), 0)
    slot_token = draw_slot_token(jax.random.fold_in(seeds[8], 71), 0)
    cotangent = centred(seeds[4], (TOKENS, MERGE * D), 1.0, 6.0, ((0, 32),))
    w_qkv = draw_w_qkv(jax.random.fold_in(seeds[8], 71), 0)
    w_out = centred(seeds[6], (HW, D), HW ** -0.5, 0.25)
    gain = jnp.clip(1.0 + 0.18 * jax.random.normal(seeds[7], (D,), jnp.float32), 0.1, 1.9)
    return dict(pixels=pixels, window_owner=window_owner, window_len=window_len, slot_token=slot_token, cotangent=cotangent, w_qkv=w_qkv, w_out=w_out, gain=gain)


def normalize(inputs, gain):
    values = inputs.astype(jnp.float32)
    mean_square = lax.optimization_barrier(jnp.mean(values * values, axis=-1, keepdims=True))
    return (values * lax.rsqrt(mean_square + 1e-06) * gain).astype(jnp.bfloat16)

def encode(windows, lengths, w_qkv, w_out, gain):
    number, window_size, feature_width = windows.shape
    inner_width = w_out.shape[0]
    flat_rows = windows.reshape(number * window_size, feature_width)
    normed = normalize(flat_rows, gain)
    projected = jnp.dot(normed.astype(jnp.float32), w_qkv.astype(jnp.float32), preferred_element_type=jnp.float32).astype(jnp.bfloat16)
    queries = projected[:, :inner_width].reshape(number, window_size, HEADS, HD).astype(jnp.float32)
    keys_all = projected[:, inner_width:2 * inner_width].reshape(number, window_size, HEADS, HD).astype(jnp.float32)
    values_all = projected[:, 2 * inner_width:].reshape(number, window_size, HEADS, HD).astype(jnp.float32)
    scores = jnp.einsum('nqhd,nkhd->nhqk', queries, keys_all) / math.sqrt(HD)
    live_keys = jnp.arange(window_size, dtype=jnp.int32)[None, :] < lengths[:, None]
    scores = jnp.where(live_keys[:, None, None, :], scores, -1e+30)
    weights = jax.nn.softmax(scores, axis=-1).astype(jnp.bfloat16)
    attended = jnp.einsum('nhqk,nkhd->nqhd', weights.astype(jnp.float32), values_all)
    attended = attended.astype(jnp.bfloat16).reshape(number * window_size, inner_width)
    encoded = flat_rows.astype(jnp.float32) + jnp.dot(attended.astype(jnp.float32), w_out.astype(jnp.float32), preferred_element_type=jnp.float32)
    return (encoded.astype(jnp.bfloat16), attended)

def reference(pixels, window_owner, window_len, slot_token, cotangent, w_qkv, w_out, gain):
    loaders = OWNERS * REPLICAS
    windows = pixels.reshape(loaders, LW, WIN, D)
    lengths = window_len.reshape(loaders, LW)

    def per_loader(members):
        return encode(members[0], members[1], w_qkv, w_out, gain)
    encoded, attended = lax.map(per_loader, (windows, lengths))
    merged = encoded.reshape(OWNERS, REPLICAS, LW, TPW, MERGE * D)
    owners = window_owner.reshape(OWNERS, REPLICAS, LW)
    slot_table = slot_token.reshape(OWNERS, REPLICAS, TOK_DEV)
    owner_ids = jnp.arange(OWNERS, dtype=jnp.int32)
    matches = (owners[None, :, :, :] == owner_ids[:, None, None, None]).astype(jnp.int32)
    chosen = lax.optimization_barrier(jnp.sum(matches * jnp.arange(LW, dtype=jnp.int32), axis=-1))
    clipped = jnp.maximum(slot_table, 0)
    source = clipped // TPW
    within = clipped % TPW
    owner_axis = owner_ids[:, None, None]
    replica_axis = jnp.arange(REPLICAS, dtype=jnp.int32)[None, :, None]
    window_pick = chosen[owner_axis, source, replica_axis]
    gathered = merged[source, replica_axis, window_pick, within]
    embeddings = jnp.where((slot_table >= 0)[..., None], gathered, jnp.zeros_like(gathered))
    embeddings = embeddings.reshape(TOKENS, MERGE * D)
    sentinel = TPW * OWNERS
    target = jnp.where(slot_table >= 0, slot_table, sentinel).astype(jnp.int32)
    positions = jnp.broadcast_to(jnp.arange(TOK_DEV, dtype=jnp.int32), slot_table.shape)
    inverse = jnp.full((OWNERS, REPLICAS, sentinel), TOK_DEV, jnp.int32)
    inverse = inverse.at[jnp.broadcast_to(owner_axis, slot_table.shape), jnp.broadcast_to(replica_axis, slot_table.shape), target].set(positions, mode='drop')
    source_axis = owner_ids[:, None, None, None]
    replica_four = jnp.arange(REPLICAS, dtype=jnp.int32)[None, :, None, None]
    token_part = jnp.arange(TPW, dtype=jnp.int32)[None, None, None, :]
    destination = owners[:, :, :, None]
    located = inverse[destination, replica_four, TPW * source_axis + token_part]
    tangents = cotangent.reshape(OWNERS, REPLICAS, TOK_DEV, MERGE * D)
    picked = tangents[destination, replica_four, jnp.minimum(located, TOK_DEV - 1)]
    d_merged = jnp.where((located < TOK_DEV)[..., None], picked, jnp.zeros_like(picked))
    d_encoded = d_merged.reshape(loaders, LW * WIN, D)

    def accumulate(summed, members):
        return (summed + jnp.dot(members[0].T.astype(jnp.float32), members[1].astype(jnp.float32), preferred_element_type=jnp.float32), None)
    summed, ignored = lax.scan(accumulate, jnp.zeros((HW, D), jnp.float32), (attended, d_encoded))
    gradient = summed / math.sqrt(PATCHES)
    return (embeddings, gradient)
```

```python
import math

import jax
import jax.numpy as jnp
from jax import lax
from jax.sharding import PartitionSpec as P

HD = 80
HEADS = 8
MERGE = 4


def normalize(inputs, gain):
    values = inputs.astype(jnp.float32)
    mean_square = jnp.mean(values * values, axis=-1, keepdims=True)
    return (values * lax.rsqrt(mean_square + 1e-06) * gain).astype(jnp.bfloat16)


def attend(windows, lengths, w_qkv, gain):
    number, window_size, feature_width = windows.shape
    inner_width = w_qkv.shape[1] // 3
    flat_rows = windows.reshape(number * window_size, feature_width)
    normed = normalize(flat_rows, gain)
    projected = jnp.dot(normed, w_qkv, preferred_element_type=jnp.float32).astype(jnp.bfloat16)
    queries = projected[:, :inner_width].reshape(number, window_size, HEADS, HD)
    keys_all = projected[:, inner_width : 2 * inner_width].reshape(number, window_size, HEADS, HD)
    values_all = projected[:, 2 * inner_width :].reshape(number, window_size, HEADS, HD)
    scores = jnp.einsum(
        "nqhd,nkhd->nhqk", queries, keys_all, preferred_element_type=jnp.float32
    ) / math.sqrt(HD)
    live_keys = jnp.arange(window_size, dtype=jnp.int32)[None, :] < lengths[:, None]
    scores = jnp.where(live_keys[:, None, None, :], scores, -1e30)
    weights = jax.nn.softmax(scores, axis=-1).astype(jnp.bfloat16)
    attended = jnp.einsum(
        "nhqk,nkhd->nqhd", weights, values_all, preferred_element_type=jnp.float32
    )
    return attended.astype(jnp.bfloat16).reshape(number * window_size, inner_width)


def project(flat_rows, attended, w_out):
    encoded = flat_rows.astype(jnp.float32) + jnp.dot(
        attended, w_out, preferred_element_type=jnp.float32
    )
    return encoded.astype(jnp.bfloat16)


def any_slice(pixels, window_owner, window_len, slot_token, cotangent, w_qkv, w_out, gain):
    group_size = lax.axis_size("enc")
    replica_count = lax.axis_size("rep")
    feature_width = pixels.shape[1]
    window_count = window_owner.shape[0]
    window_rows = pixels.shape[0] // window_count
    tokens_each = window_rows // MERGE
    merged_width = MERGE * feature_width
    owner_ids = jnp.arange(group_size, dtype=jnp.int32)
    route = (window_owner[None, :] == owner_ids[:, None]).astype(jnp.bfloat16)
    slot_ids = jnp.arange(group_size * tokens_each, dtype=jnp.int32)
    placing = (slot_token[:, None] == slot_ids[None, :]).astype(jnp.bfloat16)
    attended = attend(
        pixels.reshape(window_count, window_rows, feature_width), window_len, w_qkv, gain
    )
    encoded = project(pixels, attended, w_out)
    outgoing = jnp.dot(
        route,
        encoded.reshape(window_count, window_rows * feature_width),
        preferred_element_type=jnp.float32,
    )
    outgoing = outgoing.astype(jnp.bfloat16).reshape(group_size, tokens_each, merged_width)
    arrived = lax.all_to_all(outgoing, "enc", split_axis=0, concat_axis=0, tiled=True)
    embeddings = jnp.dot(
        placing,
        arrived.reshape(group_size * tokens_each, merged_width),
        preferred_element_type=jnp.float32,
    ).astype(jnp.bfloat16)
    returning = lax.dot_general(
        placing, cotangent, (((0,), (0,)), ((), ())), preferred_element_type=jnp.float32
    )
    returning = returning.astype(jnp.bfloat16).reshape(group_size, tokens_each, merged_width)
    answered = lax.all_to_all(returning, "enc", split_axis=0, concat_axis=0, tiled=True)
    d_encoded = lax.dot_general(
        route,
        answered.reshape(group_size, tokens_each * merged_width),
        (((0,), (0,)), ((), ())),
        preferred_element_type=jnp.float32,
    )
    d_encoded = d_encoded.astype(jnp.bfloat16).reshape(window_count * window_rows, feature_width)
    reduced = lax.psum_scatter(
        lax.dot_general(
            attended, d_encoded, (((0,), (0,)), ((), ())), preferred_element_type=jnp.float32
        ),
        "enc",
        scatter_dimension=0,
        tiled=True,
    )
    summed = lax.psum(reduced, "rep")
    patch_total = window_count * window_rows * group_size * replica_count
    gradient = summed / math.sqrt(patch_total)
    return (embeddings, gradient)


def swap(value, axis, bits):
    size = lax.axis_size(axis)
    return lax.ppermute(value, axis, [(i, i ^ bits) for i in range(size)])


def xor_slice(pixels, window_owner, window_len, slot_token, cotangent, w_qkv, w_out, gain):
    group = lax.axis_size("enc")
    replicas = lax.axis_size("rep")
    width = pixels.shape[1]
    windows = window_owner.shape[0]
    rows = pixels.shape[0]
    window_rows = rows // windows
    inner = w_out.shape[0]
    head_columns = inner // group
    row_ids = jnp.arange(rows, dtype=jnp.int32)
    slot_of = row_ids // MERGE
    me = lax.axis_index("enc")

    held = jnp.zeros((rows, width), jnp.float32)
    for j in range(MERGE):
        pick = (slot_token[None, :] == slot_of[:, None]) & (row_ids[:, None] % MERGE == j)
        held = held + jnp.dot(
            pick.astype(jnp.bfloat16),
            cotangent[:, j * width : (j + 1) * width],
            preferred_element_type=jnp.float32,
        )
    held = held.astype(jnp.bfloat16)
    blocks = {0: held}
    for b in range(2, group, 2):
        blocks[b] = swap(held, "enc", b)
    for b in range(0, group, 2):
        blocks[b + 1] = swap(blocks[b], "enc", 1)

    owner_ids = jnp.arange(group, dtype=jnp.int32)
    route = window_owner[None, :] == owner_ids[:, None]
    lengths = jnp.sum(jnp.where(route, window_len[None, :], 0), axis=1)
    by_row = jnp.repeat(jnp.repeat(route, window_rows, 0), window_rows, 1)
    by_row = by_row & (row_ids[:, None] % window_rows == row_ids[None, :] % window_rows)
    ordered = jnp.dot(
        by_row.astype(jnp.bfloat16), pixels, preferred_element_type=jnp.float32
    ).astype(jnp.bfloat16)
    attended = attend(ordered.reshape(windows, window_rows, width), lengths, w_qkv, gain)
    columns = attended.T.reshape(group, head_columns, rows)
    gathered = lax.all_to_all(columns, "enc", split_axis=0, concat_axis=0, tiled=True)
    encoded = project(ordered, attended, w_out)
    arrived = lax.all_to_all(encoded, "enc", split_axis=0, concat_axis=0, tiled=True)

    total = jnp.zeros((head_columns, width), jnp.float32)
    relative = (row_ids[:, None] // window_rows) == ((row_ids[None, :] // window_rows) ^ me)
    relative = relative & (row_ids[:, None] % window_rows == row_ids[None, :] % window_rows)
    turned = jnp.dot(
        gathered.reshape(group * head_columns, rows),
        relative.astype(jnp.bfloat16),
        preferred_element_type=jnp.float32,
    ).astype(jnp.bfloat16)
    stacked = jnp.stack([blocks[b].reshape(group, window_rows, width) for b in range(group)], 1)
    total = jnp.einsum(
        "scp,spf->cf",
        turned.reshape(group, head_columns, rows),
        stacked.reshape(group, rows, width),
        preferred_element_type=jnp.float32,
    )
    total = total / math.sqrt(rows * group * replicas)
    bit = 1
    while bit < replicas:
        part = total.astype(jnp.bfloat16)
        total = part.astype(jnp.float32) + swap(part, "rep", bit).astype(jnp.float32)
        bit *= 2

    embeddings = []
    for j in range(MERGE):
        put = (slot_token[:, None] == slot_of[None, :]) & (row_ids[None, :] % MERGE == j)
        embeddings.append(
            jnp.dot(put.astype(jnp.bfloat16), arrived, preferred_element_type=jnp.float32)
        )
    return (jnp.concatenate(embeddings, 1).astype(jnp.bfloat16), total)


def solution(mesh):
    def shards(*args):
        group = mesh.shape["enc"]
        replicas = mesh.shape["rep"]
        powers = group & (group - 1) == 0 and replicas & (replicas - 1) == 0
        whole = powers and args[1].shape[0] == group
        return (xor_slice if whole else any_slice)(*args)

    return jax.shard_map(
        shards,
        mesh=mesh,
        in_specs=(
            P(("enc", "rep"), None),
            P(("enc", "rep")),
            P(("enc", "rep")),
            P(("enc", "rep")),
            P(("enc", "rep"), None),
            P(),
            P(),
            P(),
        ),
        out_specs=(P(("enc", "rep"), None), P("enc", None)),
        check_vma=False,
    )
```

```python
import functools
import math

import jax
import jax.numpy as jnp
from jax import lax
from jax.experimental import pallas as pl
from jax.experimental.pallas import tpu as pltpu
from jax.sharding import PartitionSpec as P

HD = 80
HEADS = 8
MERGE = 4


def normalize(inputs, gain):
    values = inputs.astype(jnp.float32)
    mean_square = jnp.mean(values * values, axis=-1, keepdims=True)
    return (values * lax.rsqrt(mean_square + 1e-06) * gain).astype(jnp.bfloat16)


def attend(windows, lengths, w_qkv, gain):
    number, window_size, feature_width = windows.shape
    inner_width = w_qkv.shape[1] // 3
    flat_rows = windows.reshape(number * window_size, feature_width)
    normed = normalize(flat_rows, gain)
    projected = jnp.dot(normed, w_qkv, preferred_element_type=jnp.float32).astype(jnp.bfloat16)
    queries = projected[:, :inner_width].reshape(number, window_size, HEADS, HD)
    keys_all = projected[:, inner_width : 2 * inner_width].reshape(number, window_size, HEADS, HD)
    values_all = projected[:, 2 * inner_width :].reshape(number, window_size, HEADS, HD)
    scores = jnp.einsum(
        "nqhd,nkhd->nhqk", queries, keys_all, preferred_element_type=jnp.float32
    ) / math.sqrt(HD)
    live_keys = jnp.arange(window_size, dtype=jnp.int32)[None, :] < lengths[:, None]
    scores = jnp.where(live_keys[:, None, None, :], scores, -1e30)
    weights = jax.nn.softmax(scores, axis=-1).astype(jnp.bfloat16)
    attended = jnp.einsum(
        "nhqk,nkhd->nqhd", weights, values_all, preferred_element_type=jnp.float32
    )
    return attended.astype(jnp.bfloat16).reshape(number * window_size, inner_width)


def project(flat_rows, attended, w_out):
    encoded = flat_rows.astype(jnp.float32) + jnp.dot(
        attended, w_out, preferred_element_type=jnp.float32
    )
    return encoded.astype(jnp.bfloat16)


def any_slice(pixels, window_owner, window_len, slot_token, cotangent, w_qkv, w_out, gain):
    group_size = lax.axis_size("enc")
    replica_count = lax.axis_size("rep")
    feature_width = pixels.shape[1]
    window_count = window_owner.shape[0]
    window_rows = pixels.shape[0] // window_count
    tokens_each = window_rows // MERGE
    merged_width = MERGE * feature_width
    owner_ids = jnp.arange(group_size, dtype=jnp.int32)
    route = (window_owner[None, :] == owner_ids[:, None]).astype(jnp.bfloat16)
    slot_ids = jnp.arange(group_size * tokens_each, dtype=jnp.int32)
    placing = (slot_token[:, None] == slot_ids[None, :]).astype(jnp.bfloat16)
    attended = attend(
        pixels.reshape(window_count, window_rows, feature_width), window_len, w_qkv, gain
    )
    encoded = project(pixels, attended, w_out)
    outgoing = jnp.dot(
        route,
        encoded.reshape(window_count, window_rows * feature_width),
        preferred_element_type=jnp.float32,
    )
    outgoing = outgoing.astype(jnp.bfloat16).reshape(group_size, tokens_each, merged_width)
    arrived = lax.all_to_all(outgoing, "enc", split_axis=0, concat_axis=0, tiled=True)
    embeddings = jnp.dot(
        placing,
        arrived.reshape(group_size * tokens_each, merged_width),
        preferred_element_type=jnp.float32,
    ).astype(jnp.bfloat16)
    returning = lax.dot_general(
        placing, cotangent, (((0,), (0,)), ((), ())), preferred_element_type=jnp.float32
    )
    returning = returning.astype(jnp.bfloat16).reshape(group_size, tokens_each, merged_width)
    answered = lax.all_to_all(returning, "enc", split_axis=0, concat_axis=0, tiled=True)
    d_encoded = lax.dot_general(
        route,
        answered.reshape(group_size, tokens_each * merged_width),
        (((0,), (0,)), ((), ())),
        preferred_element_type=jnp.float32,
    )
    d_encoded = d_encoded.astype(jnp.bfloat16).reshape(window_count * window_rows, feature_width)
    reduced = lax.psum_scatter(
        lax.dot_general(
            attended, d_encoded, (((0,), (0,)), ((), ())), preferred_element_type=jnp.float32
        ),
        "enc",
        scatter_dimension=0,
        tiled=True,
    )
    summed = lax.psum(reduced, "rep")
    patch_total = window_count * window_rows * group_size * replica_count
    gradient = summed / math.sqrt(patch_total)
    return (embeddings, gradient)


LANES = 128
VMEM = pl.BlockSpec(memory_space=pltpu.VMEM)
HBM = pl.BlockSpec(memory_space=pltpu.HBM)
SMEM = pl.BlockSpec(memory_space=pltpu.SMEM)
TRANSPOSED = (((0,), (0,)), ((), ()))
ROWS_WITH_ROWS = (((1,), (1,)), ((), ()))


def iota(shape, dim):
    return lax.broadcasted_iota(jnp.int32, shape, dim)


def cost(flops, moved):
    return pl.CostEstimate(flops=flops, bytes_accessed=moved, transcendentals=0)


def params(mib):
    return pltpu.CompilerParams(vmem_limit_bytes=mib * 1024 * 1024)


def pick_kernel(slots_ref, cotangent_hbm, held_ref, parts, sems):
    rows, width = held_ref.shape
    tokens = cotangent_hbm.shape[0]
    copies = []
    for j in range(MERGE):
        columns = cotangent_hbm.at[:, pl.ds(j * width, width)]
        copies.append(pltpu.make_async_copy(columns, parts.at[j], sems.at[j]))
        copies[j].start()
    row = iota((rows, tokens), 0)
    holds = slots_ref[...] == row // MERGE
    held = None
    for j in range(MERGE):
        pick = jnp.where(holds & (row % MERGE == j), 1.0, 0.0).astype(jnp.bfloat16)
        copies[j].wait()
        term = jnp.dot(pick, parts[j], preferred_element_type=jnp.float32)
        held = term if held is None else held + term
    held_ref[...] = held.astype(jnp.bfloat16)


def pick_rows(slot_token, cotangent, rows, width):
    tokens = cotangent.shape[0]
    return pl.pallas_call(
        pick_kernel,
        out_shape=jax.ShapeDtypeStruct((rows, width), jnp.bfloat16),
        in_specs=[VMEM, HBM],
        out_specs=VMEM,
        scratch_shapes=[
            pltpu.VMEM((MERGE, tokens, width), jnp.bfloat16),
            pltpu.SemaphoreType.DMA((MERGE,)),
        ],
        compiler_params=params(16),
        cost_estimate=cost(2 * MERGE * rows * tokens * width, 2 * cotangent.size),
        name="pick_rows",
    )(slot_token.reshape(1, tokens), cotangent)


def place_of(owner, group):
    return owner % 2 * (group // 2) + owner // 2


def attend_kernel(
    owner_ref, len_ref, pixels_ref, gain_ref, w_hbm, sent_ref, attended_ref, ordered_ref,
    weights, sems,
):
    rows, width = pixels_ref.shape
    windows = owner_ref.shape[0]
    window_rows = rows // windows
    inner = attended_ref.shape[0]
    copies = []
    for part in range(3):
        columns = w_hbm.at[:, pl.ds(part * inner, inner)]
        copies.append(pltpu.make_async_copy(columns, weights.at[part], sems.at[part]))
        copies[part].start()
    key_row = iota((rows, rows), 0)
    key_window = key_row // window_rows
    live = jnp.zeros((rows, rows), jnp.int32)
    for w in range(windows):
        place = place_of(owner_ref[w], windows)
        place_rows = pl.ds(pl.multiple_of(place * window_rows, window_rows), window_rows)
        ordered_ref[place_rows, :] = pixels_ref[w * window_rows : (w + 1) * window_rows, :]
        live = jnp.where(key_window == place, len_ref[w], live)
    allowed = (key_window == iota((rows, rows), 1) // window_rows) & (
        key_row % window_rows < live
    )
    values = ordered_ref[...].astype(jnp.float32)
    mean_square = jnp.mean(values * values, axis=-1, keepdims=True)
    normed = (values * lax.rsqrt(mean_square + 1e-06) * gain_ref[...]).astype(jnp.bfloat16)
    projected = []
    for part in range(3):
        copies[part].wait()
        projected.append(jnp.dot(normed, weights[part], preferred_element_type=jnp.float32))
    queries = projected[0].astype(jnp.bfloat16)
    keys_all = projected[1].astype(jnp.bfloat16)
    values_across = projected[2].T.astype(jnp.bfloat16)
    scale = 1.0 / math.sqrt(HD)
    first_half = iota((HD, rows), 1) < rows // 2
    for pair in range(inner // HD // 2):
        across = []
        for head in (2 * pair, 2 * pair + 1):
            first = head * HD
            low = first // LANES * LANES
            high = -(-(first + HD) // LANES) * LANES
            lane = iota((rows, high - low), 1) + low
            own = (lane >= first) & (lane < first + HD)
            keys = jnp.where(own, keys_all[:, low:high], jnp.zeros((), jnp.bfloat16))
            scores = lax.dot_general(
                keys, queries[:, low:high], ROWS_WITH_ROWS, preferred_element_type=jnp.float32
            )
            scores = jnp.where(allowed, scores * scale, -1e30)
            raised = jnp.exp(scores - jnp.max(scores, axis=0, keepdims=True))
            weight = (raised / jnp.sum(raised, axis=0, keepdims=True)).astype(jnp.bfloat16)
            mixed = jnp.dot(
                values_across[first : first + HD, :], weight, preferred_element_type=jnp.float32
            )
            attended_ref[first : first + HD, :] = mixed.astype(jnp.bfloat16)
            across.append(mixed)
        one, two = across
        first = 2 * pair * HD
        sent_ref[first : first + HD, :] = jnp.where(
            first_half, one, pltpu.roll(two, rows // 2, 1)
        ).astype(jnp.bfloat16)
        sent_ref[first + HD : first + 2 * HD, :] = jnp.where(
            first_half, pltpu.roll(one, rows // 2, 1), two
        ).astype(jnp.bfloat16)


def attend_ordered(window_owner, window_len, pixels, gain, w_qkv):
    rows, width = pixels.shape
    inner = w_qkv.shape[1] // 3
    return pl.pallas_call(
        attend_kernel,
        out_shape=(
            jax.ShapeDtypeStruct((inner, rows), jnp.bfloat16),
            jax.ShapeDtypeStruct((inner, rows), jnp.bfloat16),
            jax.ShapeDtypeStruct((rows, width), jnp.bfloat16),
        ),
        in_specs=[SMEM, SMEM, VMEM, VMEM, HBM],
        out_specs=(VMEM, VMEM, VMEM),
        scratch_shapes=[
            pltpu.VMEM((3, width, inner), jnp.bfloat16),
            pltpu.SemaphoreType.DMA((3,)),
        ],
        compiler_params=params(60),
        cost_estimate=cost(2 * rows * width * 3 * inner, 2 * w_qkv.size),
        name="attend",
    )(window_owner, window_len, pixels, gain.reshape(1, width), w_qkv)


def project_kernel(group, attended_ref, ordered_ref, w_ref, encoded_ref):
    window_rows = ordered_ref.shape[0] // group
    added = lax.dot_general(
        attended_ref[...], w_ref[...], TRANSPOSED, preferred_element_type=jnp.float32
    )
    encoded = (ordered_ref[...].astype(jnp.float32) + added).astype(jnp.bfloat16)
    for owner in range(group):
        place = place_of(owner, group) * window_rows
        encoded_ref[owner * window_rows : (owner + 1) * window_rows, :] = encoded[
            place : place + window_rows
        ]


def project_ordered(attended, ordered, w_out, group):
    return pl.pallas_call(
        functools.partial(project_kernel, group),
        out_shape=jax.ShapeDtypeStruct(ordered.shape, jnp.bfloat16),
        in_specs=[VMEM] * 3,
        out_specs=VMEM,
        compiler_params=params(16),
        cost_estimate=cost(2 * ordered.size * w_out.shape[0], 2 * w_out.size),
        name="project",
    )(attended, ordered, w_out)


def gradient_kernel(scale, me_ref, gathered_ref, *refs):
    kept_ref, given_ref = refs[-2:]
    blocks = refs[:-2]
    pairs = len(blocks)
    group = 2 * pairs
    rows = gathered_ref.shape[1]
    half = rows // 2
    window_rows = half // pairs
    head = gathered_ref.shape[0] // group
    mine = me_ref[0] // 2
    source = iota((rows, rows), 0)
    target = iota((rows, rows), 1)
    same = (source // window_rows % pairs == (target // window_rows % pairs) ^ mine) & (
        source % window_rows == target % window_rows
    )
    straight = jnp.where(same & (source // half == target // half), 1.0, 0.0)
    crossed = jnp.where(same & (source // half != target // half), 1.0, 0.0)
    gathered = gathered_ref[...]
    straight = jnp.dot(
        gathered, straight.astype(jnp.bfloat16), preferred_element_type=jnp.float32
    ).astype(jnp.bfloat16)
    crossed = jnp.dot(
        gathered, crossed.astype(jnp.bfloat16), preferred_element_type=jnp.float32
    ).astype(jnp.bfloat16)
    left = iota((head, rows), 1) < half
    one, two = [], []
    for s in range(0, group, 2):
        here = slice(s * head, (s + 1) * head)
        there = slice((s + 1) * head, (s + 2) * head)
        one.append(jnp.where(left, straight[here], crossed[there]))
        two.append(jnp.where(left, crossed[here], straight[there]))
    columns = jnp.concatenate([jnp.concatenate(one, 1), jnp.concatenate(two, 1)], 0)
    against = jnp.concatenate(
        [
            block[s * window_rows : (s + 1) * window_rows, :]
            for s in range(group)
            for block in blocks
        ],
        0,
    )
    total = jnp.dot(columns, against, preferred_element_type=jnp.float32) * scale
    first = me_ref[0] % 2 == 0
    kept_ref[...] = jnp.where(first, total[:head], total[head:])
    given_ref[...] = jnp.where(first, total[head:], total[:head]).astype(jnp.bfloat16)


def gradient_rows(me, gathered, blocks, scale):
    group = 2 * len(blocks)
    head = gathered.shape[0] // group
    rows, width = blocks[0].shape
    return pl.pallas_call(
        functools.partial(gradient_kernel, scale),
        out_shape=(
            jax.ShapeDtypeStruct((head, width), jnp.float32),
            jax.ShapeDtypeStruct((head, width), jnp.bfloat16),
        ),
        in_specs=[SMEM] + [VMEM] * (1 + len(blocks)),
        out_specs=(VMEM, VMEM),
        compiler_params=params(24),
        cost_estimate=cost(2 * head * rows * group * width, group * rows * width),
        name="gradient_rows",
    )(me.reshape(1), gathered, *blocks)


def place_kernel(slots_ref, arrived_ref, embeddings_ref):
    rows, width = arrived_ref.shape
    tokens = embeddings_ref.shape[0]
    row = iota((tokens, rows), 1)
    holds = slots_ref[...] == row // MERGE
    for j in range(MERGE):
        put = jnp.where(holds & (row % MERGE == j), 1.0, 0.0).astype(jnp.bfloat16)
        part = jnp.dot(put, arrived_ref[...], preferred_element_type=jnp.float32)
        embeddings_ref[:, j * width : (j + 1) * width] = part.astype(jnp.bfloat16)


def place_rows(slot_token, arrived):
    rows, width = arrived.shape
    tokens = slot_token.shape[0]
    return pl.pallas_call(
        place_kernel,
        out_shape=jax.ShapeDtypeStruct((tokens, MERGE * width), jnp.bfloat16),
        in_specs=[VMEM, VMEM],
        out_specs=VMEM,
        compiler_params=params(16),
        cost_estimate=cost(2 * MERGE * rows * tokens * width, 2 * MERGE * tokens * width),
        name="place_rows",
    )(slot_token.reshape(tokens, 1), arrived)


def after(value, other):
    return lax.optimization_barrier((value, other))[0]


def swap(value, axis, bits):
    size = lax.axis_size(axis)
    return lax.ppermute(value, axis, [(i, i ^ bits) for i in range(size)])


def xor_slice(pixels, window_owner, window_len, slot_token, cotangent, w_qkv, w_out, gain):
    group = lax.axis_size("enc")
    replicas = lax.axis_size("rep")
    rows, width = pixels.shape
    inner = w_out.shape[0]
    me = lax.axis_index("enc")

    held = pick_rows(slot_token, cotangent, rows, width)
    blocks = [held] + [swap(held, "enc", b) for b in range(2, group, 2)]
    sent, attended, ordered = attend_ordered(window_owner, window_len, pixels, gain, w_qkv)
    gathered = lax.all_to_all(
        sent.reshape(group, inner // group, rows), "enc", split_axis=0, concat_axis=0, tiled=True
    )
    encoded = project_ordered(attended, ordered, w_out, group)
    scale = 1.0 / math.sqrt(rows * group * replicas)
    kept, given = gradient_rows(me, gathered.reshape(inner, rows), blocks, scale)
    part = (kept + swap(given, "enc", 1).astype(jnp.float32)).astype(jnp.bfloat16)
    arrived = lax.all_to_all(
        after(encoded, part), "enc", split_axis=0, concat_axis=0, tiled=True
    )
    bit = 1
    while bit < replicas:
        total = part.astype(jnp.float32) + swap(part, "rep", bit).astype(jnp.float32)
        part = total.astype(jnp.bfloat16)
        bit *= 2
    embeddings = place_rows(slot_token, arrived)
    return (embeddings, total)


def solution(mesh):
    def shards(*args):
        group = mesh.shape["enc"]
        replicas = mesh.shape["rep"]
        powers = group & (group - 1) == 0 and replicas & (replicas - 1) == 0
        whole = powers and args[1].shape[0] == group
        return (xor_slice if whole else any_slice)(*args)

    return jax.shard_map(
        shards,
        mesh=mesh,
        in_specs=(
            P(("enc", "rep"), None),
            P(("enc", "rep")),
            P(("enc", "rep")),
            P(("enc", "rep")),
            P(("enc", "rep"), None),
            P(),
            P(),
            P(),
        ),
        out_specs=(P(("enc", "rep"), None), P("enc", None)),
        check_vma=False,
    )
```

```python
import functools
import math

import jax
import jax.numpy as jnp
from jax import lax
from jax.experimental import pallas as pl
from jax.experimental.pallas import tpu as pltpu
from jax.sharding import PartitionSpec as P

HD = 80
HEADS = 8
MERGE = 4


def normalize(inputs, gain):
    values = inputs.astype(jnp.float32)
    mean_square = jnp.mean(values * values, axis=-1, keepdims=True)
    return (values * lax.rsqrt(mean_square + 1e-06) * gain).astype(jnp.bfloat16)


def attend(windows, lengths, w_qkv, gain):
    number, window_size, feature_width = windows.shape
    inner_width = w_qkv.shape[1] // 3
    flat_rows = windows.reshape(number * window_size, feature_width)
    normed = normalize(flat_rows, gain)
    projected = jnp.dot(normed, w_qkv, preferred_element_type=jnp.float32).astype(jnp.bfloat16)
    queries = projected[:, :inner_width].reshape(number, window_size, HEADS, HD)
    keys_all = projected[:, inner_width : 2 * inner_width].reshape(number, window_size, HEADS, HD)
    values_all = projected[:, 2 * inner_width :].reshape(number, window_size, HEADS, HD)
    scores = jnp.einsum(
        "nqhd,nkhd->nhqk", queries, keys_all, preferred_element_type=jnp.float32
    ) / math.sqrt(HD)
    live_keys = jnp.arange(window_size, dtype=jnp.int32)[None, :] < lengths[:, None]
    scores = jnp.where(live_keys[:, None, None, :], scores, -1e30)
    weights = jax.nn.softmax(scores, axis=-1).astype(jnp.bfloat16)
    attended = jnp.einsum(
        "nhqk,nkhd->nqhd", weights, values_all, preferred_element_type=jnp.float32
    )
    return attended.astype(jnp.bfloat16).reshape(number * window_size, inner_width)


def project(flat_rows, attended, w_out):
    encoded = flat_rows.astype(jnp.float32) + jnp.dot(
        attended, w_out, preferred_element_type=jnp.float32
    )
    return encoded.astype(jnp.bfloat16)


def any_slice(pixels, window_owner, window_len, slot_token, cotangent, w_qkv, w_out, gain):
    group_size = lax.axis_size("enc")
    replica_count = lax.axis_size("rep")
    feature_width = pixels.shape[1]
    window_count = window_owner.shape[0]
    window_rows = pixels.shape[0] // window_count
    tokens_each = window_rows // MERGE
    merged_width = MERGE * feature_width
    owner_ids = jnp.arange(group_size, dtype=jnp.int32)
    route = (window_owner[None, :] == owner_ids[:, None]).astype(jnp.bfloat16)
    slot_ids = jnp.arange(group_size * tokens_each, dtype=jnp.int32)
    placing = (slot_token[:, None] == slot_ids[None, :]).astype(jnp.bfloat16)
    attended = attend(
        pixels.reshape(window_count, window_rows, feature_width), window_len, w_qkv, gain
    )
    encoded = project(pixels, attended, w_out)
    outgoing = jnp.dot(
        route,
        encoded.reshape(window_count, window_rows * feature_width),
        preferred_element_type=jnp.float32,
    )
    outgoing = outgoing.astype(jnp.bfloat16).reshape(group_size, tokens_each, merged_width)
    arrived = lax.all_to_all(outgoing, "enc", split_axis=0, concat_axis=0, tiled=True)
    embeddings = jnp.dot(
        placing,
        arrived.reshape(group_size * tokens_each, merged_width),
        preferred_element_type=jnp.float32,
    ).astype(jnp.bfloat16)
    returning = lax.dot_general(
        placing, cotangent, (((0,), (0,)), ((), ())), preferred_element_type=jnp.float32
    )
    returning = returning.astype(jnp.bfloat16).reshape(group_size, tokens_each, merged_width)
    answered = lax.all_to_all(returning, "enc", split_axis=0, concat_axis=0, tiled=True)
    d_encoded = lax.dot_general(
        route,
        answered.reshape(group_size, tokens_each * merged_width),
        (((0,), (0,)), ((), ())),
        preferred_element_type=jnp.float32,
    )
    d_encoded = d_encoded.astype(jnp.bfloat16).reshape(window_count * window_rows, feature_width)
    reduced = lax.psum_scatter(
        lax.dot_general(
            attended, d_encoded, (((0,), (0,)), ((), ())), preferred_element_type=jnp.float32
        ),
        "enc",
        scatter_dimension=0,
        tiled=True,
    )
    summed = lax.psum(reduced, "rep")
    patch_total = window_count * window_rows * group_size * replica_count
    gradient = summed / math.sqrt(patch_total)
    return (embeddings, gradient)


LANES = 128
SUBLANES = 16
PAIR_BITS = 2
VMEM = pl.BlockSpec(memory_space=pltpu.VMEM)
HBM = pl.BlockSpec(memory_space=pltpu.HBM)
SMEM = pl.BlockSpec(memory_space=pltpu.SMEM)
TRANSPOSED = (((0,), (0,)), ((), ()))
ROWS_WITH_ROWS = (((1,), (1,)), ((), ()))


def turn(relative, core):
    other = relative % 2 * 2 + relative // 2
    if isinstance(core, int):
        return other if core else relative
    return jnp.where(core == 1, other, relative)


def iota(shape, dim):
    return lax.broadcasted_iota(jnp.int32, shape, dim)


def cost(flops, moved):
    return pl.CostEstimate(flops=flops, bytes_accessed=moved, transcendentals=0)


def params(mib):
    return pltpu.CompilerParams(vmem_limit_bytes=mib * 1024 * 1024)


def in_hbm(value):
    return pltpu.with_memory_space_constraint(value, pltpu.HBM)


def place(index, size):
    return pl.ds(pl.multiple_of(index * size, size), size)


def slot_of_row(row, me, window_rows):
    pair = turn(row // (2 * window_rows), me % 2) ^ (me // 2)
    source = pair * 2 + row // window_rows % 2
    return source * (window_rows // MERGE) + row % window_rows // MERGE


def pick_kernel(
    me_ref, owner_ref, len_ref, slots_ref, pixels_hbm, cotangent_hbm,
    held_ref, kept_ref, given_ref, parts, pixels_buf, windows_buf, sems,
):
    rows, width = held_ref.shape
    tokens = cotangent_hbm.shape[0]
    windows = owner_ref.shape[0]
    window_rows = rows // windows
    me = me_ref[0]
    copies = [pltpu.make_async_copy(pixels_hbm, pixels_buf, sems.at[MERGE])]
    copies[0].start()
    for j in range(MERGE):
        columns = cotangent_hbm.at[:, pl.ds(j * width, width)]
        copies.append(pltpu.make_async_copy(columns, parts.at[j], sems.at[j]))
        copies[1 + j].start()
    row = iota((rows, tokens), 0)
    holds = slots_ref[...] == slot_of_row(row, me, window_rows)
    picks = [
        jnp.where(holds & (row % MERGE == j), 1.0, 0.0).astype(jnp.bfloat16) for j in range(MERGE)
    ]
    copies[0].wait()
    which = iota((SUBLANES, width), 0)
    lengths = [jnp.zeros((SUBLANES, width), jnp.int32)] * 2
    for w in range(windows):
        owner = owner_ref[w]
        across = (owner + me) % 2
        relative = turn((owner // 2) ^ (me // 2), owner % 2)
        windows_buf[across, place(relative, window_rows), :] = pixels_buf[
            w * window_rows : (w + 1) * window_rows, :
        ]
        for side in range(2):
            here = jnp.where(across == side, relative, -1)
            lengths[side] = jnp.where(which == here, len_ref[w], lengths[side])
    for side, ref in enumerate((kept_ref, given_ref)):
        ref[: rows // 2, :] = windows_buf[side]
        ref[rows // 2 :, :] = lengths[side].astype(jnp.float32).astype(jnp.bfloat16)
    held = None
    for j in range(MERGE):
        copies[1 + j].wait()
        term = jnp.dot(picks[j], parts[j], preferred_element_type=jnp.float32)
        held = term if held is None else held + term
    held_ref[...] = held.astype(jnp.bfloat16)


def pick_rows(me, window_owner, window_len, slot_token, pixels, cotangent):
    rows, width = pixels.shape
    tokens = cotangent.shape[0]
    half = jax.ShapeDtypeStruct((rows // 2 + SUBLANES, width), jnp.bfloat16)
    return pl.pallas_call(
        pick_kernel,
        out_shape=(jax.ShapeDtypeStruct((rows, width), jnp.bfloat16), half, half),
        in_specs=[SMEM, SMEM, SMEM, VMEM, HBM, HBM],
        out_specs=(VMEM, VMEM, VMEM),
        scratch_shapes=[
            pltpu.VMEM((MERGE, tokens, width), jnp.bfloat16),
            pltpu.VMEM((rows, width), jnp.bfloat16),
            pltpu.VMEM((2, rows // 2, width), jnp.bfloat16),
            pltpu.SemaphoreType.DMA((MERGE + 1,)),
        ],
        compiler_params=params(16),
        cost_estimate=cost(2 * MERGE * rows * tokens * width, 2 * cotangent.size),
        name="pick_rows",
    )(
        me,
        in_hbm(window_owner),
        in_hbm(window_len),
        in_hbm(slot_token.reshape(1, tokens)),
        in_hbm(pixels),
        in_hbm(cotangent),
    )


def attend_kernel(
    me_ref, kept_ref, given_ref, gain_ref, w_hbm, *refs
):
    attended_ref, ordered_ref = refs[:2]
    sent_refs = refs[2:-3]
    sent, weights, sems = refs[-3:]
    rows, width = ordered_ref.shape
    pairs = len(sent_refs)
    window_rows = rows // (2 * pairs)
    inner = attended_ref.shape[0]
    me = me_ref[0]
    core = me % 2
    copies = []
    for part in range(3):
        columns = w_hbm.at[:, pl.ds(part * inner, inner)]
        copies.append(pltpu.make_async_copy(columns, weights.at[part], sems.at[part]))
        copies[part].start()
    key_row = iota((rows, rows), 0)
    key_window = key_row // window_rows
    live = jnp.zeros((rows, rows), jnp.float32)
    for ref, side in ((kept_ref, core), (given_ref, 1 - core)):
        lengths = ref[rows // 2 :, :rows].astype(jnp.float32)
        for b in range(pairs):
            window = 2 * b + side
            ordered_ref[place(window, window_rows), :] = ref[
                b * window_rows : (b + 1) * window_rows, :
            ]
            live = jnp.where(key_window == window, lengths[b : b + 1], live)
    allowed = (key_window == iota((rows, rows), 1) // window_rows) & (
        (key_row % window_rows).astype(jnp.float32) < live
    )
    values = ordered_ref[...].astype(jnp.float32)
    mean_square = jnp.mean(values * values, axis=-1, keepdims=True)
    normed = (values * lax.rsqrt(mean_square + 1e-06) * gain_ref[...][None, :]).astype(jnp.bfloat16)
    projected = []
    for part in range(3):
        copies[part].wait()
        projected.append(jnp.dot(normed, weights[part], preferred_element_type=jnp.float32))
    queries = projected[0].astype(jnp.bfloat16)
    keys_all = projected[1].astype(jnp.bfloat16)
    values_across = projected[2].T.astype(jnp.bfloat16)
    scale = 1.0 / math.sqrt(HD)
    for head in range(inner // HD):
        first = head * HD
        low = first // LANES * LANES
        high = -(-(first + HD) // LANES) * LANES
        lane = iota((rows, high - low), 1) + low
        own = (lane >= first) & (lane < first + HD)
        keys = jnp.where(own, keys_all[:, low:high], jnp.zeros((), jnp.bfloat16))
        scores = lax.dot_general(
            keys, queries[:, low:high], ROWS_WITH_ROWS, preferred_element_type=jnp.float32
        )
        scores = jnp.where(allowed, scores * scale, -1e30)
        raised = jnp.exp(scores - jnp.max(scores, axis=0, keepdims=True))
        weight = (raised / jnp.sum(raised, axis=0, keepdims=True)).astype(jnp.bfloat16)
        mixed = jnp.dot(
            values_across[first : first + HD, :], weight, preferred_element_type=jnp.float32
        ).astype(jnp.bfloat16)
        attended_ref[first : first + HD, :] = mixed
        relative = turn((head // 2) ^ (me // 2), core)
        sent[relative, head % 2 * HD : (head % 2 + 1) * HD, :] = mixed
    for b in range(pairs):
        sent_refs[b][...] = sent[b]


def attend_ordered(me, kept, given, gain, w_qkv, pairs):
    width = kept.shape[1]
    rows = 2 * (kept.shape[0] - SUBLANES)
    inner = w_qkv.shape[1] // 3
    heads = inner // pairs
    return pl.pallas_call(
        attend_kernel,
        out_shape=(
            jax.ShapeDtypeStruct((inner, rows), jnp.bfloat16),
            jax.ShapeDtypeStruct((rows, width), jnp.bfloat16),
        )
        + (jax.ShapeDtypeStruct((heads, rows), jnp.bfloat16),) * pairs,
        in_specs=[SMEM, VMEM, VMEM, VMEM, HBM],
        out_specs=(VMEM,) * (2 + pairs),
        scratch_shapes=[
            pltpu.VMEM((pairs, heads, rows), jnp.bfloat16),
            pltpu.VMEM((3, width, inner), jnp.bfloat16),
            pltpu.SemaphoreType.DMA((3,)),
        ],
        compiler_params=params(24),
        cost_estimate=cost(2 * rows * width * 3 * inner, 2 * w_qkv.size),
        name="attend",
    )(me, kept, given, in_hbm(gain), in_hbm(w_qkv))


def project_kernel(attended_ref, ordered_ref, w_ref, *encoded_refs):
    added = lax.dot_general(
        attended_ref[...], w_ref[...], TRANSPOSED, preferred_element_type=jnp.float32
    )
    encoded = (ordered_ref[...].astype(jnp.float32) + added).astype(jnp.bfloat16)
    size = ordered_ref.shape[0] // len(encoded_refs)
    for b, ref in enumerate(encoded_refs):
        ref[...] = encoded[b * size : (b + 1) * size]


def project_ordered(attended, ordered, w_out, pairs):
    rows, width = ordered.shape
    return pl.pallas_call(
        project_kernel,
        out_shape=(jax.ShapeDtypeStruct((rows // pairs, width), jnp.bfloat16),) * pairs,
        in_specs=[VMEM] * 3,
        out_specs=(VMEM,) * pairs,
        compiler_params=params(16),
        cost_estimate=cost(2 * ordered.size * w_out.shape[0], 2 * w_out.size),
        name="project",
    )(attended, ordered, w_out)


def gradient_kernel(scale, pairs, me_ref, *refs):
    columns, blocks = refs[:pairs], refs[pairs : 2 * pairs]
    kept_ref, given_ref = refs[2 * pairs :]
    size = blocks[0].shape[0] // pairs
    head = kept_ref.shape[0]
    left = jnp.concatenate([ref[...] for ref in columns], 1)
    right = jnp.concatenate(
        [
            blocks[b ^ r][r * size : (r + 1) * size, :]
            for b in range(pairs)
            for r in range(pairs)
        ],
        0,
    )
    total = jnp.dot(left, right, preferred_element_type=jnp.float32) * scale
    first = me_ref[0] % 2 == 0
    kept_ref[...] = jnp.where(first, total[:head], total[head:])
    given_ref[...] = jnp.where(first, total[head:], total[:head]).astype(jnp.bfloat16)


def gradient_rows(me, columns, blocks, scale):
    pairs = len(blocks)
    heads, rows = columns[0].shape
    width = blocks[0].shape[1]
    return pl.pallas_call(
        functools.partial(gradient_kernel, scale, pairs),
        out_shape=(
            jax.ShapeDtypeStruct((heads // 2, width), jnp.float32),
            jax.ShapeDtypeStruct((heads // 2, width), jnp.bfloat16),
        ),
        in_specs=[SMEM] + [VMEM] * (2 * pairs),
        out_specs=(VMEM, VMEM),
        compiler_params=params(24),
        cost_estimate=cost(2 * heads * rows * pairs * width, 2 * pairs * rows * width),
        name="gradient_rows",
    )(me, *columns, *blocks)


def place_kernel(me_ref, slots_ref, *refs):
    embeddings_ref = refs[-1]
    arrived = jnp.concatenate([ref[...] for ref in refs[:-1]], 0)
    rows, width = arrived.shape
    tokens = embeddings_ref.shape[0]
    row = iota((rows, tokens), 0)
    window_rows = rows // (2 * (len(refs) - 1))
    holds = slots_ref[...] == slot_of_row(row, me_ref[0], window_rows)
    for j in range(MERGE):
        put = jnp.where(holds & (row % MERGE == j), 1.0, 0.0).astype(jnp.bfloat16)
        part = lax.dot_general(put, arrived, TRANSPOSED, preferred_element_type=jnp.float32)
        embeddings_ref[:, j * width : (j + 1) * width] = part.astype(jnp.bfloat16)


def place_rows(me, slot_token, arrived):
    size, width = arrived[0].shape
    rows = size * len(arrived)
    tokens = slot_token.shape[0]
    return pl.pallas_call(
        place_kernel,
        out_shape=jax.ShapeDtypeStruct((tokens, MERGE * width), jnp.bfloat16),
        in_specs=[SMEM, VMEM] + [VMEM] * len(arrived),
        out_specs=VMEM,
        compiler_params=params(16),
        cost_estimate=cost(2 * MERGE * rows * tokens * width, 2 * MERGE * tokens * width),
        name="place_rows",
    )(me, slot_token.reshape(1, tokens), *arrived)


def after(value, other):
    return lax.optimization_barrier((value, other))[0]


def swap(value, axis, bits):
    size = lax.axis_size(axis)
    return lax.ppermute(value, axis, [(i, i ^ bits) for i in range(size)])


def chip_swap(value, relative):
    size = lax.axis_size("enc")
    return lax.ppermute(value, "enc", [(i, i ^ 2 * turn(relative, i % 2)) for i in range(size)])


def xor_slice(pixels, window_owner, window_len, slot_token, cotangent, w_qkv, w_out, gain):
    group = lax.axis_size("enc")
    replicas = lax.axis_size("rep")
    pairs = group // 2
    rows = pixels.shape[0]
    me = lax.axis_index("enc").astype(jnp.int32).reshape(1)

    held, kept, given = pick_rows(me, window_owner, window_len, slot_token, pixels, cotangent)
    given = swap(given, "enc", 1)
    blocks = [held, chip_swap(held, 1), chip_swap(held, 2)]
    attended, ordered, *sent = attend_ordered(me, kept, given, gain, w_qkv, pairs)
    blocks.append(chip_swap(after(blocks[1], attended), 2))
    columns = [sent[0]] + [chip_swap(sent[b], b) for b in range(1, pairs)]
    encoded = project_ordered(attended, ordered, w_out, pairs)
    scale = 1.0 / math.sqrt(rows * group * replicas)
    mine, other = gradient_rows(me, columns, blocks, scale)
    part = (mine + swap(other, "enc", 1).astype(jnp.float32)).astype(jnp.bfloat16)
    arrived = [encoded[0]]
    for b in range(1, pairs):
        arrived.append(chip_swap(after(encoded[b], part), b))
    bit = 1
    while bit < replicas:
        total = part.astype(jnp.float32) + swap(part, "rep", bit).astype(jnp.float32)
        part = total.astype(jnp.bfloat16)
        bit *= 2
    embeddings = place_rows(me, slot_token, arrived)
    return (embeddings, total)


def solution(mesh):
    def shards(*args):
        group = mesh.shape["enc"]
        replicas = mesh.shape["rep"]
        square = group == 2 << PAIR_BITS and replicas & (replicas - 1) == 0
        whole = square and args[1].shape[0] == group
        return (xor_slice if whole else any_slice)(*args)

    return jax.shard_map(
        shards,
        mesh=mesh,
        in_specs=(
            P(("enc", "rep"), None),
            P(("enc", "rep")),
            P(("enc", "rep")),
            P(("enc", "rep")),
            P(("enc", "rep"), None),
            P(),
            P(),
            P(),
        ),
        out_specs=(P(("enc", "rep"), None), P("enc", None)),
        check_vma=False,
    )
```

```python
import functools
import math

import jax
import jax.numpy as jnp
from jax import lax
from jax.experimental import pallas as pl
from jax.experimental.pallas import tpu as pltpu
from jax.sharding import PartitionSpec as P

HD = 80
HEADS = 8
MERGE = 4


def normalize(inputs, gain):
    values = inputs.astype(jnp.float32)
    mean_square = jnp.mean(values * values, axis=-1, keepdims=True)
    return (values * lax.rsqrt(mean_square + 1e-06) * gain).astype(jnp.bfloat16)


def attend(windows, lengths, w_qkv, gain):
    number, window_size, feature_width = windows.shape
    inner_width = w_qkv.shape[1] // 3
    flat_rows = windows.reshape(number * window_size, feature_width)
    normed = normalize(flat_rows, gain)
    projected = jnp.dot(normed, w_qkv, preferred_element_type=jnp.float32).astype(jnp.bfloat16)
    queries = projected[:, :inner_width].reshape(number, window_size, HEADS, HD)
    keys_all = projected[:, inner_width : 2 * inner_width].reshape(number, window_size, HEADS, HD)
    values_all = projected[:, 2 * inner_width :].reshape(number, window_size, HEADS, HD)
    scores = jnp.einsum(
        "nqhd,nkhd->nhqk", queries, keys_all, preferred_element_type=jnp.float32
    ) / math.sqrt(HD)
    live_keys = jnp.arange(window_size, dtype=jnp.int32)[None, :] < lengths[:, None]
    scores = jnp.where(live_keys[:, None, None, :], scores, -1e30)
    weights = jax.nn.softmax(scores, axis=-1).astype(jnp.bfloat16)
    attended = jnp.einsum(
        "nhqk,nkhd->nqhd", weights, values_all, preferred_element_type=jnp.float32
    )
    return attended.astype(jnp.bfloat16).reshape(number * window_size, inner_width)


def project(flat_rows, attended, w_out):
    encoded = flat_rows.astype(jnp.float32) + jnp.dot(
        attended, w_out, preferred_element_type=jnp.float32
    )
    return encoded.astype(jnp.bfloat16)


def any_slice(pixels, window_owner, window_len, slot_token, cotangent, w_qkv, w_out, gain):
    group_size = lax.axis_size("enc")
    replica_count = lax.axis_size("rep")
    feature_width = pixels.shape[1]
    window_count = window_owner.shape[0]
    window_rows = pixels.shape[0] // window_count
    tokens_each = window_rows // MERGE
    merged_width = MERGE * feature_width
    owner_ids = jnp.arange(group_size, dtype=jnp.int32)
    route = (window_owner[None, :] == owner_ids[:, None]).astype(jnp.bfloat16)
    slot_ids = jnp.arange(group_size * tokens_each, dtype=jnp.int32)
    placing = (slot_token[:, None] == slot_ids[None, :]).astype(jnp.bfloat16)
    attended = attend(
        pixels.reshape(window_count, window_rows, feature_width), window_len, w_qkv, gain
    )
    encoded = project(pixels, attended, w_out)
    outgoing = jnp.dot(
        route,
        encoded.reshape(window_count, window_rows * feature_width),
        preferred_element_type=jnp.float32,
    )
    outgoing = outgoing.astype(jnp.bfloat16).reshape(group_size, tokens_each, merged_width)
    arrived = lax.all_to_all(outgoing, "enc", split_axis=0, concat_axis=0, tiled=True)
    embeddings = jnp.dot(
        placing,
        arrived.reshape(group_size * tokens_each, merged_width),
        preferred_element_type=jnp.float32,
    ).astype(jnp.bfloat16)
    returning = lax.dot_general(
        placing, cotangent, (((0,), (0,)), ((), ())), preferred_element_type=jnp.float32
    )
    returning = returning.astype(jnp.bfloat16).reshape(group_size, tokens_each, merged_width)
    answered = lax.all_to_all(returning, "enc", split_axis=0, concat_axis=0, tiled=True)
    d_encoded = lax.dot_general(
        route,
        answered.reshape(group_size, tokens_each * merged_width),
        (((0,), (0,)), ((), ())),
        preferred_element_type=jnp.float32,
    )
    d_encoded = d_encoded.astype(jnp.bfloat16).reshape(window_count * window_rows, feature_width)
    reduced = lax.psum_scatter(
        lax.dot_general(
            attended, d_encoded, (((0,), (0,)), ((), ())), preferred_element_type=jnp.float32
        ),
        "enc",
        scatter_dimension=0,
        tiled=True,
    )
    summed = lax.psum(reduced, "rep")
    patch_total = window_count * window_rows * group_size * replica_count
    gradient = summed / math.sqrt(patch_total)
    return (embeddings, gradient)


LANES = 128
SUBLANES = 16
PAIR_BITS = 2
VMEM = pl.BlockSpec(memory_space=pltpu.VMEM)
HBM = pl.BlockSpec(memory_space=pltpu.HBM)
SMEM = pl.BlockSpec(memory_space=pltpu.SMEM)
TRANSPOSED = (((0,), (0,)), ((), ()))
ROWS_WITH_ROWS = (((1,), (1,)), ((), ()))


def turn(relative, core):
    other = relative % 2 * 2 + relative // 2
    if isinstance(core, int):
        return other if core else relative
    return jnp.where(core == 1, other, relative)


def iota(shape, dim):
    return lax.broadcasted_iota(jnp.int32, shape, dim)


def cost(flops, moved):
    return pl.CostEstimate(flops=flops, bytes_accessed=moved, transcendentals=0)


def params(mib):
    return pltpu.CompilerParams(vmem_limit_bytes=mib * 1024 * 1024)


def in_hbm(value):
    return pltpu.with_memory_space_constraint(value, pltpu.HBM)


def in_vmem(value):
    return pltpu.with_memory_space_constraint(value, pltpu.VMEM)


def place(index, size):
    return pl.ds(pl.multiple_of(index * size, size), size)


def slot_of_row(row, me, window_rows):
    pair = turn(row // (2 * window_rows), me % 2) ^ (me // 2)
    source = pair * 2 + row // window_rows % 2
    return source * (window_rows // MERGE) + row % window_rows // MERGE


def pick_kernel(
    owner_hbm, len_hbm, slots_hbm, pixels_hbm, cotangent_hbm, held_ref, kept_ref, given_ref,
    owner_ref, len_ref, slots_ref, pixels_buf, parts, windows_buf, sems,
):
    rows, width = held_ref.shape
    tokens = cotangent_hbm.shape[0]
    windows = owner_ref.shape[0]
    window_rows = rows // windows
    me = lax.axis_index("enc")
    pairs_of_refs = [
        (slots_hbm, slots_ref),
        (owner_hbm, owner_ref),
        (len_hbm, len_ref),
    ]
    for j in range(MERGE):
        pairs_of_refs.append((cotangent_hbm.at[:, pl.ds(j * width, width)], parts.at[j]))
    pairs_of_refs.append((pixels_hbm, pixels_buf))
    copies = [
        pltpu.make_async_copy(source, target, sems.at[i])
        for i, (source, target) in enumerate(pairs_of_refs)
    ]
    for copy in copies:
        copy.start()
    row = iota((rows, tokens), 0)
    copies[0].wait()
    holds = slots_ref[...] == slot_of_row(row, me, window_rows)
    picks = [
        jnp.where(holds & (row % MERGE == j), 1.0, 0.0).astype(jnp.bfloat16) for j in range(MERGE)
    ]
    held = None
    for j in range(MERGE):
        copies[3 + j].wait()
        term = jnp.dot(picks[j], parts[j], preferred_element_type=jnp.float32)
        held = term if held is None else held + term
    held_ref[...] = held.astype(jnp.bfloat16)
    copies[1].wait()
    copies[2].wait()
    copies[3 + MERGE].wait()
    which = iota((SUBLANES, width), 0)
    lengths = [jnp.zeros((SUBLANES, width), jnp.int32)] * 2
    for w in range(windows):
        owner = owner_ref[w]
        across = (owner + me) % 2
        relative = turn((owner // 2) ^ (me // 2), owner % 2)
        windows_buf[across, place(relative, window_rows), :] = pixels_buf[
            w * window_rows : (w + 1) * window_rows, :
        ]
        for side in range(2):
            here = jnp.where(across == side, relative, -1)
            lengths[side] = jnp.where(which == here, len_ref[w], lengths[side])
    for side, ref in enumerate((kept_ref, given_ref)):
        ref[: rows // 2, :] = windows_buf[side]
        ref[rows // 2 :, :] = lengths[side].astype(jnp.float32).astype(jnp.bfloat16)


def pick_rows(window_owner, window_len, slot_token, pixels, cotangent):
    rows, width = pixels.shape
    tokens = cotangent.shape[0]
    half = jax.ShapeDtypeStruct((rows // 2 + SUBLANES, width), jnp.bfloat16)
    return pl.pallas_call(
        pick_kernel,
        out_shape=(jax.ShapeDtypeStruct((rows, width), jnp.bfloat16), half, half),
        in_specs=[HBM] * 5,
        out_specs=(VMEM, VMEM, VMEM),
        scratch_shapes=[
            pltpu.SMEM(window_owner.shape, jnp.int32),
            pltpu.SMEM(window_len.shape, jnp.int32),
            pltpu.VMEM((1, tokens), jnp.int32),
            pltpu.VMEM((rows, width), jnp.bfloat16),
            pltpu.VMEM((MERGE, tokens, width), jnp.bfloat16),
            pltpu.VMEM((2, rows // 2, width), jnp.bfloat16),
            pltpu.SemaphoreType.DMA((MERGE + 4,)),
        ],
        compiler_params=params(16),
        cost_estimate=cost(200 * MERGE * rows * tokens * width, 2 * cotangent.size),
        name="pick_rows",
    )(
        in_hbm(window_owner),
        in_hbm(window_len),
        in_hbm(slot_token.reshape(1, tokens)),
        in_hbm(pixels),
        in_hbm(cotangent),
    )


def attend_kernel(
    kept_ref, given_ref, gain_ref, w_ref, *refs
):
    attended_ref, ordered_ref = refs[:2]
    sent_refs = refs[2:-1]
    sent = refs[-1]
    rows, width = ordered_ref.shape
    pairs = len(sent_refs)
    window_rows = rows // (2 * pairs)
    inner = attended_ref.shape[0]
    me = lax.axis_index("enc")
    core = me % 2
    key_row = iota((rows, rows), 0)
    key_window = key_row // window_rows
    live = jnp.zeros((rows, rows), jnp.float32)
    for ref, side in ((kept_ref, core), (given_ref, 1 - core)):
        lengths = ref[rows // 2 :, :rows].astype(jnp.float32)
        for b in range(pairs):
            window = 2 * b + side
            ordered_ref[place(window, window_rows), :] = ref[
                b * window_rows : (b + 1) * window_rows, :
            ]
            live = jnp.where(key_window == window, lengths[b : b + 1], live)
    allowed = (key_window == iota((rows, rows), 1) // window_rows) & (
        (key_row % window_rows).astype(jnp.float32) < live
    )
    values = ordered_ref[...].astype(jnp.float32)
    mean_square = jnp.mean(values * values, axis=-1, keepdims=True)
    normed = (values * lax.rsqrt(mean_square + 1e-06) * gain_ref[...][None, :]).astype(jnp.bfloat16)
    projected = []
    for part in range(3):
        columns = w_ref[:, part * inner : (part + 1) * inner]
        projected.append(jnp.dot(normed, columns, preferred_element_type=jnp.float32))
    queries = projected[0].astype(jnp.bfloat16)
    keys_all = projected[1].astype(jnp.bfloat16)
    values_across = projected[2].T.astype(jnp.bfloat16)
    scale = 1.0 / math.sqrt(HD)
    for head in range(inner // HD):
        first = head * HD
        low = first // LANES * LANES
        high = -(-(first + HD) // LANES) * LANES
        lane = iota((rows, high - low), 1) + low
        own = (lane >= first) & (lane < first + HD)
        keys = jnp.where(own, keys_all[:, low:high], jnp.zeros((), jnp.bfloat16))
        scores = lax.dot_general(
            keys, queries[:, low:high], ROWS_WITH_ROWS, preferred_element_type=jnp.float32
        )
        scores = jnp.where(allowed, scores * scale, -1e30)
        raised = jnp.exp(scores - jnp.max(scores, axis=0, keepdims=True))
        weight = (raised / jnp.sum(raised, axis=0, keepdims=True)).astype(jnp.bfloat16)
        mixed = jnp.dot(
            values_across[first : first + HD, :], weight, preferred_element_type=jnp.float32
        ).astype(jnp.bfloat16)
        attended_ref[first : first + HD, :] = mixed
        relative = turn((head // 2) ^ (me // 2), core)
        sent[relative, head % 2 * HD : (head % 2 + 1) * HD, :] = mixed
    for b in range(pairs):
        sent_refs[b][...] = sent[b]


def attend_ordered(kept, given, gain, w_qkv, pairs):
    width = kept.shape[1]
    rows = 2 * (kept.shape[0] - SUBLANES)
    inner = w_qkv.shape[1] // 3
    heads = inner // pairs
    return pl.pallas_call(
        attend_kernel,
        out_shape=(
            jax.ShapeDtypeStruct((inner, rows), jnp.bfloat16),
            jax.ShapeDtypeStruct((rows, width), jnp.bfloat16),
        )
        + (jax.ShapeDtypeStruct((heads, rows), jnp.bfloat16),) * pairs,
        in_specs=[VMEM] * 4,
        out_specs=(VMEM,) * (2 + pairs),
        scratch_shapes=[
            pltpu.VMEM((pairs, heads, rows), jnp.bfloat16),
        ],
        compiler_params=params(24),
        cost_estimate=cost(2 * rows * width * 3 * inner, 2 * w_qkv.size),
        name="attend",
    )(kept, given, in_hbm(gain), in_vmem(w_qkv))


def project_kernel(attended_ref, ordered_ref, w_ref, *encoded_refs):
    added = lax.dot_general(
        attended_ref[...], w_ref[...], TRANSPOSED, preferred_element_type=jnp.float32
    )
    encoded = (ordered_ref[...].astype(jnp.float32) + added).astype(jnp.bfloat16)
    size = ordered_ref.shape[0] // len(encoded_refs)
    for b, ref in enumerate(encoded_refs):
        ref[...] = encoded[b * size : (b + 1) * size]


def project_ordered(attended, ordered, w_out, pairs):
    rows, width = ordered.shape
    return pl.pallas_call(
        project_kernel,
        out_shape=(jax.ShapeDtypeStruct((rows // pairs, width), jnp.bfloat16),) * pairs,
        in_specs=[VMEM] * 3,
        out_specs=(VMEM,) * pairs,
        compiler_params=params(16),
        cost_estimate=cost(2 * ordered.size * w_out.shape[0], 2 * w_out.size),
        name="project",
    )(attended, ordered, w_out)


def gradient_kernel(scale, pairs, *refs):
    columns, blocks = refs[:pairs], refs[pairs : 2 * pairs]
    kept_ref, given_ref = refs[2 * pairs :]
    size = blocks[0].shape[0] // pairs
    head = kept_ref.shape[0]
    left = jnp.concatenate([ref[...] for ref in columns], 1)
    right = jnp.concatenate(
        [
            blocks[b ^ r][r * size : (r + 1) * size, :]
            for b in range(pairs)
            for r in range(pairs)
        ],
        0,
    )
    total = jnp.dot(left, right, preferred_element_type=jnp.float32) * scale
    first = lax.axis_index("enc") % 2 == 0
    kept_ref[...] = jnp.where(first, total[:head], total[head:])
    given_ref[...] = jnp.where(first, total[head:], total[:head]).astype(jnp.bfloat16)


def gradient_rows(columns, blocks, scale):
    pairs = len(blocks)
    heads, rows = columns[0].shape
    width = blocks[0].shape[1]
    return pl.pallas_call(
        functools.partial(gradient_kernel, scale, pairs),
        out_shape=(
            jax.ShapeDtypeStruct((heads // 2, width), jnp.float32),
            jax.ShapeDtypeStruct((heads // 2, width), jnp.bfloat16),
        ),
        in_specs=[VMEM] * (2 * pairs),
        out_specs=(VMEM, VMEM),
        compiler_params=params(24),
        cost_estimate=cost(2 * heads * rows * pairs * width, 2 * pairs * rows * width),
        name="gradient_rows",
    )(*columns, *blocks)


def place_kernel(slots_ref, *refs):
    embeddings_ref = refs[-1]
    arrived = jnp.concatenate([ref[...] for ref in refs[:-1]], 0)
    rows, width = arrived.shape
    tokens = embeddings_ref.shape[0]
    row = iota((rows, tokens), 0)
    window_rows = rows // (2 * (len(refs) - 1))
    holds = slots_ref[...] == slot_of_row(row, lax.axis_index("enc"), window_rows)
    for j in range(MERGE):
        put = jnp.where(holds & (row % MERGE == j), 1.0, 0.0).astype(jnp.bfloat16)
        part = lax.dot_general(put, arrived, TRANSPOSED, preferred_element_type=jnp.float32)
        embeddings_ref[:, j * width : (j + 1) * width] = part.astype(jnp.bfloat16)


def place_rows(slot_token, arrived):
    size, width = arrived[0].shape
    rows = size * len(arrived)
    tokens = slot_token.shape[0]
    return pl.pallas_call(
        place_kernel,
        out_shape=jax.ShapeDtypeStruct((tokens, MERGE * width), jnp.bfloat16),
        in_specs=[VMEM] * (1 + len(arrived)),
        out_specs=VMEM,
        compiler_params=params(16),
        cost_estimate=cost(2 * MERGE * rows * tokens * width, 2 * MERGE * tokens * width),
        name="place_rows",
    )(slot_token.reshape(1, tokens), *arrived)


def add_kernel(split, *refs):
    ins = len(refs) - (2 if split else 1)
    sums = [
        refs[i][...].astype(jnp.float32) + refs[i + 1][...].astype(jnp.float32)
        for i in range(0, ins, 2)
    ]
    outs = refs[ins:]
    whole = sums[0] if len(sums) == 1 else jnp.concatenate(sums, 1)
    width = outs[0].shape[1]
    for i, ref in enumerate(outs):
        ref[...] = whole[:, i * width : (i + 1) * width].astype(ref.dtype)


def add_halves(terms, kind, split):
    rows = terms[0][0].shape[0]
    width = sum(pair[0].shape[1] for pair in terms)
    count = 2 if split else 1
    return pl.pallas_call(
        functools.partial(add_kernel, split),
        out_shape=(jax.ShapeDtypeStruct((rows, width // count), kind),) * count,
        in_specs=[VMEM] * (2 * len(terms)),
        out_specs=(VMEM,) * count,
        compiler_params=params(8),
        cost_estimate=cost(rows * width, 8 * rows * width),
        name="add_halves",
    )(*[value for pair in terms for value in pair])


def after(value, other):
    return lax.optimization_barrier((value, other))[0]


def swap(value, axis, bits):
    size = lax.axis_size(axis)
    return lax.ppermute(value, axis, [(i, i ^ bits) for i in range(size)])


def chip_swap(value, relative):
    size = lax.axis_size("enc")
    return lax.ppermute(value, "enc", [(i, i ^ 2 * turn(relative, i % 2)) for i in range(size)])


def xor_slice(pixels, window_owner, window_len, slot_token, cotangent, w_qkv, w_out, gain):
    group = lax.axis_size("enc")
    replicas = lax.axis_size("rep")
    pairs = group // 2
    rows = pixels.shape[0]

    held, kept, given = pick_rows(window_owner, window_len, slot_token, pixels, cotangent)
    given = swap(given, "enc", 1)
    blocks = [held] + [chip_swap(held, b) for b in range(1, pairs)]
    attended, ordered, *sent = attend_ordered(kept, given, gain, w_qkv, pairs)
    columns = [sent[0]] + [chip_swap(sent[b], b) for b in range(1, pairs)]
    encoded = project_ordered(attended, ordered, w_out, pairs)
    scale = 1.0 / math.sqrt(rows * group * replicas)
    mine, other = gradient_rows(columns, blocks, scale)
    halves = add_halves([(mine, swap(other, "enc", 1))], jnp.bfloat16, split=True)
    arrived = [encoded[0]]
    for b in range(1, pairs):
        arrived.append(chip_swap(after(encoded[b], halves[0]), b))
    bits = [1 << i for i in range(replicas.bit_length() - 1)]
    for first, last in zip(bits, bits[::-1]):
        done = first == bits[-1]
        if done:
            halves = [after(half, arrived) for half in halves]
        swapped = [swap(halves[0], "rep", first), swap(halves[1], "rep", last)]
        halves = add_halves(
            list(zip(halves, swapped)), jnp.float32 if done else jnp.bfloat16, split=not done
        )
    total = halves[0]
    embeddings = place_rows(slot_token, arrived)
    return (embeddings, total)


def solution(mesh):
    def shards(*args):
        group = mesh.shape["enc"]
        replicas = mesh.shape["rep"]
        square = group == 2 << PAIR_BITS and replicas & (replicas - 1) == 0 and replicas > 1
        whole = square and args[1].shape[0] == group
        return (xor_slice if whole else any_slice)(*args)

    return jax.shard_map(
        shards,
        mesh=mesh,
        in_specs=(
            P(("enc", "rep"), None),
            P(("enc", "rep")),
            P(("enc", "rep")),
            P(("enc", "rep")),
            P(("enc", "rep"), None),
            P(),
            P(),
            P(),
        ),
        out_specs=(P(("enc", "rep"), None), P("enc", None)),
        check_vma=False,
    )
```

```python
import functools
import math

import jax
import jax.numpy as jnp
from jax import lax
from jax.experimental import pallas as pl
from jax.experimental.pallas import tpu as pltpu
from jax.sharding import PartitionSpec as P

HD = 80
HEADS = 8
MERGE = 4


def normalize(inputs, gain):
    values = inputs.astype(jnp.float32)
    mean_square = jnp.mean(values * values, axis=-1, keepdims=True)
    return (values * lax.rsqrt(mean_square + 1e-06) * gain).astype(jnp.bfloat16)


def attend(windows, lengths, w_qkv, gain):
    number, window_size, feature_width = windows.shape
    inner_width = w_qkv.shape[1] // 3
    flat_rows = windows.reshape(number * window_size, feature_width)
    normed = normalize(flat_rows, gain)
    projected = jnp.dot(normed, w_qkv, preferred_element_type=jnp.float32).astype(jnp.bfloat16)
    queries = projected[:, :inner_width].reshape(number, window_size, HEADS, HD)
    keys_all = projected[:, inner_width : 2 * inner_width].reshape(number, window_size, HEADS, HD)
    values_all = projected[:, 2 * inner_width :].reshape(number, window_size, HEADS, HD)
    scores = jnp.einsum(
        "nqhd,nkhd->nhqk", queries, keys_all, preferred_element_type=jnp.float32
    ) / math.sqrt(HD)
    live_keys = jnp.arange(window_size, dtype=jnp.int32)[None, :] < lengths[:, None]
    scores = jnp.where(live_keys[:, None, None, :], scores, -1e30)
    weights = jax.nn.softmax(scores, axis=-1).astype(jnp.bfloat16)
    attended = jnp.einsum(
        "nhqk,nkhd->nqhd", weights, values_all, preferred_element_type=jnp.float32
    )
    return attended.astype(jnp.bfloat16).reshape(number * window_size, inner_width)


def project(flat_rows, attended, w_out):
    encoded = flat_rows.astype(jnp.float32) + jnp.dot(
        attended, w_out, preferred_element_type=jnp.float32
    )
    return encoded.astype(jnp.bfloat16)


def any_slice(pixels, window_owner, window_len, slot_token, cotangent, w_qkv, w_out, gain):
    group_size = lax.axis_size("enc")
    replica_count = lax.axis_size("rep")
    feature_width = pixels.shape[1]
    window_count = window_owner.shape[0]
    window_rows = pixels.shape[0] // window_count
    tokens_each = window_rows // MERGE
    merged_width = MERGE * feature_width
    owner_ids = jnp.arange(group_size, dtype=jnp.int32)
    route = (window_owner[None, :] == owner_ids[:, None]).astype(jnp.bfloat16)
    slot_ids = jnp.arange(group_size * tokens_each, dtype=jnp.int32)
    placing = (slot_token[:, None] == slot_ids[None, :]).astype(jnp.bfloat16)
    attended = attend(
        pixels.reshape(window_count, window_rows, feature_width), window_len, w_qkv, gain
    )
    encoded = project(pixels, attended, w_out)
    outgoing = jnp.dot(
        route,
        encoded.reshape(window_count, window_rows * feature_width),
        preferred_element_type=jnp.float32,
    )
    outgoing = outgoing.astype(jnp.bfloat16).reshape(group_size, tokens_each, merged_width)
    arrived = lax.all_to_all(outgoing, "enc", split_axis=0, concat_axis=0, tiled=True)
    embeddings = jnp.dot(
        placing,
        arrived.reshape(group_size * tokens_each, merged_width),
        preferred_element_type=jnp.float32,
    ).astype(jnp.bfloat16)
    returning = lax.dot_general(
        placing, cotangent, (((0,), (0,)), ((), ())), preferred_element_type=jnp.float32
    )
    returning = returning.astype(jnp.bfloat16).reshape(group_size, tokens_each, merged_width)
    answered = lax.all_to_all(returning, "enc", split_axis=0, concat_axis=0, tiled=True)
    d_encoded = lax.dot_general(
        route,
        answered.reshape(group_size, tokens_each * merged_width),
        (((0,), (0,)), ((), ())),
        preferred_element_type=jnp.float32,
    )
    d_encoded = d_encoded.astype(jnp.bfloat16).reshape(window_count * window_rows, feature_width)
    reduced = lax.psum_scatter(
        lax.dot_general(
            attended, d_encoded, (((0,), (0,)), ((), ())), preferred_element_type=jnp.float32
        ),
        "enc",
        scatter_dimension=0,
        tiled=True,
    )
    summed = lax.psum(reduced, "rep")
    patch_total = window_count * window_rows * group_size * replica_count
    gradient = summed / math.sqrt(patch_total)
    return (embeddings, gradient)


LANES = 128
SUBLANES = 16
PAIR_BITS = 2
NEAR = 100
PLACE = 200
VMEM = pl.BlockSpec(memory_space=pltpu.VMEM)
HBM = pl.BlockSpec(memory_space=pltpu.HBM)
SMEM = pl.BlockSpec(memory_space=pltpu.SMEM)
TRANSPOSED = (((0,), (0,)), ((), ()))
ROWS_WITH_ROWS = (((1,), (1,)), ((), ()))


def turn(relative, core):
    other = relative % 2 * 2 + relative // 2
    if isinstance(core, int):
        return other if core else relative
    return jnp.where(core == 1, other, relative)


def iota(shape, dim):
    return lax.broadcasted_iota(jnp.int32, shape, dim)


def cost(flops, moved):
    return pl.CostEstimate(flops=flops, bytes_accessed=moved, transcendentals=0)


def params(mib):
    return pltpu.CompilerParams(vmem_limit_bytes=mib * 1024 * 1024)


def in_hbm(value):
    return pltpu.with_memory_space_constraint(value, pltpu.HBM)


def in_vmem(value):
    return pltpu.with_memory_space_constraint(value, pltpu.VMEM)


def place(index, size):
    return pl.ds(pl.multiple_of(index * size, size), size)


def slot_of_row(row, me, window_rows):
    pair = turn(row // (2 * window_rows), me % 2) ^ (me // 2)
    source = pair * 2 + row // window_rows % 2
    return source * (window_rows // MERGE) + row % window_rows // MERGE


def pick_kernel(
    owner_hbm, len_hbm, slots_hbm, pixels_hbm, cotangent_hbm, held_ref, kept_ref, given_ref,
    owner_ref, len_ref, slots_ref, pixels_buf, parts, windows_buf, sems,
):
    rows, width = held_ref.shape
    tokens = cotangent_hbm.shape[0]
    windows = owner_ref.shape[0]
    window_rows = rows // windows
    me = lax.axis_index("enc")
    pairs_of_refs = [
        (slots_hbm, slots_ref),
        (owner_hbm, owner_ref),
        (len_hbm, len_ref),
    ]
    for j in range(MERGE):
        pairs_of_refs.append((cotangent_hbm.at[:, pl.ds(j * width, width)], parts.at[j]))
    pairs_of_refs.append((pixels_hbm, pixels_buf))
    copies = [
        pltpu.make_async_copy(source, target, sems.at[i])
        for i, (source, target) in enumerate(pairs_of_refs)
    ]
    for copy in copies:
        copy.start()
    row = iota((rows, tokens), 0)
    copies[0].wait()
    holds = slots_ref[...] == slot_of_row(row, me, window_rows)
    picks = [
        jnp.where(holds & (row % MERGE == j), 1.0, 0.0).astype(jnp.bfloat16) for j in range(MERGE)
    ]
    held = None
    for j in range(MERGE):
        copies[3 + j].wait()
        term = jnp.dot(picks[j], parts[j], preferred_element_type=jnp.float32)
        held = term if held is None else held + term
    held_ref[...] = held.astype(jnp.bfloat16)
    copies[1].wait()
    copies[2].wait()
    copies[3 + MERGE].wait()
    which = iota((SUBLANES, width), 0)
    lengths = [jnp.zeros((SUBLANES, width), jnp.int32)] * 2
    for w in range(windows):
        owner = owner_ref[w]
        across = (owner + me) % 2
        relative = turn((owner // 2) ^ (me // 2), owner % 2)
        windows_buf[across, place(relative, window_rows), :] = pixels_buf[
            w * window_rows : (w + 1) * window_rows, :
        ]
        for side in range(2):
            here = jnp.where(across == side, relative, -1)
            lengths[side] = jnp.where(which == here, len_ref[w], lengths[side])
    for side, ref in enumerate((kept_ref, given_ref)):
        ref[: rows // 2, :] = windows_buf[side]
        ref[rows // 2 :, :] = lengths[side].astype(jnp.float32).astype(jnp.bfloat16)


def pick_rows(window_owner, window_len, slot_token, pixels, cotangent):
    rows, width = pixels.shape
    tokens = cotangent.shape[0]
    half = jax.ShapeDtypeStruct((rows // 2 + SUBLANES, width), jnp.bfloat16)
    return pl.pallas_call(
        pick_kernel,
        out_shape=(jax.ShapeDtypeStruct((rows, width), jnp.bfloat16), half, half),
        in_specs=[HBM] * 5,
        out_specs=(VMEM, VMEM, VMEM),
        scratch_shapes=[
            pltpu.SMEM(window_owner.shape, jnp.int32),
            pltpu.SMEM(window_len.shape, jnp.int32),
            pltpu.VMEM((1, tokens), jnp.int32),
            pltpu.VMEM((rows, width), jnp.bfloat16),
            pltpu.VMEM((MERGE, tokens, width), jnp.bfloat16),
            pltpu.VMEM((2, rows // 2, width), jnp.bfloat16),
            pltpu.SemaphoreType.DMA((MERGE + 4,)),
        ],
        compiler_params=params(16),
        cost_estimate=cost(200 * MERGE * rows * tokens * width, 2 * cotangent.size),
        name="pick_rows",
    )(
        in_hbm(window_owner),
        in_hbm(window_len),
        in_hbm(slot_token.reshape(1, tokens)),
        in_hbm(pixels),
        in_hbm(cotangent),
    )


def attend_kernel(
    kept_ref, given_ref, gain_ref, w_ref, *refs
):
    attended_ref, ordered_ref = refs[:2]
    sent_refs = refs[2:-1]
    sent = refs[-1]
    rows, width = ordered_ref.shape
    pairs = len(sent_refs)
    window_rows = rows // (2 * pairs)
    inner = attended_ref.shape[0]
    me = lax.axis_index("enc")
    core = me % 2
    key_row = iota((rows, rows), 0)
    key_window = key_row // window_rows
    live = jnp.zeros((rows, rows), jnp.float32)
    for ref, side in ((kept_ref, core), (given_ref, 1 - core)):
        lengths = ref[rows // 2 :, :rows].astype(jnp.float32)
        for b in range(pairs):
            window = 2 * b + side
            ordered_ref[place(window, window_rows), :] = ref[
                b * window_rows : (b + 1) * window_rows, :
            ]
            live = jnp.where(key_window == window, lengths[b : b + 1], live)
    allowed = (key_window == iota((rows, rows), 1) // window_rows) & (
        (key_row % window_rows).astype(jnp.float32) < live
    )
    values = ordered_ref[...].astype(jnp.float32)
    mean_square = jnp.mean(values * values, axis=-1, keepdims=True)
    normed = (values * lax.rsqrt(mean_square + 1e-06) * gain_ref[...][None, :]).astype(jnp.bfloat16)
    projected = []
    for part in range(3):
        columns = w_ref[:, part * inner : (part + 1) * inner]
        projected.append(jnp.dot(normed, columns, preferred_element_type=jnp.float32))
    queries = projected[0].astype(jnp.bfloat16)
    keys_all = projected[1].astype(jnp.bfloat16)
    values_across = projected[2].T.astype(jnp.bfloat16)
    scale = 1.0 / math.sqrt(HD)
    for head in range(inner // HD):
        first = head * HD
        low = first // LANES * LANES
        high = -(-(first + HD) // LANES) * LANES
        lane = iota((rows, high - low), 1) + low
        own = (lane >= first) & (lane < first + HD)
        keys = jnp.where(own, keys_all[:, low:high], jnp.zeros((), jnp.bfloat16))
        scores = lax.dot_general(
            keys, queries[:, low:high], ROWS_WITH_ROWS, preferred_element_type=jnp.float32
        )
        scores = jnp.where(allowed, scores * scale, -1e30)
        raised = jnp.exp(scores - jnp.max(scores, axis=0, keepdims=True))
        weight = (raised / jnp.sum(raised, axis=0, keepdims=True)).astype(jnp.bfloat16)
        mixed = jnp.dot(
            values_across[first : first + HD, :], weight, preferred_element_type=jnp.float32
        ).astype(jnp.bfloat16)
        attended_ref[first : first + HD, :] = mixed
        relative = turn((head // 2) ^ (me // 2), core)
        sent[relative, head % 2 * HD : (head % 2 + 1) * HD, :] = mixed
    for b in range(pairs):
        sent_refs[b][...] = sent[b]


def attend_ordered(kept, given, gain, w_qkv, pairs):
    width = kept.shape[1]
    rows = 2 * (kept.shape[0] - SUBLANES)
    inner = w_qkv.shape[1] // 3
    heads = inner // pairs
    return pl.pallas_call(
        attend_kernel,
        out_shape=(
            jax.ShapeDtypeStruct((inner, rows), jnp.bfloat16),
            jax.ShapeDtypeStruct((rows, width), jnp.bfloat16),
        )
        + (jax.ShapeDtypeStruct((heads, rows), jnp.bfloat16),) * pairs,
        in_specs=[VMEM] * 4,
        out_specs=(VMEM,) * (2 + pairs),
        scratch_shapes=[
            pltpu.VMEM((pairs, heads, rows), jnp.bfloat16),
        ],
        compiler_params=params(24),
        cost_estimate=cost(2 * rows * width * 3 * inner, 2 * w_qkv.size),
        name="attend",
    )(kept, given, in_hbm(gain), in_vmem(w_qkv))


def project_kernel(attended_ref, ordered_ref, w_ref, *encoded_refs):
    added = lax.dot_general(
        attended_ref[...], w_ref[...], TRANSPOSED, preferred_element_type=jnp.float32
    )
    encoded = (ordered_ref[...].astype(jnp.float32) + added).astype(jnp.bfloat16)
    size = ordered_ref.shape[0] // len(encoded_refs)
    for b, ref in enumerate(encoded_refs):
        ref[...] = encoded[b * size : (b + 1) * size]


def project_ordered(attended, ordered, w_out, pairs):
    rows, width = ordered.shape
    return pl.pallas_call(
        project_kernel,
        out_shape=(jax.ShapeDtypeStruct((rows // pairs, width), jnp.bfloat16),) * pairs,
        in_specs=[VMEM] * 3,
        out_specs=(VMEM,) * pairs,
        compiler_params=params(16),
        cost_estimate=cost(2 * ordered.size * w_out.shape[0], 2 * w_out.size),
        name="project",
    )(attended, ordered, w_out)


def products(columns, blocks, offsets):
    pairs = len(columns)
    size = columns[0].shape[1] // pairs
    left, right = [], []
    for b in range(pairs):
        for offset in offsets:
            r = b ^ offset
            left.append(columns[b][:, r * size : (r + 1) * size])
            right.append(blocks[offsets.index(offset)][r * size : (r + 1) * size, :])
    return jnp.dot(
        jnp.concatenate(left, 1), jnp.concatenate(right, 0), preferred_element_type=jnp.float32
    )


def near_kernel(pairs, *refs):
    columns, blocks = refs[:pairs], refs[pairs:-1]
    refs[-1][...] = products(columns, blocks, list(range(pairs - 1)))


def far_kernel(scale, pairs, *refs):
    columns, block, near_ref = refs[:pairs], refs[pairs], refs[pairs + 1]
    kept_ref, given_ref = refs[pairs + 2 :]
    head = kept_ref.shape[0]
    total = (near_ref[...] + products(columns, [block], [pairs - 1])) * scale
    first = lax.axis_index("enc") % 2 == 0
    kept_ref[...] = jnp.where(first, total[:head], total[head:])
    given_ref[...] = jnp.where(first, total[head:], total[:head]).astype(jnp.bfloat16)


def near_rows(columns, blocks):
    heads, rows = columns[0].shape
    width = blocks[0].shape[1]
    return pl.pallas_call(
        functools.partial(near_kernel, len(columns)),
        out_shape=jax.ShapeDtypeStruct((heads, width), jnp.float32),
        in_specs=[VMEM] * (len(columns) + len(blocks)),
        out_specs=VMEM,
        compiler_params=params(24),
        cost_estimate=cost(NEAR * heads * rows * len(blocks) * width, 2 * len(blocks) * rows * width),
        name="near_rows",
    )(*columns, *blocks)


def far_rows(columns, block, near, scale):
    heads, rows = columns[0].shape
    width = block.shape[1]
    return pl.pallas_call(
        functools.partial(far_kernel, scale, len(columns)),
        out_shape=(
            jax.ShapeDtypeStruct((heads // 2, width), jnp.float32),
            jax.ShapeDtypeStruct((heads // 2, width), jnp.bfloat16),
        ),
        in_specs=[VMEM] * (len(columns) + 2),
        out_specs=(VMEM, VMEM),
        compiler_params=params(24),
        cost_estimate=cost(2 * heads * rows * width, 2 * rows * width),
        name="far_rows",
    )(*columns, block, near)


def place_kernel(slots_ref, *refs):
    embeddings_ref = refs[-1]
    arrived = jnp.concatenate([ref[...] for ref in refs[:-1]], 0)
    rows, width = arrived.shape
    tokens = embeddings_ref.shape[0]
    row = iota((rows, tokens), 0)
    window_rows = rows // (2 * (len(refs) - 1))
    holds = slots_ref[...] == slot_of_row(row, lax.axis_index("enc"), window_rows)
    for j in range(MERGE):
        put = jnp.where(holds & (row % MERGE == j), 1.0, 0.0).astype(jnp.bfloat16)
        part = lax.dot_general(put, arrived, TRANSPOSED, preferred_element_type=jnp.float32)
        embeddings_ref[:, j * width : (j + 1) * width] = part.astype(jnp.bfloat16)


def place_rows(slot_token, arrived):
    size, width = arrived[0].shape
    rows = size * len(arrived)
    tokens = slot_token.shape[0]
    return pl.pallas_call(
        place_kernel,
        out_shape=jax.ShapeDtypeStruct((tokens, MERGE * width), jnp.bfloat16),
        in_specs=[VMEM] * (1 + len(arrived)),
        out_specs=VMEM,
        compiler_params=params(16),
        cost_estimate=cost(PLACE * MERGE * rows * tokens * width, 2 * MERGE * tokens * width),
        name="place_rows",
    )(slot_token.reshape(1, tokens), *arrived)


def add_kernel(split, *refs):
    ins = len(refs) - (2 if split else 1)
    sums = [
        refs[i][...].astype(jnp.float32) + refs[i + 1][...].astype(jnp.float32)
        for i in range(0, ins, 2)
    ]
    outs = refs[ins:]
    whole = sums[0] if len(sums) == 1 else jnp.concatenate(sums, 1)
    width = outs[0].shape[1]
    for i, ref in enumerate(outs):
        ref[...] = whole[:, i * width : (i + 1) * width].astype(ref.dtype)


def add_halves(terms, kind, split):
    rows = terms[0][0].shape[0]
    width = sum(pair[0].shape[1] for pair in terms)
    count = 2 if split else 1
    return pl.pallas_call(
        functools.partial(add_kernel, split),
        out_shape=(jax.ShapeDtypeStruct((rows, width // count), kind),) * count,
        in_specs=[VMEM] * (2 * len(terms)),
        out_specs=(VMEM,) * count,
        compiler_params=params(8),
        cost_estimate=cost(rows * width, 8 * rows * width),
        name="add_halves",
    )(*[value for pair in terms for value in pair])


def after(value, other):
    return lax.optimization_barrier((value, other))[0]


def swap(value, axis, bits):
    size = lax.axis_size(axis)
    return lax.ppermute(value, axis, [(i, i ^ bits) for i in range(size)])


def chip_swap(value, relative):
    size = lax.axis_size("enc")
    return lax.ppermute(value, "enc", [(i, i ^ 2 * turn(relative, i % 2)) for i in range(size)])


def xor_slice(pixels, window_owner, window_len, slot_token, cotangent, w_qkv, w_out, gain):
    group = lax.axis_size("enc")
    replicas = lax.axis_size("rep")
    pairs = group // 2
    rows = pixels.shape[0]

    held, kept, given = pick_rows(window_owner, window_len, slot_token, pixels, cotangent)
    given = swap(given, "enc", 1)
    blocks = [held, chip_swap(held, 1), chip_swap(held, 2)]
    attended, ordered, *sent = attend_ordered(kept, given, gain, w_qkv, pairs)
    columns = [sent[0]] + [chip_swap(sent[b], b) for b in range(1, pairs)]
    encoded = project_ordered(attended, ordered, w_out, pairs)
    blocks.append(chip_swap(after(blocks[1], encoded), 2))
    scale = 1.0 / math.sqrt(rows * group * replicas)
    near = near_rows(columns, blocks[:-1])
    mine, other = far_rows(columns, blocks[-1], near, scale)
    halves = add_halves([(mine, swap(other, "enc", 1))], jnp.bfloat16, split=True)
    arrived = [encoded[0]]
    for b in range(1, pairs):
        arrived.append(chip_swap(after(encoded[b], halves[0]), b))
    bits = [1 << i for i in range(replicas.bit_length() - 1)]
    for first, last in zip(bits, bits[::-1]):
        done = first == bits[-1]
        swapped = [swap(halves[0], "rep", first), swap(halves[1], "rep", last)]
        halves = add_halves(
            list(zip(halves, swapped)), jnp.float32 if done else jnp.bfloat16, split=not done
        )
    total = halves[0]
    embeddings = place_rows(slot_token, arrived)
    return (embeddings, total)


def solution(mesh):
    def shards(*args):
        group = mesh.shape["enc"]
        replicas = mesh.shape["rep"]
        square = group == 2 << PAIR_BITS and replicas & (replicas - 1) == 0 and replicas > 1
        whole = square and args[1].shape[0] == group
        return (xor_slice if whole else any_slice)(*args)

    return jax.shard_map(
        shards,
        mesh=mesh,
        in_specs=(
            P(("enc", "rep"), None),
            P(("enc", "rep")),
            P(("enc", "rep")),
            P(("enc", "rep")),
            P(("enc", "rep"), None),
            P(),
            P(),
            P(),
        ),
        out_specs=(P(("enc", "rep"), None), P("enc", None)),
        check_vma=False,
    )
```

```python
import functools
import math

import jax
import jax.numpy as jnp
from jax import lax
from jax.experimental import pallas as pl
from jax.experimental.pallas import tpu as pltpu
from jax.sharding import PartitionSpec as P

HD = 80
HEADS = 8
MERGE = 4


def normalize(inputs, gain):
    values = inputs.astype(jnp.float32)
    mean_square = jnp.mean(values * values, axis=-1, keepdims=True)
    return (values * lax.rsqrt(mean_square + 1e-06) * gain).astype(jnp.bfloat16)


def attend(windows, lengths, w_qkv, gain):
    number, window_size, feature_width = windows.shape
    inner_width = w_qkv.shape[1] // 3
    flat_rows = windows.reshape(number * window_size, feature_width)
    normed = normalize(flat_rows, gain)
    projected = jnp.dot(normed, w_qkv, preferred_element_type=jnp.float32).astype(jnp.bfloat16)
    queries = projected[:, :inner_width].reshape(number, window_size, HEADS, HD)
    keys_all = projected[:, inner_width : 2 * inner_width].reshape(number, window_size, HEADS, HD)
    values_all = projected[:, 2 * inner_width :].reshape(number, window_size, HEADS, HD)
    scores = jnp.einsum(
        "nqhd,nkhd->nhqk", queries, keys_all, preferred_element_type=jnp.float32
    ) / math.sqrt(HD)
    live_keys = jnp.arange(window_size, dtype=jnp.int32)[None, :] < lengths[:, None]
    scores = jnp.where(live_keys[:, None, None, :], scores, -1e30)
    weights = jax.nn.softmax(scores, axis=-1).astype(jnp.bfloat16)
    attended = jnp.einsum(
        "nhqk,nkhd->nqhd", weights, values_all, preferred_element_type=jnp.float32
    )
    return attended.astype(jnp.bfloat16).reshape(number * window_size, inner_width)


def project(flat_rows, attended, w_out):
    encoded = flat_rows.astype(jnp.float32) + jnp.dot(
        attended, w_out, preferred_element_type=jnp.float32
    )
    return encoded.astype(jnp.bfloat16)


def any_slice(pixels, window_owner, window_len, slot_token, cotangent, w_qkv, w_out, gain):
    group_size = lax.axis_size("enc")
    replica_count = lax.axis_size("rep")
    feature_width = pixels.shape[1]
    window_count = window_owner.shape[0]
    window_rows = pixels.shape[0] // window_count
    tokens_each = window_rows // MERGE
    merged_width = MERGE * feature_width
    owner_ids = jnp.arange(group_size, dtype=jnp.int32)
    route = (window_owner[None, :] == owner_ids[:, None]).astype(jnp.bfloat16)
    slot_ids = jnp.arange(group_size * tokens_each, dtype=jnp.int32)
    placing = (slot_token[:, None] == slot_ids[None, :]).astype(jnp.bfloat16)
    attended = attend(
        pixels.reshape(window_count, window_rows, feature_width), window_len, w_qkv, gain
    )
    encoded = project(pixels, attended, w_out)
    outgoing = jnp.dot(
        route,
        encoded.reshape(window_count, window_rows * feature_width),
        preferred_element_type=jnp.float32,
    )
    outgoing = outgoing.astype(jnp.bfloat16).reshape(group_size, tokens_each, merged_width)
    arrived = lax.all_to_all(outgoing, "enc", split_axis=0, concat_axis=0, tiled=True)
    embeddings = jnp.dot(
        placing,
        arrived.reshape(group_size * tokens_each, merged_width),
        preferred_element_type=jnp.float32,
    ).astype(jnp.bfloat16)
    returning = lax.dot_general(
        placing, cotangent, (((0,), (0,)), ((), ())), preferred_element_type=jnp.float32
    )
    returning = returning.astype(jnp.bfloat16).reshape(group_size, tokens_each, merged_width)
    answered = lax.all_to_all(returning, "enc", split_axis=0, concat_axis=0, tiled=True)
    d_encoded = lax.dot_general(
        route,
        answered.reshape(group_size, tokens_each * merged_width),
        (((0,), (0,)), ((), ())),
        preferred_element_type=jnp.float32,
    )
    d_encoded = d_encoded.astype(jnp.bfloat16).reshape(window_count * window_rows, feature_width)
    reduced = lax.psum_scatter(
        lax.dot_general(
            attended, d_encoded, (((0,), (0,)), ((), ())), preferred_element_type=jnp.float32
        ),
        "enc",
        scatter_dimension=0,
        tiled=True,
    )
    summed = lax.psum(reduced, "rep")
    patch_total = window_count * window_rows * group_size * replica_count
    gradient = summed / math.sqrt(patch_total)
    return (embeddings, gradient)


LANES = 128
SUBLANES = 16
PAIR_BITS = 2
NEAR = 100
PLACE = 200
VMEM = pl.BlockSpec(memory_space=pltpu.VMEM)
HBM = pl.BlockSpec(memory_space=pltpu.HBM)
SMEM = pl.BlockSpec(memory_space=pltpu.SMEM)
TRANSPOSED = (((0,), (0,)), ((), ()))
ROWS_WITH_ROWS = (((1,), (1,)), ((), ()))


def turn(relative, core):
    other = relative % 2 * 2 + relative // 2
    if isinstance(core, int):
        return other if core else relative
    return jnp.where(core == 1, other, relative)


def iota(shape, dim):
    return lax.broadcasted_iota(jnp.int32, shape, dim)


def cost(flops, moved):
    return pl.CostEstimate(flops=flops, bytes_accessed=moved, transcendentals=0)


def params(mib):
    return pltpu.CompilerParams(vmem_limit_bytes=mib * 1024 * 1024)


def in_hbm(value):
    return pltpu.with_memory_space_constraint(value, pltpu.HBM)


def in_vmem(value):
    return pltpu.with_memory_space_constraint(value, pltpu.VMEM)


def place(index, size):
    return pl.ds(pl.multiple_of(index * size, size), size)


def slot_of_row(row, me, window_rows):
    pair = turn(row // (2 * window_rows), me % 2) ^ (me // 2)
    source = pair * 2 + row // window_rows % 2
    return source * (window_rows // MERGE) + row % window_rows // MERGE


def pick_kernel(
    owner_hbm, len_hbm, slots_hbm, pixels_hbm, cotangent_hbm, held_ref, kept_ref, given_ref,
    owner_ref, len_ref, slots_ref, pixels_buf, parts, windows_buf, sems,
):
    rows, width = held_ref.shape
    tokens = cotangent_hbm.shape[0]
    windows = owner_ref.shape[0]
    window_rows = rows // windows
    me = lax.axis_index("enc")
    pairs_of_refs = [
        (slots_hbm, slots_ref),
        (owner_hbm, owner_ref),
        (len_hbm, len_ref),
    ]
    for j in range(MERGE):
        pairs_of_refs.append((cotangent_hbm.at[:, pl.ds(j * width, width)], parts.at[j]))
    pairs_of_refs.append((pixels_hbm, pixels_buf))
    copies = [
        pltpu.make_async_copy(source, target, sems.at[i])
        for i, (source, target) in enumerate(pairs_of_refs)
    ]
    for copy in copies:
        copy.start()
    row = iota((rows, tokens), 0)
    copies[0].wait()
    holds = slots_ref[...] == slot_of_row(row, me, window_rows)
    picks = [
        jnp.where(holds & (row % MERGE == j), 1.0, 0.0).astype(jnp.bfloat16) for j in range(MERGE)
    ]
    held = None
    for j in range(MERGE):
        copies[3 + j].wait()
        term = jnp.dot(picks[j], parts[j], preferred_element_type=jnp.float32)
        held = term if held is None else held + term
    held_ref[...] = held.astype(jnp.bfloat16)
    copies[1].wait()
    copies[2].wait()
    copies[3 + MERGE].wait()
    which = iota((SUBLANES, width), 0)
    lengths = [jnp.zeros((SUBLANES, width), jnp.int32)] * 2
    for w in range(windows):
        owner = owner_ref[w]
        across = (owner + me) % 2
        relative = turn((owner // 2) ^ (me // 2), owner % 2)
        windows_buf[across, place(relative, window_rows), :] = pixels_buf[
            w * window_rows : (w + 1) * window_rows, :
        ]
        for side in range(2):
            here = jnp.where(across == side, relative, -1)
            lengths[side] = jnp.where(which == here, len_ref[w], lengths[side])
    for side, ref in enumerate((kept_ref, given_ref)):
        ref[: rows // 2, :] = windows_buf[side]
        ref[rows // 2 :, :] = lengths[side].astype(jnp.float32).astype(jnp.bfloat16)


def pick_rows(window_owner, window_len, slot_token, pixels, cotangent):
    rows, width = pixels.shape
    tokens = cotangent.shape[0]
    half = jax.ShapeDtypeStruct((rows // 2 + SUBLANES, width), jnp.bfloat16)
    return pl.pallas_call(
        pick_kernel,
        out_shape=(jax.ShapeDtypeStruct((rows, width), jnp.bfloat16), half, half),
        in_specs=[HBM] * 5,
        out_specs=(VMEM, VMEM, VMEM),
        scratch_shapes=[
            pltpu.SMEM(window_owner.shape, jnp.int32),
            pltpu.SMEM(window_len.shape, jnp.int32),
            pltpu.VMEM((1, tokens), jnp.int32),
            pltpu.VMEM((rows, width), jnp.bfloat16),
            pltpu.VMEM((MERGE, tokens, width), jnp.bfloat16),
            pltpu.VMEM((2, rows // 2, width), jnp.bfloat16),
            pltpu.SemaphoreType.DMA((MERGE + 4,)),
        ],
        compiler_params=params(16),
        cost_estimate=cost(200 * MERGE * rows * tokens * width, 2 * cotangent.size),
        name="pick_rows",
    )(
        in_hbm(window_owner),
        in_hbm(window_len),
        in_hbm(slot_token.reshape(1, tokens)),
        in_hbm(pixels),
        in_hbm(cotangent),
    )


def attend_kernel(
    kept_ref, given_ref, gain_ref, w_ref, *refs
):
    attended_ref, ordered_ref = refs[:2]
    sent_refs = refs[2:-1]
    sent = refs[-1]
    rows, width = ordered_ref.shape
    pairs = len(sent_refs)
    window_rows = rows // (2 * pairs)
    inner = attended_ref.shape[0]
    me = lax.axis_index("enc")
    core = me % 2
    key_row = iota((rows, rows), 0)
    key_window = key_row // window_rows
    live = jnp.zeros((rows, rows), jnp.float32)
    for ref, side in ((kept_ref, core), (given_ref, 1 - core)):
        lengths = ref[rows // 2 :, :rows].astype(jnp.float32)
        for b in range(pairs):
            window = 2 * b + side
            ordered_ref[place(window, window_rows), :] = ref[
                b * window_rows : (b + 1) * window_rows, :
            ]
            live = jnp.where(key_window == window, lengths[b : b + 1], live)
    allowed = (key_window == iota((rows, rows), 1) // window_rows) & (
        (key_row % window_rows).astype(jnp.float32) < live
    )
    values = ordered_ref[...].astype(jnp.float32)
    mean_square = jnp.mean(values * values, axis=-1, keepdims=True)
    normed = (values * lax.rsqrt(mean_square + 1e-06) * gain_ref[...][None, :]).astype(jnp.bfloat16)
    projected = []
    for part in range(3):
        columns = w_ref[:, part * inner : (part + 1) * inner]
        projected.append(jnp.dot(normed, columns, preferred_element_type=jnp.float32))
    queries = projected[0].astype(jnp.bfloat16)
    keys_all = projected[1].astype(jnp.bfloat16)
    values_across = projected[2].T.astype(jnp.bfloat16)
    scale = 1.0 / math.sqrt(HD)
    for head in range(inner // HD):
        first = head * HD
        low = first // LANES * LANES
        high = -(-(first + HD) // LANES) * LANES
        lane = iota((rows, high - low), 1) + low
        own = (lane >= first) & (lane < first + HD)
        keys = jnp.where(own, keys_all[:, low:high], jnp.zeros((), jnp.bfloat16))
        scores = lax.dot_general(
            keys, queries[:, low:high], ROWS_WITH_ROWS, preferred_element_type=jnp.float32
        )
        scores = jnp.where(allowed, scores * scale, -1e30)
        raised = jnp.exp(scores - jnp.max(scores, axis=0, keepdims=True))
        weight = (raised / jnp.sum(raised, axis=0, keepdims=True)).astype(jnp.bfloat16)
        mixed = jnp.dot(
            values_across[first : first + HD, :], weight, preferred_element_type=jnp.float32
        ).astype(jnp.bfloat16)
        attended_ref[first : first + HD, :] = mixed
        relative = turn((head // 2) ^ (me // 2), core)
        sent[relative, head % 2 * HD : (head % 2 + 1) * HD, :] = mixed
    for b in range(pairs):
        sent_refs[b][...] = sent[b]


def attend_ordered(kept, given, gain, w_qkv, pairs):
    width = kept.shape[1]
    rows = 2 * (kept.shape[0] - SUBLANES)
    inner = w_qkv.shape[1] // 3
    heads = inner // pairs
    return pl.pallas_call(
        attend_kernel,
        out_shape=(
            jax.ShapeDtypeStruct((inner, rows), jnp.bfloat16),
            jax.ShapeDtypeStruct((rows, width), jnp.bfloat16),
        )
        + (jax.ShapeDtypeStruct((heads, rows), jnp.bfloat16),) * pairs,
        in_specs=[VMEM] * 4,
        out_specs=(VMEM,) * (2 + pairs),
        scratch_shapes=[
            pltpu.VMEM((pairs, heads, rows), jnp.bfloat16),
        ],
        compiler_params=params(24),
        cost_estimate=cost(2 * rows * width * 3 * inner, 2 * w_qkv.size),
        name="attend",
    )(kept, given, in_hbm(gain), in_vmem(w_qkv))


def project_kernel(attended_ref, ordered_ref, w_ref, *encoded_refs):
    added = lax.dot_general(
        attended_ref[...], w_ref[...], TRANSPOSED, preferred_element_type=jnp.float32
    )
    encoded = (ordered_ref[...].astype(jnp.float32) + added).astype(jnp.bfloat16)
    size = ordered_ref.shape[0] // len(encoded_refs)
    for b, ref in enumerate(encoded_refs):
        ref[...] = encoded[b * size : (b + 1) * size]


def project_ordered(attended, ordered, w_out, pairs):
    rows, width = ordered.shape
    return pl.pallas_call(
        project_kernel,
        out_shape=(jax.ShapeDtypeStruct((rows // pairs, width), jnp.bfloat16),) * pairs,
        in_specs=[VMEM] * 3,
        out_specs=(VMEM,) * pairs,
        compiler_params=params(16),
        cost_estimate=cost(2 * ordered.size * w_out.shape[0], 2 * w_out.size),
        name="project",
    )(attended, ordered, w_out)


def products(columns, blocks, offsets):
    pairs = len(columns)
    size = columns[0].shape[1] // pairs
    left, right = [], []
    for b in range(pairs):
        for offset in offsets:
            r = b ^ offset
            left.append(columns[b][:, r * size : (r + 1) * size])
            right.append(blocks[offsets.index(offset)][r * size : (r + 1) * size, :])
    return jnp.dot(
        jnp.concatenate(left, 1), jnp.concatenate(right, 0), preferred_element_type=jnp.float32
    )


def near_kernel(pairs, *refs):
    columns, blocks = refs[:pairs], refs[pairs:-1]
    refs[-1][...] = products(columns, blocks, list(range(pairs - 1)))


def far_kernel(scale, pairs, *refs):
    columns, block, near_ref = refs[:pairs], refs[pairs], refs[pairs + 1]
    kept_ref, given_ref = refs[pairs + 2 :]
    head = kept_ref.shape[0]
    total = (near_ref[...] + products(columns, [block], [pairs - 1])) * scale
    first = lax.axis_index("enc") % 2 == 0
    kept_ref[...] = jnp.where(first, total[:head], total[head:])
    given_ref[...] = jnp.where(first, total[head:], total[:head]).astype(jnp.bfloat16)


def near_rows(columns, blocks):
    heads, rows = columns[0].shape
    width = blocks[0].shape[1]
    return pl.pallas_call(
        functools.partial(near_kernel, len(columns)),
        out_shape=jax.ShapeDtypeStruct((heads, width), jnp.float32),
        in_specs=[VMEM] * (len(columns) + len(blocks)),
        out_specs=VMEM,
        compiler_params=params(24),
        cost_estimate=cost(NEAR * heads * rows * len(blocks) * width, 2 * len(blocks) * rows * width),
        name="near_rows",
    )(*columns, *blocks)


def far_rows(columns, block, near, scale):
    heads, rows = columns[0].shape
    width = block.shape[1]
    return pl.pallas_call(
        functools.partial(far_kernel, scale, len(columns)),
        out_shape=(
            jax.ShapeDtypeStruct((heads // 2, width), jnp.float32),
            jax.ShapeDtypeStruct((heads // 2, width), jnp.bfloat16),
        ),
        in_specs=[VMEM] * (len(columns) + 2),
        out_specs=(VMEM, VMEM),
        compiler_params=params(24),
        cost_estimate=cost(2 * heads * rows * width, 2 * rows * width),
        name="far_rows",
    )(*columns, block, near)


def place_kernel(slots_ref, *refs):
    embeddings_ref = refs[-1]
    arrived = jnp.concatenate([ref[...] for ref in refs[:-1]], 0)
    rows, width = arrived.shape
    tokens = embeddings_ref.shape[0]
    row = iota((rows, tokens), 0)
    window_rows = rows // (2 * (len(refs) - 1))
    holds = slots_ref[...] == slot_of_row(row, lax.axis_index("enc"), window_rows)
    for j in range(MERGE):
        put = jnp.where(holds & (row % MERGE == j), 1.0, 0.0).astype(jnp.bfloat16)
        part = lax.dot_general(put, arrived, TRANSPOSED, preferred_element_type=jnp.float32)
        embeddings_ref[:, j * width : (j + 1) * width] = part.astype(jnp.bfloat16)


def place_rows(slot_token, arrived):
    size, width = arrived[0].shape
    rows = size * len(arrived)
    tokens = slot_token.shape[0]
    return pl.pallas_call(
        place_kernel,
        out_shape=jax.ShapeDtypeStruct((tokens, MERGE * width), jnp.bfloat16),
        in_specs=[VMEM] * (1 + len(arrived)),
        out_specs=VMEM,
        compiler_params=params(16),
        cost_estimate=cost(PLACE * MERGE * rows * tokens * width, 2 * MERGE * tokens * width),
        name="place_rows",
    )(slot_token.reshape(1, tokens), *arrived)


def add_kernel(split, *refs):
    ins = len(refs) - (2 if split else 1)
    sums = [
        refs[i][...].astype(jnp.float32) + refs[i + 1][...].astype(jnp.float32)
        for i in range(0, ins, 2)
    ]
    outs = refs[ins:]
    whole = sums[0] if len(sums) == 1 else jnp.concatenate(sums, 1)
    width = outs[0].shape[1]
    for i, ref in enumerate(outs):
        ref[...] = whole[:, i * width : (i + 1) * width].astype(ref.dtype)


def add_halves(terms, kind, split):
    rows = terms[0][0].shape[0]
    width = sum(pair[0].shape[1] for pair in terms)
    count = 2 if split else 1
    return pl.pallas_call(
        functools.partial(add_kernel, split),
        out_shape=(jax.ShapeDtypeStruct((rows, width // count), kind),) * count,
        in_specs=[VMEM] * (2 * len(terms)),
        out_specs=(VMEM,) * count,
        compiler_params=params(8),
        cost_estimate=cost(rows * width, 8 * rows * width),
        name="add_halves",
    )(*[value for pair in terms for value in pair])


def after(value, other):
    return lax.optimization_barrier((value, other))[0]


def swap(value, axis, bits):
    size = lax.axis_size(axis)
    return lax.ppermute(value, axis, [(i, i ^ bits) for i in range(size)])


def chip_swap(value, relative):
    size = lax.axis_size("enc")
    return lax.ppermute(value, "enc", [(i, i ^ 2 * turn(relative, i % 2)) for i in range(size)])


def xor_slice(pixels, window_owner, window_len, slot_token, cotangent, w_qkv, w_out, gain):
    group = lax.axis_size("enc")
    replicas = lax.axis_size("rep")
    pairs = group // 2
    rows = pixels.shape[0]

    held, kept, given = pick_rows(window_owner, window_len, slot_token, pixels, cotangent)
    given = swap(given, "enc", 1)
    blocks = [held, chip_swap(held, 1), chip_swap(after(held, given), 2)]
    attended, ordered, *sent = attend_ordered(kept, given, gain, w_qkv, pairs)
    columns = [sent[0]] + [chip_swap(sent[b], b) for b in range(1, pairs)]
    encoded = project_ordered(attended, ordered, w_out, pairs)
    blocks.append(chip_swap(after(blocks[1], attended), 2))
    scale = 1.0 / math.sqrt(rows * group * replicas)
    near = near_rows(columns, blocks[:-1])
    mine, other = far_rows(columns, blocks[-1], near, scale)
    halves = add_halves([(mine, swap(other, "enc", 1))], jnp.bfloat16, split=True)
    arrived = [encoded[0]]
    for b in range(1, pairs):
        arrived.append(chip_swap(after(encoded[b], halves[0]), b))
    bits = [1 << i for i in range(replicas.bit_length() - 1)]
    for first, last in zip(bits, bits[::-1]):
        done = first == bits[-1]
        swapped = [swap(halves[0], "rep", first), swap(halves[1], "rep", last)]
        halves = add_halves(
            list(zip(halves, swapped)), jnp.float32 if done else jnp.bfloat16, split=not done
        )
    total = halves[0]
    embeddings = place_rows(slot_token, arrived)
    return (embeddings, total)


def solution(mesh):
    def shards(*args):
        group = mesh.shape["enc"]
        replicas = mesh.shape["rep"]
        square = group == 2 << PAIR_BITS and replicas & (replicas - 1) == 0 and replicas > 1
        whole = square and args[1].shape[0] == group
        return (xor_slice if whole else any_slice)(*args)

    return jax.shard_map(
        shards,
        mesh=mesh,
        in_specs=(
            P(("enc", "rep"), None),
            P(("enc", "rep")),
            P(("enc", "rep")),
            P(("enc", "rep")),
            P(("enc", "rep"), None),
            P(),
            P(),
            P(),
        ),
        out_specs=(P(("enc", "rep"), None), P("enc", None)),
        check_vma=False,
    )
```

```python
import functools
import math

import jax
import jax.numpy as jnp
from jax import lax
from jax.experimental import pallas as pl
from jax.experimental.pallas import tpu as pltpu
from jax.sharding import PartitionSpec as P

HD = 80
HEADS = 8
MERGE = 4


def normalize(inputs, gain):
    values = inputs.astype(jnp.float32)
    mean_square = jnp.mean(values * values, axis=-1, keepdims=True)
    return (values * lax.rsqrt(mean_square + 1e-06) * gain).astype(jnp.bfloat16)


def attend(windows, lengths, w_qkv, gain):
    number, window_size, feature_width = windows.shape
    inner_width = w_qkv.shape[1] // 3
    flat_rows = windows.reshape(number * window_size, feature_width)
    normed = normalize(flat_rows, gain)
    projected = jnp.dot(normed, w_qkv, preferred_element_type=jnp.float32).astype(jnp.bfloat16)
    queries = projected[:, :inner_width].reshape(number, window_size, HEADS, HD)
    keys_all = projected[:, inner_width : 2 * inner_width].reshape(number, window_size, HEADS, HD)
    values_all = projected[:, 2 * inner_width :].reshape(number, window_size, HEADS, HD)
    scores = jnp.einsum(
        "nqhd,nkhd->nhqk", queries, keys_all, preferred_element_type=jnp.float32
    ) / math.sqrt(HD)
    live_keys = jnp.arange(window_size, dtype=jnp.int32)[None, :] < lengths[:, None]
    scores = jnp.where(live_keys[:, None, None, :], scores, -1e30)
    weights = jax.nn.softmax(scores, axis=-1).astype(jnp.bfloat16)
    attended = jnp.einsum(
        "nhqk,nkhd->nqhd", weights, values_all, preferred_element_type=jnp.float32
    )
    return attended.astype(jnp.bfloat16).reshape(number * window_size, inner_width)


def project(flat_rows, attended, w_out):
    encoded = flat_rows.astype(jnp.float32) + jnp.dot(
        attended, w_out, preferred_element_type=jnp.float32
    )
    return encoded.astype(jnp.bfloat16)


def any_slice(pixels, window_owner, window_len, slot_token, cotangent, w_qkv, w_out, gain):
    group_size = lax.axis_size("enc")
    replica_count = lax.axis_size("rep")
    feature_width = pixels.shape[1]
    window_count = window_owner.shape[0]
    window_rows = pixels.shape[0] // window_count
    tokens_each = window_rows // MERGE
    merged_width = MERGE * feature_width
    owner_ids = jnp.arange(group_size, dtype=jnp.int32)
    route = (window_owner[None, :] == owner_ids[:, None]).astype(jnp.bfloat16)
    slot_ids = jnp.arange(group_size * tokens_each, dtype=jnp.int32)
    placing = (slot_token[:, None] == slot_ids[None, :]).astype(jnp.bfloat16)
    attended = attend(
        pixels.reshape(window_count, window_rows, feature_width), window_len, w_qkv, gain
    )
    encoded = project(pixels, attended, w_out)
    outgoing = jnp.dot(
        route,
        encoded.reshape(window_count, window_rows * feature_width),
        preferred_element_type=jnp.float32,
    )
    outgoing = outgoing.astype(jnp.bfloat16).reshape(group_size, tokens_each, merged_width)
    arrived = lax.all_to_all(outgoing, "enc", split_axis=0, concat_axis=0, tiled=True)
    embeddings = jnp.dot(
        placing,
        arrived.reshape(group_size * tokens_each, merged_width),
        preferred_element_type=jnp.float32,
    ).astype(jnp.bfloat16)
    returning = lax.dot_general(
        placing, cotangent, (((0,), (0,)), ((), ())), preferred_element_type=jnp.float32
    )
    returning = returning.astype(jnp.bfloat16).reshape(group_size, tokens_each, merged_width)
    answered = lax.all_to_all(returning, "enc", split_axis=0, concat_axis=0, tiled=True)
    d_encoded = lax.dot_general(
        route,
        answered.reshape(group_size, tokens_each * merged_width),
        (((0,), (0,)), ((), ())),
        preferred_element_type=jnp.float32,
    )
    d_encoded = d_encoded.astype(jnp.bfloat16).reshape(window_count * window_rows, feature_width)
    reduced = lax.psum_scatter(
        lax.dot_general(
            attended, d_encoded, (((0,), (0,)), ((), ())), preferred_element_type=jnp.float32
        ),
        "enc",
        scatter_dimension=0,
        tiled=True,
    )
    summed = lax.psum(reduced, "rep")
    patch_total = window_count * window_rows * group_size * replica_count
    gradient = summed / math.sqrt(patch_total)
    return (embeddings, gradient)


LANES = 128
SUBLANES = 16
PAIR_BITS = 2
NEAR = 40
PLACE = 200
VMEM = pl.BlockSpec(memory_space=pltpu.VMEM)
HBM = pl.BlockSpec(memory_space=pltpu.HBM)
SMEM = pl.BlockSpec(memory_space=pltpu.SMEM)
TRANSPOSED = (((0,), (0,)), ((), ()))
ROWS_WITH_ROWS = (((1,), (1,)), ((), ()))


def turn(relative, core):
    other = relative % 2 * 2 + relative // 2
    if isinstance(core, int):
        return other if core else relative
    return jnp.where(core == 1, other, relative)


def iota(shape, dim):
    return lax.broadcasted_iota(jnp.int32, shape, dim)


def cost(flops, moved):
    return pl.CostEstimate(flops=flops, bytes_accessed=moved, transcendentals=0)


def params(mib):
    return pltpu.CompilerParams(vmem_limit_bytes=mib * 1024 * 1024)


def in_hbm(value):
    return pltpu.with_memory_space_constraint(value, pltpu.HBM)


def in_vmem(value):
    return pltpu.with_memory_space_constraint(value, pltpu.VMEM)


def place(index, size):
    return pl.ds(pl.multiple_of(index * size, size), size)


def slot_of_row(row, me, window_rows):
    pair = turn(row // (2 * window_rows), me % 2) ^ (me // 2)
    source = pair * 2 + row // window_rows % 2
    return source * (window_rows // MERGE) + row % window_rows // MERGE


def pick_kernel(
    owner_hbm, len_hbm, slots_hbm, pixels_hbm, cotangent_hbm, held_ref, kept_ref, given_ref,
    owner_ref, len_ref, slots_ref, pixels_buf, parts, windows_buf, sems,
):
    rows, width = held_ref.shape
    tokens = cotangent_hbm.shape[0]
    windows = owner_ref.shape[0]
    window_rows = rows // windows
    me = lax.axis_index("enc")
    pairs_of_refs = [
        (owner_hbm, owner_ref),
        (len_hbm, len_ref),
        (slots_hbm, slots_ref),
        (pixels_hbm, pixels_buf),
    ]
    for j in range(MERGE):
        pairs_of_refs.append((cotangent_hbm.at[:, pl.ds(j * width, width)], parts.at[j]))
    copies = [
        pltpu.make_async_copy(source, target, sems.at[i])
        for i, (source, target) in enumerate(pairs_of_refs)
    ]
    for copy in copies:
        copy.start()
    for i in (0, 1, 3):
        copies[i].wait()
    which = iota((SUBLANES, width), 0)
    lengths = [jnp.zeros((SUBLANES, width), jnp.int32)] * 2
    for w in range(windows):
        owner = owner_ref[w]
        across = (owner + me) % 2
        relative = turn((owner // 2) ^ (me // 2), owner % 2)
        windows_buf[across, place(relative, window_rows), :] = pixels_buf[
            w * window_rows : (w + 1) * window_rows, :
        ]
        for side in range(2):
            here = jnp.where(across == side, relative, -1)
            lengths[side] = jnp.where(which == here, len_ref[w], lengths[side])
    for side, ref in enumerate((kept_ref, given_ref)):
        ref[: rows // 2, :] = windows_buf[side]
        ref[rows // 2 :, :] = lengths[side].astype(jnp.float32).astype(jnp.bfloat16)
    row = iota((rows, tokens), 0)
    copies[2].wait()
    holds = slots_ref[...] == slot_of_row(row, me, window_rows)
    picks = [
        jnp.where(holds & (row % MERGE == j), 1.0, 0.0).astype(jnp.bfloat16) for j in range(MERGE)
    ]
    held = None
    for j in range(MERGE):
        copies[4 + j].wait()
        term = jnp.dot(picks[j], parts[j], preferred_element_type=jnp.float32)
        held = term if held is None else held + term
    held_ref[...] = held.astype(jnp.bfloat16)

def pick_rows(window_owner, window_len, slot_token, pixels, cotangent):
    rows, width = pixels.shape
    tokens = cotangent.shape[0]
    half = jax.ShapeDtypeStruct((rows // 2 + SUBLANES, width), jnp.bfloat16)
    return pl.pallas_call(
        pick_kernel,
        out_shape=(jax.ShapeDtypeStruct((rows, width), jnp.bfloat16), half, half),
        in_specs=[HBM] * 5,
        out_specs=(VMEM, VMEM, VMEM),
        scratch_shapes=[
            pltpu.SMEM(window_owner.shape, jnp.int32),
            pltpu.SMEM(window_len.shape, jnp.int32),
            pltpu.VMEM((1, tokens), jnp.int32),
            pltpu.VMEM((rows, width), jnp.bfloat16),
            pltpu.VMEM((MERGE, tokens, width), jnp.bfloat16),
            pltpu.VMEM((2, rows // 2, width), jnp.bfloat16),
            pltpu.SemaphoreType.DMA((MERGE + 4,)),
        ],
        compiler_params=params(16),
        cost_estimate=cost(200 * MERGE * rows * tokens * width, 2 * cotangent.size),
        name="pick_rows",
    )(
        in_hbm(window_owner),
        in_hbm(window_len),
        in_hbm(slot_token.reshape(1, tokens)),
        in_hbm(pixels),
        in_hbm(cotangent),
    )


def attend_kernel(
    kept_ref, given_ref, gain_ref, w_ref, *refs
):
    attended_ref, ordered_ref = refs[:2]
    sent_refs = refs[2:-1]
    sent = refs[-1]
    rows, width = ordered_ref.shape
    pairs = len(sent_refs)
    window_rows = rows // (2 * pairs)
    inner = attended_ref.shape[0]
    me = lax.axis_index("enc")
    core = me % 2
    key_row = iota((rows, rows), 0)
    key_window = key_row // window_rows
    live = jnp.zeros((rows, rows), jnp.float32)
    for ref, side in ((kept_ref, core), (given_ref, 1 - core)):
        lengths = ref[rows // 2 :, :rows].astype(jnp.float32)
        for b in range(pairs):
            window = 2 * b + side
            ordered_ref[place(window, window_rows), :] = ref[
                b * window_rows : (b + 1) * window_rows, :
            ]
            live = jnp.where(key_window == window, lengths[b : b + 1], live)
    allowed = (key_window == iota((rows, rows), 1) // window_rows) & (
        (key_row % window_rows).astype(jnp.float32) < live
    )
    values = ordered_ref[...].astype(jnp.float32)
    mean_square = jnp.mean(values * values, axis=-1, keepdims=True)
    normed = (values * lax.rsqrt(mean_square + 1e-06) * gain_ref[...][None, :]).astype(jnp.bfloat16)
    projected = []
    for part in range(3):
        columns = w_ref[:, part * inner : (part + 1) * inner]
        projected.append(jnp.dot(normed, columns, preferred_element_type=jnp.float32))
    queries = projected[0].astype(jnp.bfloat16)
    keys_all = projected[1].astype(jnp.bfloat16)
    values_across = projected[2].T.astype(jnp.bfloat16)
    scale = 1.0 / math.sqrt(HD)
    for head in range(inner // HD):
        first = head * HD
        low = first // LANES * LANES
        high = -(-(first + HD) // LANES) * LANES
        lane = iota((rows, high - low), 1) + low
        own = (lane >= first) & (lane < first + HD)
        keys = jnp.where(own, keys_all[:, low:high], jnp.zeros((), jnp.bfloat16))
        scores = lax.dot_general(
            keys, queries[:, low:high], ROWS_WITH_ROWS, preferred_element_type=jnp.float32
        )
        scores = jnp.where(allowed, scores * scale, -1e30)
        raised = jnp.exp(scores - jnp.max(scores, axis=0, keepdims=True))
        weight = (raised / jnp.sum(raised, axis=0, keepdims=True)).astype(jnp.bfloat16)
        mixed = jnp.dot(
            values_across[first : first + HD, :], weight, preferred_element_type=jnp.float32
        ).astype(jnp.bfloat16)
        attended_ref[first : first + HD, :] = mixed
        relative = turn((head // 2) ^ (me // 2), core)
        sent[relative, head % 2 * HD : (head % 2 + 1) * HD, :] = mixed
    for b in range(pairs):
        sent_refs[b][...] = sent[b]


def attend_ordered(kept, given, gain, w_qkv, pairs):
    width = kept.shape[1]
    rows = 2 * (kept.shape[0] - SUBLANES)
    inner = w_qkv.shape[1] // 3
    heads = inner // pairs
    return pl.pallas_call(
        attend_kernel,
        out_shape=(
            jax.ShapeDtypeStruct((inner, rows), jnp.bfloat16),
            jax.ShapeDtypeStruct((rows, width), jnp.bfloat16),
        )
        + (jax.ShapeDtypeStruct((heads, rows), jnp.bfloat16),) * pairs,
        in_specs=[VMEM] * 4,
        out_specs=(VMEM,) * (2 + pairs),
        scratch_shapes=[
            pltpu.VMEM((pairs, heads, rows), jnp.bfloat16),
        ],
        compiler_params=params(24),
        cost_estimate=cost(2 * rows * width * 3 * inner, 2 * w_qkv.size),
        name="attend",
    )(kept, given, in_hbm(gain), in_vmem(w_qkv))


def project_kernel(attended_ref, ordered_ref, w_ref, *encoded_refs):
    added = lax.dot_general(
        attended_ref[...], w_ref[...], TRANSPOSED, preferred_element_type=jnp.float32
    )
    encoded = (ordered_ref[...].astype(jnp.float32) + added).astype(jnp.bfloat16)
    size = ordered_ref.shape[0] // len(encoded_refs)
    for b, ref in enumerate(encoded_refs):
        ref[...] = encoded[b * size : (b + 1) * size]


def project_ordered(attended, ordered, w_out, pairs):
    rows, width = ordered.shape
    return pl.pallas_call(
        project_kernel,
        out_shape=(jax.ShapeDtypeStruct((rows // pairs, width), jnp.bfloat16),) * pairs,
        in_specs=[VMEM] * 3,
        out_specs=(VMEM,) * pairs,
        compiler_params=params(16),
        cost_estimate=cost(2 * ordered.size * w_out.shape[0], 2 * w_out.size),
        name="project",
    )(attended, ordered, w_out)


def products(columns, blocks, places):
    left, right = [], []
    for b, o in places:
        size = columns[b].shape[1] // (1 << PAIR_BITS)
        r = b ^ o
        left.append(columns[b][:, r * size : (r + 1) * size])
        right.append(blocks[o][r * size : (r + 1) * size, :])
    return jnp.dot(
        jnp.concatenate(left, 1), jnp.concatenate(right, 0), preferred_element_type=jnp.float32
    )


def near_kernel(pairs, *refs):
    columns, blocks = refs[: pairs - 1], refs[pairs - 1 : -1]
    near = range(pairs - 1)
    refs[-1][...] = products(columns, blocks, [(b, o) for b in near for o in near])


def far_kernel(scale, pairs, *refs):
    columns, blocks, near_ref = refs[:pairs], refs[pairs : 2 * pairs], refs[2 * pairs]
    kept_ref, given_ref = refs[2 * pairs + 1 :]
    head = kept_ref.shape[0]
    last = pairs - 1
    places = [(last, o) for o in range(pairs)] + [(b, last) for b in range(last)]
    total = (near_ref[...] + products(columns, blocks, places)) * scale
    first = lax.axis_index("enc") % 2 == 0
    kept_ref[...] = jnp.where(first, total[:head], total[head:])
    given_ref[...] = jnp.where(first, total[head:], total[:head]).astype(jnp.bfloat16)


def near_rows(columns, blocks):
    heads, rows = columns[0].shape
    width = blocks[0].shape[1]
    return pl.pallas_call(
        functools.partial(near_kernel, len(columns) + 1),
        out_shape=jax.ShapeDtypeStruct((heads, width), jnp.float32),
        in_specs=[VMEM] * (len(columns) + len(blocks)),
        out_specs=VMEM,
        compiler_params=params(24),
        cost_estimate=cost(NEAR * heads * rows * len(blocks) * width, 2 * len(blocks) * rows * width),
        name="near_rows",
    )(*columns, *blocks)


def far_rows(columns, blocks, near, scale):
    heads, rows = columns[0].shape
    width = near.shape[1]
    return pl.pallas_call(
        functools.partial(far_kernel, scale, len(columns)),
        out_shape=(
            jax.ShapeDtypeStruct((heads // 2, width), jnp.float32),
            jax.ShapeDtypeStruct((heads // 2, width), jnp.bfloat16),
        ),
        in_specs=[VMEM] * (2 * len(columns) + 1),
        out_specs=(VMEM, VMEM),
        compiler_params=params(24),
        cost_estimate=cost(2 * heads * rows * width, 2 * rows * width),
        name="far_rows",
    )(*columns, *blocks, near)


def place_kernel(slots_ref, *refs):
    embeddings_ref = refs[-1]
    arrived = jnp.concatenate([ref[...] for ref in refs[:-1]], 0)
    rows, width = arrived.shape
    tokens = embeddings_ref.shape[0]
    row = iota((rows, tokens), 0)
    window_rows = rows // (2 * (len(refs) - 1))
    holds = slots_ref[...] == slot_of_row(row, lax.axis_index("enc"), window_rows)
    for j in range(MERGE):
        put = jnp.where(holds & (row % MERGE == j), 1.0, 0.0).astype(jnp.bfloat16)
        part = lax.dot_general(put, arrived, TRANSPOSED, preferred_element_type=jnp.float32)
        embeddings_ref[:, j * width : (j + 1) * width] = part.astype(jnp.bfloat16)


def place_rows(slot_token, arrived):
    size, width = arrived[0].shape
    rows = size * len(arrived)
    tokens = slot_token.shape[0]
    return pl.pallas_call(
        place_kernel,
        out_shape=jax.ShapeDtypeStruct((tokens, MERGE * width), jnp.bfloat16),
        in_specs=[VMEM] * (1 + len(arrived)),
        out_specs=VMEM,
        compiler_params=params(16),
        cost_estimate=cost(PLACE * MERGE * rows * tokens * width, 2 * MERGE * tokens * width),
        name="place_rows",
    )(slot_token.reshape(1, tokens), *arrived)


def add_kernel(split, *refs):
    ins = len(refs) - (2 if split else 1)
    sums = [
        refs[i][...].astype(jnp.float32) + refs[i + 1][...].astype(jnp.float32)
        for i in range(0, ins, 2)
    ]
    outs = refs[ins:]
    whole = sums[0] if len(sums) == 1 else jnp.concatenate(sums, 1)
    width = outs[0].shape[1]
    for i, ref in enumerate(outs):
        ref[...] = whole[:, i * width : (i + 1) * width].astype(ref.dtype)


def add_halves(terms, kind, split):
    rows = terms[0][0].shape[0]
    width = sum(pair[0].shape[1] for pair in terms)
    count = 2 if split else 1
    return pl.pallas_call(
        functools.partial(add_kernel, split),
        out_shape=(jax.ShapeDtypeStruct((rows, width // count), kind),) * count,
        in_specs=[VMEM] * (2 * len(terms)),
        out_specs=(VMEM,) * count,
        compiler_params=params(8),
        cost_estimate=cost(rows * width, 8 * rows * width),
        name="add_halves",
    )(*[value for pair in terms for value in pair])


def after(value, other):
    return lax.optimization_barrier((value, other))[0]


def swap(value, axis, bits):
    size = lax.axis_size(axis)
    return lax.ppermute(value, axis, [(i, i ^ bits) for i in range(size)])


def chip_swap(value, relative):
    size = lax.axis_size("enc")
    return lax.ppermute(value, "enc", [(i, i ^ 2 * turn(relative, i % 2)) for i in range(size)])


def xor_slice(pixels, window_owner, window_len, slot_token, cotangent, w_qkv, w_out, gain):
    group = lax.axis_size("enc")
    replicas = lax.axis_size("rep")
    pairs = group // 2
    rows = pixels.shape[0]

    held, kept, given = pick_rows(window_owner, window_len, slot_token, pixels, cotangent)
    given = swap(given, "enc", 1)
    attended, ordered, *sent = attend_ordered(kept, given, gain, w_qkv, pairs)
    blocks = [held, chip_swap(held, 1), chip_swap(after(held, attended), 2)]
    blocks.append(chip_swap(after(blocks[1], attended), 2))
    columns = [sent[0]] + [chip_swap(sent[b], b) for b in range(1, pairs)]
    encoded = project_ordered(attended, ordered, w_out, pairs)
    scale = 1.0 / math.sqrt(rows * group * replicas)
    near = near_rows(columns[:-1], blocks[:-1])
    mine, other = far_rows(columns, blocks, near, scale)
    halves = add_halves([(mine, swap(other, "enc", 1))], jnp.bfloat16, split=True)
    arrived = [encoded[0]]
    for b in range(1, pairs):
        arrived.append(chip_swap(after(encoded[b], halves[0]), b))
    bits = [1 << i for i in range(replicas.bit_length() - 1)]
    for first, last in zip(bits, bits[::-1]):
        done = first == bits[-1]
        swapped = [swap(halves[0], "rep", first), swap(halves[1], "rep", last)]
        halves = add_halves(
            list(zip(halves, swapped)), jnp.float32 if done else jnp.bfloat16, split=not done
        )
    total = halves[0]
    embeddings = place_rows(slot_token, arrived)
    return (embeddings, total)


def solution(mesh):
    def shards(*args):
        group = mesh.shape["enc"]
        replicas = mesh.shape["rep"]
        square = group == 2 << PAIR_BITS and replicas & (replicas - 1) == 0 and replicas > 1
        whole = square and args[1].shape[0] == group
        return (xor_slice if whole else any_slice)(*args)

    return jax.shard_map(
        shards,
        mesh=mesh,
        in_specs=(
            P(("enc", "rep"), None),
            P(("enc", "rep")),
            P(("enc", "rep")),
            P(("enc", "rep")),
            P(("enc", "rep"), None),
            P(),
            P(),
            P(),
        ),
        out_specs=(P(("enc", "rep"), None), P("enc", None)),
        check_vma=False,
    )
```

```python
import functools
import math

import jax
import jax.numpy as jnp
from jax import lax
from jax.experimental import pallas as pl
from jax.experimental.pallas import tpu as pltpu
from jax.sharding import PartitionSpec as P

HD = 80
HEADS = 8
MERGE = 4


def normalize(inputs, gain):
    values = inputs.astype(jnp.float32)
    mean_square = jnp.mean(values * values, axis=-1, keepdims=True)
    return (values * lax.rsqrt(mean_square + 1e-06) * gain).astype(jnp.bfloat16)


def attend(windows, lengths, w_qkv, gain):
    number, window_size, feature_width = windows.shape
    inner_width = w_qkv.shape[1] // 3
    flat_rows = windows.reshape(number * window_size, feature_width)
    normed = normalize(flat_rows, gain)
    projected = jnp.dot(normed, w_qkv, preferred_element_type=jnp.float32).astype(jnp.bfloat16)
    queries = projected[:, :inner_width].reshape(number, window_size, HEADS, HD)
    keys_all = projected[:, inner_width : 2 * inner_width].reshape(number, window_size, HEADS, HD)
    values_all = projected[:, 2 * inner_width :].reshape(number, window_size, HEADS, HD)
    scores = jnp.einsum(
        "nqhd,nkhd->nhqk", queries, keys_all, preferred_element_type=jnp.float32
    ) / math.sqrt(HD)
    live_keys = jnp.arange(window_size, dtype=jnp.int32)[None, :] < lengths[:, None]
    scores = jnp.where(live_keys[:, None, None, :], scores, -1e30)
    weights = jax.nn.softmax(scores, axis=-1).astype(jnp.bfloat16)
    attended = jnp.einsum(
        "nhqk,nkhd->nqhd", weights, values_all, preferred_element_type=jnp.float32
    )
    return attended.astype(jnp.bfloat16).reshape(number * window_size, inner_width)


def project(flat_rows, attended, w_out):
    encoded = flat_rows.astype(jnp.float32) + jnp.dot(
        attended, w_out, preferred_element_type=jnp.float32
    )
    return encoded.astype(jnp.bfloat16)


def any_slice(pixels, window_owner, window_len, slot_token, cotangent, w_qkv, w_out, gain):
    group_size = lax.axis_size("enc")
    replica_count = lax.axis_size("rep")
    feature_width = pixels.shape[1]
    window_count = window_owner.shape[0]
    window_rows = pixels.shape[0] // window_count
    tokens_each = window_rows // MERGE
    merged_width = MERGE * feature_width
    owner_ids = jnp.arange(group_size, dtype=jnp.int32)
    route = (window_owner[None, :] == owner_ids[:, None]).astype(jnp.bfloat16)
    slot_ids = jnp.arange(group_size * tokens_each, dtype=jnp.int32)
    placing = (slot_token[:, None] == slot_ids[None, :]).astype(jnp.bfloat16)
    attended = attend(
        pixels.reshape(window_count, window_rows, feature_width), window_len, w_qkv, gain
    )
    encoded = project(pixels, attended, w_out)
    outgoing = jnp.dot(
        route,
        encoded.reshape(window_count, window_rows * feature_width),
        preferred_element_type=jnp.float32,
    )
    outgoing = outgoing.astype(jnp.bfloat16).reshape(group_size, tokens_each, merged_width)
    arrived = lax.all_to_all(outgoing, "enc", split_axis=0, concat_axis=0, tiled=True)
    embeddings = jnp.dot(
        placing,
        arrived.reshape(group_size * tokens_each, merged_width),
        preferred_element_type=jnp.float32,
    ).astype(jnp.bfloat16)
    returning = lax.dot_general(
        placing, cotangent, (((0,), (0,)), ((), ())), preferred_element_type=jnp.float32
    )
    returning = returning.astype(jnp.bfloat16).reshape(group_size, tokens_each, merged_width)
    answered = lax.all_to_all(returning, "enc", split_axis=0, concat_axis=0, tiled=True)
    d_encoded = lax.dot_general(
        route,
        answered.reshape(group_size, tokens_each * merged_width),
        (((0,), (0,)), ((), ())),
        preferred_element_type=jnp.float32,
    )
    d_encoded = d_encoded.astype(jnp.bfloat16).reshape(window_count * window_rows, feature_width)
    reduced = lax.psum_scatter(
        lax.dot_general(
            attended, d_encoded, (((0,), (0,)), ((), ())), preferred_element_type=jnp.float32
        ),
        "enc",
        scatter_dimension=0,
        tiled=True,
    )
    summed = lax.psum(reduced, "rep")
    patch_total = window_count * window_rows * group_size * replica_count
    gradient = summed / math.sqrt(patch_total)
    return (embeddings, gradient)


LANES = 128
SUBLANES = 16
PAIR_BITS = 2
NEAR = 40
PLACE = 200
VMEM = pl.BlockSpec(memory_space=pltpu.VMEM)
HBM = pl.BlockSpec(memory_space=pltpu.HBM)
SMEM = pl.BlockSpec(memory_space=pltpu.SMEM)
TRANSPOSED = (((0,), (0,)), ((), ()))
ROWS_WITH_ROWS = (((1,), (1,)), ((), ()))


def turn(relative, core):
    other = relative % 2 * 2 + relative // 2
    if isinstance(core, int):
        return other if core else relative
    return jnp.where(core == 1, other, relative)


def iota(shape, dim):
    return lax.broadcasted_iota(jnp.int32, shape, dim)


def cost(flops, moved):
    return pl.CostEstimate(flops=flops, bytes_accessed=moved, transcendentals=0)


def params(mib):
    return pltpu.CompilerParams(vmem_limit_bytes=mib * 1024 * 1024)


def in_hbm(value):
    return pltpu.with_memory_space_constraint(value, pltpu.HBM)


def in_vmem(value):
    return pltpu.with_memory_space_constraint(value, pltpu.VMEM)


def place(index, size):
    return pl.ds(pl.multiple_of(index * size, size), size)


def slot_of_row(row, me, window_rows):
    pair = turn(row // (2 * window_rows), me % 2) ^ (me // 2)
    source = pair * 2 + row // window_rows % 2
    return source * (window_rows // MERGE) + row % window_rows // MERGE


def pick_kernel(
    owner_hbm, len_hbm, slots_hbm, pixels_hbm, cotangent_hbm, held_ref, kept_ref, given_ref,
    owner_ref, len_ref, slots_ref, pixels_buf, parts, windows_buf, sems,
):
    rows, width = held_ref.shape
    tokens = cotangent_hbm.shape[0]
    windows = owner_ref.shape[0]
    window_rows = rows // windows
    me = lax.axis_index("enc")
    pairs_of_refs = [
        (owner_hbm, owner_ref),
        (len_hbm, len_ref),
        (slots_hbm, slots_ref),
        (pixels_hbm, pixels_buf),
    ]
    for j in range(MERGE):
        pairs_of_refs.append((cotangent_hbm.at[:, pl.ds(j * width, width)], parts.at[j]))
    copies = [
        pltpu.make_async_copy(source, target, sems.at[i])
        for i, (source, target) in enumerate(pairs_of_refs)
    ]
    for copy in copies:
        copy.start()
    for i in (0, 1, 3):
        copies[i].wait()
    which = iota((SUBLANES, width), 0)
    lengths = [jnp.zeros((SUBLANES, width), jnp.int32)] * 2
    for w in range(windows):
        owner = owner_ref[w]
        across = (owner + me) % 2
        relative = turn((owner // 2) ^ (me // 2), owner % 2)
        windows_buf[across, place(relative, window_rows), :] = pixels_buf[
            w * window_rows : (w + 1) * window_rows, :
        ]
        for side in range(2):
            here = jnp.where(across == side, relative, -1)
            lengths[side] = jnp.where(which == here, len_ref[w], lengths[side])
    for side, ref in enumerate((kept_ref, given_ref)):
        ref[: rows // 2, :] = windows_buf[side]
        ref[rows // 2 :, :] = lengths[side].astype(jnp.float32).astype(jnp.bfloat16)
    row = iota((rows, tokens), 0)
    copies[2].wait()
    holds = slots_ref[...] == slot_of_row(row, me, window_rows)
    picks = [
        jnp.where(holds & (row % MERGE == j), 1.0, 0.0).astype(jnp.bfloat16) for j in range(MERGE)
    ]
    held = None
    for j in range(MERGE):
        copies[4 + j].wait()
        term = jnp.dot(picks[j], parts[j], preferred_element_type=jnp.float32)
        held = term if held is None else held + term
    held_ref[...] = held.astype(jnp.bfloat16)

def pick_rows(window_owner, window_len, slot_token, pixels, cotangent):
    rows, width = pixels.shape
    tokens = cotangent.shape[0]
    half = jax.ShapeDtypeStruct((rows // 2 + SUBLANES, width), jnp.bfloat16)
    return pl.pallas_call(
        pick_kernel,
        out_shape=(jax.ShapeDtypeStruct((rows, width), jnp.bfloat16), half, half),
        in_specs=[HBM] * 5,
        out_specs=(VMEM, VMEM, VMEM),
        scratch_shapes=[
            pltpu.SMEM(window_owner.shape, jnp.int32),
            pltpu.SMEM(window_len.shape, jnp.int32),
            pltpu.VMEM((1, tokens), jnp.int32),
            pltpu.VMEM((rows, width), jnp.bfloat16),
            pltpu.VMEM((MERGE, tokens, width), jnp.bfloat16),
            pltpu.VMEM((2, rows // 2, width), jnp.bfloat16),
            pltpu.SemaphoreType.DMA((MERGE + 4,)),
        ],
        compiler_params=params(16),
        cost_estimate=cost(200 * MERGE * rows * tokens * width, 2 * cotangent.size),
        name="pick_rows",
    )(
        in_hbm(window_owner),
        in_hbm(window_len),
        in_hbm(slot_token.reshape(1, tokens)),
        in_hbm(pixels),
        in_hbm(cotangent),
    )


def qkv_kernel(kept_ref, given_ref, gain_ref, w_ref, qkv_ref, ordered_ref):
    rows = ordered_ref.shape[0]
    pairs = 1 << PAIR_BITS
    window_rows = rows // (2 * pairs)
    core = lax.axis_index("enc") % 2
    for ref, side in ((kept_ref, core), (given_ref, 1 - core)):
        for b in range(pairs):
            ordered_ref[place(2 * b + side, window_rows), :] = ref[
                b * window_rows : (b + 1) * window_rows, :
            ]
    values = ordered_ref[...].astype(jnp.float32)
    mean_square = jnp.mean(values * values, axis=-1, keepdims=True)
    normed = (values * lax.rsqrt(mean_square + 1e-06) * gain_ref[...][None, :]).astype(
        jnp.bfloat16
    )
    inner = w_ref.shape[1] // 3
    for part in range(3):
        columns = slice(part * inner, (part + 1) * inner)
        qkv_ref[:, columns] = jnp.dot(
            normed, w_ref[:, columns], preferred_element_type=jnp.float32
        ).astype(jnp.bfloat16)


def qkv_ordered(kept, given, gain, w_qkv):
    width = kept.shape[1]
    rows = 2 * (kept.shape[0] - SUBLANES)
    return pl.pallas_call(
        qkv_kernel,
        out_shape=(
            jax.ShapeDtypeStruct((rows, w_qkv.shape[1]), jnp.bfloat16),
            jax.ShapeDtypeStruct((rows, width), jnp.bfloat16),
        ),
        in_specs=[VMEM] * 4,
        out_specs=(VMEM,) * 2,
        compiler_params=params(24),
        cost_estimate=cost(2 * rows * w_qkv.size, 2 * w_qkv.size),
        name="qkv",
    )(kept, given, in_hbm(gain), in_vmem(w_qkv))


def attend_kernel(kept_ref, given_ref, qkv_ref, *refs):
    attended_ref, sent_refs, sent = refs[0], refs[1:-1], refs[-1]
    rows = qkv_ref.shape[0]
    pairs = len(sent_refs)
    window_rows = rows // (2 * pairs)
    inner = attended_ref.shape[0]
    me = lax.axis_index("enc")
    core = me % 2
    key_row = iota((rows, rows), 0)
    key_window = key_row // window_rows
    live = jnp.zeros((rows, rows), jnp.float32)
    for ref, side in ((kept_ref, core), (given_ref, 1 - core)):
        lengths = ref[rows // 2 :, :rows].astype(jnp.float32)
        for b in range(pairs):
            live = jnp.where(key_window == 2 * b + side, lengths[b : b + 1], live)
    allowed = (key_window == iota((rows, rows), 1) // window_rows) & (
        (key_row % window_rows).astype(jnp.float32) < live
    )
    values_across = qkv_ref[:, 2 * inner :].astype(jnp.float32).T.astype(jnp.bfloat16)
    scale = 1.0 / math.sqrt(HD)
    for head in range(inner // HD):
        first = head * HD
        low = first // LANES * LANES
        high = -(-(first + HD) // LANES) * LANES
        lane = iota((rows, high - low), 1) + low
        own = (lane >= first) & (lane < first + HD)
        keys = qkv_ref[:, inner + low : inner + high]
        keys = jnp.where(own, keys, jnp.zeros((), jnp.bfloat16))
        scores = lax.dot_general(
            keys, qkv_ref[:, low:high], ROWS_WITH_ROWS, preferred_element_type=jnp.float32
        )
        scores = jnp.where(allowed, scores * scale, -1e30)
        raised = jnp.exp(scores - jnp.max(scores, axis=0, keepdims=True))
        weight = (raised / jnp.sum(raised, axis=0, keepdims=True)).astype(jnp.bfloat16)
        mixed = jnp.dot(
            values_across[first : first + HD, :], weight, preferred_element_type=jnp.float32
        ).astype(jnp.bfloat16)
        attended_ref[first : first + HD, :] = mixed
        relative = turn((head // 2) ^ (me // 2), core)
        sent[relative, head % 2 * HD : (head % 2 + 1) * HD, :] = mixed
    for b in range(pairs):
        sent_refs[b][...] = sent[b]


def attend_ordered(kept, given, qkv, pairs):
    rows = qkv.shape[0]
    inner = qkv.shape[1] // 3
    heads = inner // pairs
    return pl.pallas_call(
        attend_kernel,
        out_shape=(jax.ShapeDtypeStruct((inner, rows), jnp.bfloat16),)
        + (jax.ShapeDtypeStruct((heads, rows), jnp.bfloat16),) * pairs,
        in_specs=[VMEM] * 3,
        out_specs=(VMEM,) * (1 + pairs),
        scratch_shapes=[pltpu.VMEM((pairs, heads, rows), jnp.bfloat16)],
        compiler_params=params(24),
        cost_estimate=cost(4 * rows * rows * inner, 6 * rows * inner),
        name="attend",
    )(kept, given, qkv)


def project_kernel(attended_ref, ordered_ref, w_ref, *encoded_refs):
    added = lax.dot_general(
        attended_ref[...], w_ref[...], TRANSPOSED, preferred_element_type=jnp.float32
    )
    encoded = (ordered_ref[...].astype(jnp.float32) + added).astype(jnp.bfloat16)
    size = ordered_ref.shape[0] // len(encoded_refs)
    for b, ref in enumerate(encoded_refs):
        ref[...] = encoded[b * size : (b + 1) * size]


def project_ordered(attended, ordered, w_out, pairs):
    rows, width = ordered.shape
    return pl.pallas_call(
        project_kernel,
        out_shape=(jax.ShapeDtypeStruct((rows // pairs, width), jnp.bfloat16),) * pairs,
        in_specs=[VMEM] * 3,
        out_specs=(VMEM,) * pairs,
        compiler_params=params(16),
        cost_estimate=cost(2 * ordered.size * w_out.shape[0], 2 * w_out.size),
        name="project",
    )(attended, ordered, w_out)


def products(columns, blocks, places):
    left, right = [], []
    for b, o in places:
        size = columns[b].shape[1] // (1 << PAIR_BITS)
        r = b ^ o
        left.append(columns[b][:, r * size : (r + 1) * size])
        right.append(blocks[o][r * size : (r + 1) * size, :])
    return jnp.dot(
        jnp.concatenate(left, 1), jnp.concatenate(right, 0), preferred_element_type=jnp.float32
    )


def near_kernel(pairs, *refs):
    columns, blocks = refs[: pairs - 1], refs[pairs - 1 : -1]
    near = range(pairs - 1)
    refs[-1][...] = products(columns, blocks, [(b, o) for b in near for o in near])


def far_kernel(scale, pairs, *refs):
    columns, blocks, near_ref = refs[:pairs], refs[pairs : 2 * pairs], refs[2 * pairs]
    kept_ref, given_ref = refs[2 * pairs + 1 :]
    head = kept_ref.shape[0]
    last = pairs - 1
    places = [(last, o) for o in range(pairs)] + [(b, last) for b in range(last)]
    total = (near_ref[...] + products(columns, blocks, places)) * scale
    first = lax.axis_index("enc") % 2 == 0
    kept_ref[...] = jnp.where(first, total[:head], total[head:])
    given_ref[...] = jnp.where(first, total[head:], total[:head]).astype(jnp.bfloat16)


def near_rows(columns, blocks):
    heads, rows = columns[0].shape
    width = blocks[0].shape[1]
    return pl.pallas_call(
        functools.partial(near_kernel, len(columns) + 1),
        out_shape=jax.ShapeDtypeStruct((heads, width), jnp.float32),
        in_specs=[VMEM] * (len(columns) + len(blocks)),
        out_specs=VMEM,
        compiler_params=params(24),
        cost_estimate=cost(NEAR * heads * rows * len(blocks) * width, 2 * len(blocks) * rows * width),
        name="near_rows",
    )(*columns, *blocks)


def far_rows(columns, blocks, near, scale):
    heads, rows = columns[0].shape
    width = near.shape[1]
    return pl.pallas_call(
        functools.partial(far_kernel, scale, len(columns)),
        out_shape=(
            jax.ShapeDtypeStruct((heads // 2, width), jnp.float32),
            jax.ShapeDtypeStruct((heads // 2, width), jnp.bfloat16),
        ),
        in_specs=[VMEM] * (2 * len(columns) + 1),
        out_specs=(VMEM, VMEM),
        compiler_params=params(24),
        cost_estimate=cost(2 * heads * rows * width, 2 * rows * width),
        name="far_rows",
    )(*columns, *blocks, near)


def place_kernel(slots_ref, *refs):
    embeddings_ref = refs[-1]
    arrived = jnp.concatenate([ref[...] for ref in refs[:-1]], 0)
    rows, width = arrived.shape
    tokens = embeddings_ref.shape[0]
    row = iota((rows, tokens), 0)
    window_rows = rows // (2 * (len(refs) - 1))
    holds = slots_ref[...] == slot_of_row(row, lax.axis_index("enc"), window_rows)
    for j in range(MERGE):
        put = jnp.where(holds & (row % MERGE == j), 1.0, 0.0).astype(jnp.bfloat16)
        part = lax.dot_general(put, arrived, TRANSPOSED, preferred_element_type=jnp.float32)
        embeddings_ref[:, j * width : (j + 1) * width] = part.astype(jnp.bfloat16)


def place_rows(slot_token, arrived):
    size, width = arrived[0].shape
    rows = size * len(arrived)
    tokens = slot_token.shape[0]
    return pl.pallas_call(
        place_kernel,
        out_shape=jax.ShapeDtypeStruct((tokens, MERGE * width), jnp.bfloat16),
        in_specs=[VMEM] * (1 + len(arrived)),
        out_specs=VMEM,
        compiler_params=params(16),
        cost_estimate=cost(PLACE * MERGE * rows * tokens * width, 2 * MERGE * tokens * width),
        name="place_rows",
    )(slot_token.reshape(1, tokens), *arrived)


def add_kernel(split, *refs):
    ins = len(refs) - (2 if split else 1)
    sums = [
        refs[i][...].astype(jnp.float32) + refs[i + 1][...].astype(jnp.float32)
        for i in range(0, ins, 2)
    ]
    outs = refs[ins:]
    whole = sums[0] if len(sums) == 1 else jnp.concatenate(sums, 1)
    width = outs[0].shape[1]
    for i, ref in enumerate(outs):
        ref[...] = whole[:, i * width : (i + 1) * width].astype(ref.dtype)


def add_halves(terms, kind, split):
    rows = terms[0][0].shape[0]
    width = sum(pair[0].shape[1] for pair in terms)
    count = 2 if split else 1
    return pl.pallas_call(
        functools.partial(add_kernel, split),
        out_shape=(jax.ShapeDtypeStruct((rows, width // count), kind),) * count,
        in_specs=[VMEM] * (2 * len(terms)),
        out_specs=(VMEM,) * count,
        compiler_params=params(8),
        cost_estimate=cost(rows * width, 8 * rows * width),
        name="add_halves",
    )(*[value for pair in terms for value in pair])


def after(value, other):
    return lax.optimization_barrier((value, other))[0]


def swap(value, axis, bits):
    size = lax.axis_size(axis)
    return lax.ppermute(value, axis, [(i, i ^ bits) for i in range(size)])


def chip_swap(value, relative):
    size = lax.axis_size("enc")
    return lax.ppermute(value, "enc", [(i, i ^ 2 * turn(relative, i % 2)) for i in range(size)])


def xor_slice(pixels, window_owner, window_len, slot_token, cotangent, w_qkv, w_out, gain):
    group = lax.axis_size("enc")
    replicas = lax.axis_size("rep")
    pairs = group // 2
    rows = pixels.shape[0]

    held, kept, given = pick_rows(window_owner, window_len, slot_token, pixels, cotangent)
    given = swap(given, "enc", 1)
    qkv, ordered = qkv_ordered(kept, given, gain, w_qkv)
    attended, *sent = attend_ordered(kept, given, qkv, pairs)
    blocks = [held, chip_swap(held, 1), chip_swap(after(held, qkv), 2)]
    blocks.append(chip_swap(after(blocks[1], attended), 2))
    columns = [sent[0]] + [chip_swap(sent[b], b) for b in range(1, pairs)]
    encoded = project_ordered(attended, ordered, w_out, pairs)
    scale = 1.0 / math.sqrt(rows * group * replicas)
    near = near_rows(columns[:-1], blocks[:-1])
    mine, other = far_rows(columns, blocks, near, scale)
    halves = add_halves([(mine, swap(other, "enc", 1))], jnp.bfloat16, split=True)
    arrived = [encoded[0]]
    for b in range(1, pairs):
        arrived.append(chip_swap(after(encoded[b], halves[0]), b))
    bits = [1 << i for i in range(replicas.bit_length() - 1)]
    for first, last in zip(bits, bits[::-1]):
        done = first == bits[-1]
        swapped = [swap(halves[0], "rep", first), swap(halves[1], "rep", last)]
        halves = add_halves(
            list(zip(halves, swapped)), jnp.float32 if done else jnp.bfloat16, split=not done
        )
    total = halves[0]
    embeddings = place_rows(slot_token, arrived)
    return (embeddings, total)


def solution(mesh):
    def shards(*args):
        group = mesh.shape["enc"]
        replicas = mesh.shape["rep"]
        square = group == 2 << PAIR_BITS and replicas & (replicas - 1) == 0 and replicas > 1
        whole = square and args[1].shape[0] == group
        return (xor_slice if whole else any_slice)(*args)

    return jax.shard_map(
        shards,
        mesh=mesh,
        in_specs=(
            P(("enc", "rep"), None),
            P(("enc", "rep")),
            P(("enc", "rep")),
            P(("enc", "rep")),
            P(("enc", "rep"), None),
            P(),
            P(),
            P(),
        ),
        out_specs=(P(("enc", "rep"), None), P("enc", None)),
        check_vma=False,
    )
```

```python
import functools
import math

import jax
import jax.numpy as jnp
from jax import lax
from jax.experimental import pallas as pl
from jax.experimental.pallas import tpu as pltpu
from jax.sharding import PartitionSpec as P

HD = 80
HEADS = 8
MERGE = 4


def normalize(inputs, gain):
    values = inputs.astype(jnp.float32)
    mean_square = jnp.mean(values * values, axis=-1, keepdims=True)
    return (values * lax.rsqrt(mean_square + 1e-06) * gain).astype(jnp.bfloat16)


def attend(windows, lengths, w_qkv, gain):
    number, window_size, feature_width = windows.shape
    inner_width = w_qkv.shape[1] // 3
    flat_rows = windows.reshape(number * window_size, feature_width)
    normed = normalize(flat_rows, gain)
    projected = jnp.dot(normed, w_qkv, preferred_element_type=jnp.float32).astype(jnp.bfloat16)
    queries = projected[:, :inner_width].reshape(number, window_size, HEADS, HD)
    keys_all = projected[:, inner_width : 2 * inner_width].reshape(number, window_size, HEADS, HD)
    values_all = projected[:, 2 * inner_width :].reshape(number, window_size, HEADS, HD)
    scores = jnp.einsum(
        "nqhd,nkhd->nhqk", queries, keys_all, preferred_element_type=jnp.float32
    ) / math.sqrt(HD)
    live_keys = jnp.arange(window_size, dtype=jnp.int32)[None, :] < lengths[:, None]
    scores = jnp.where(live_keys[:, None, None, :], scores, -1e30)
    weights = jax.nn.softmax(scores, axis=-1).astype(jnp.bfloat16)
    attended = jnp.einsum(
        "nhqk,nkhd->nqhd", weights, values_all, preferred_element_type=jnp.float32
    )
    return attended.astype(jnp.bfloat16).reshape(number * window_size, inner_width)


def project(flat_rows, attended, w_out):
    encoded = flat_rows.astype(jnp.float32) + jnp.dot(
        attended, w_out, preferred_element_type=jnp.float32
    )
    return encoded.astype(jnp.bfloat16)


def any_slice(pixels, window_owner, window_len, slot_token, cotangent, w_qkv, w_out, gain):
    group_size = lax.axis_size("enc")
    replica_count = lax.axis_size("rep")
    feature_width = pixels.shape[1]
    window_count = window_owner.shape[0]
    window_rows = pixels.shape[0] // window_count
    tokens_each = window_rows // MERGE
    merged_width = MERGE * feature_width
    owner_ids = jnp.arange(group_size, dtype=jnp.int32)
    route = (window_owner[None, :] == owner_ids[:, None]).astype(jnp.bfloat16)
    slot_ids = jnp.arange(group_size * tokens_each, dtype=jnp.int32)
    placing = (slot_token[:, None] == slot_ids[None, :]).astype(jnp.bfloat16)
    attended = attend(
        pixels.reshape(window_count, window_rows, feature_width), window_len, w_qkv, gain
    )
    encoded = project(pixels, attended, w_out)
    outgoing = jnp.dot(
        route,
        encoded.reshape(window_count, window_rows * feature_width),
        preferred_element_type=jnp.float32,
    )
    outgoing = outgoing.astype(jnp.bfloat16).reshape(group_size, tokens_each, merged_width)
    arrived = lax.all_to_all(outgoing, "enc", split_axis=0, concat_axis=0, tiled=True)
    embeddings = jnp.dot(
        placing,
        arrived.reshape(group_size * tokens_each, merged_width),
        preferred_element_type=jnp.float32,
    ).astype(jnp.bfloat16)
    returning = lax.dot_general(
        placing, cotangent, (((0,), (0,)), ((), ())), preferred_element_type=jnp.float32
    )
    returning = returning.astype(jnp.bfloat16).reshape(group_size, tokens_each, merged_width)
    answered = lax.all_to_all(returning, "enc", split_axis=0, concat_axis=0, tiled=True)
    d_encoded = lax.dot_general(
        route,
        answered.reshape(group_size, tokens_each * merged_width),
        (((0,), (0,)), ((), ())),
        preferred_element_type=jnp.float32,
    )
    d_encoded = d_encoded.astype(jnp.bfloat16).reshape(window_count * window_rows, feature_width)
    reduced = lax.psum_scatter(
        lax.dot_general(
            attended, d_encoded, (((0,), (0,)), ((), ())), preferred_element_type=jnp.float32
        ),
        "enc",
        scatter_dimension=0,
        tiled=True,
    )
    summed = lax.psum(reduced, "rep")
    patch_total = window_count * window_rows * group_size * replica_count
    gradient = summed / math.sqrt(patch_total)
    return (embeddings, gradient)


LANES = 128
SUBLANES = 16
PAIR_BITS = 2
NEAR = 40
LATE = 1
PLACE = 200
VMEM = pl.BlockSpec(memory_space=pltpu.VMEM)
HBM = pl.BlockSpec(memory_space=pltpu.HBM)
SMEM = pl.BlockSpec(memory_space=pltpu.SMEM)
TRANSPOSED = (((0,), (0,)), ((), ()))
ROWS_WITH_ROWS = (((1,), (1,)), ((), ()))


def turn(relative, core):
    other = relative % 2 * 2 + relative // 2
    if isinstance(core, int):
        return other if core else relative
    return jnp.where(core == 1, other, relative)


def iota(shape, dim):
    return lax.broadcasted_iota(jnp.int32, shape, dim)


def cost(flops, moved):
    return pl.CostEstimate(flops=flops, bytes_accessed=moved, transcendentals=0)


def params(mib):
    return pltpu.CompilerParams(vmem_limit_bytes=mib * 1024 * 1024)


def in_hbm(value):
    return pltpu.with_memory_space_constraint(value, pltpu.HBM)


def in_vmem(value):
    return pltpu.with_memory_space_constraint(value, pltpu.VMEM)


def place(index, size):
    return pl.ds(pl.multiple_of(index * size, size), size)


def slot_of_row(row, me, window_rows):
    pair = turn(row // (2 * window_rows), me % 2) ^ (me // 2)
    source = pair * 2 + row // window_rows % 2
    return source * (window_rows // MERGE) + row % window_rows // MERGE


def pick_kernel(
    owner_hbm, len_hbm, slots_hbm, pixels_hbm, cotangent_hbm, held_ref, kept_ref, given_ref,
    owner_ref, len_ref, slots_ref, pixels_buf, parts, windows_buf, sems,
):
    rows, width = held_ref.shape
    tokens = cotangent_hbm.shape[0]
    windows = owner_ref.shape[0]
    window_rows = rows // windows
    me = lax.axis_index("enc")
    pairs_of_refs = [
        (owner_hbm, owner_ref),
        (len_hbm, len_ref),
        (slots_hbm, slots_ref),
        (pixels_hbm, pixels_buf),
    ]
    for j in range(MERGE):
        pairs_of_refs.append((cotangent_hbm.at[:, pl.ds(j * width, width)], parts.at[j]))
    copies = [
        pltpu.make_async_copy(source, target, sems.at[i])
        for i, (source, target) in enumerate(pairs_of_refs)
    ]
    for copy in copies:
        copy.start()
    for i in (0, 1, 3):
        copies[i].wait()
    which = iota((SUBLANES, width), 0)
    lengths = [jnp.zeros((SUBLANES, width), jnp.int32)] * 2
    for w in range(windows):
        owner = owner_ref[w]
        across = (owner + me) % 2
        relative = turn((owner // 2) ^ (me // 2), owner % 2)
        windows_buf[across, place(relative, window_rows), :] = pixels_buf[
            w * window_rows : (w + 1) * window_rows, :
        ]
        for side in range(2):
            here = jnp.where(across == side, relative, -1)
            lengths[side] = jnp.where(which == here, len_ref[w], lengths[side])
    for side, ref in enumerate((kept_ref, given_ref)):
        ref[: rows // 2, :] = windows_buf[side]
        ref[rows // 2 :, :] = lengths[side].astype(jnp.float32).astype(jnp.bfloat16)
    row = iota((rows, tokens), 0)
    copies[2].wait()
    holds = slots_ref[...] == slot_of_row(row, me, window_rows)
    picks = [
        jnp.where(holds & (row % MERGE == j), 1.0, 0.0).astype(jnp.bfloat16) for j in range(MERGE)
    ]
    held = None
    for j in range(MERGE):
        copies[4 + j].wait()
        term = jnp.dot(picks[j], parts[j], preferred_element_type=jnp.float32)
        held = term if held is None else held + term
    held_ref[...] = held.astype(jnp.bfloat16)

def pick_rows(window_owner, window_len, slot_token, pixels, cotangent):
    rows, width = pixels.shape
    tokens = cotangent.shape[0]
    half = jax.ShapeDtypeStruct((rows // 2 + SUBLANES, width), jnp.bfloat16)
    return pl.pallas_call(
        pick_kernel,
        out_shape=(jax.ShapeDtypeStruct((rows, width), jnp.bfloat16), half, half),
        in_specs=[HBM] * 5,
        out_specs=(VMEM, VMEM, VMEM),
        scratch_shapes=[
            pltpu.SMEM(window_owner.shape, jnp.int32),
            pltpu.SMEM(window_len.shape, jnp.int32),
            pltpu.VMEM((1, tokens), jnp.int32),
            pltpu.VMEM((rows, width), jnp.bfloat16),
            pltpu.VMEM((MERGE, tokens, width), jnp.bfloat16),
            pltpu.VMEM((2, rows // 2, width), jnp.bfloat16),
            pltpu.SemaphoreType.DMA((MERGE + 4,)),
        ],
        compiler_params=params(16),
        cost_estimate=cost(200 * MERGE * rows * tokens * width, 2 * cotangent.size),
        name="pick_rows",
    )(
        in_hbm(window_owner),
        in_hbm(window_len),
        in_hbm(slot_token.reshape(1, tokens)),
        in_hbm(pixels),
        in_hbm(cotangent),
    )


def qkv_kernel(kept_ref, given_ref, gain_ref, w_ref, qkv_ref, ordered_ref):
    rows = ordered_ref.shape[0]
    pairs = 1 << PAIR_BITS
    window_rows = rows // (2 * pairs)
    core = lax.axis_index("enc") % 2
    for ref, side in ((kept_ref, core), (given_ref, 1 - core)):
        for b in range(pairs):
            ordered_ref[place(2 * b + side, window_rows), :] = ref[
                b * window_rows : (b + 1) * window_rows, :
            ]
    values = ordered_ref[...].astype(jnp.float32)
    mean_square = jnp.mean(values * values, axis=-1, keepdims=True)
    normed = (values * lax.rsqrt(mean_square + 1e-06) * gain_ref[...][None, :]).astype(
        jnp.bfloat16
    )
    inner = w_ref.shape[1] // 3
    for part in range(3):
        columns = slice(part * inner, (part + 1) * inner)
        qkv_ref[:, columns] = jnp.dot(
            normed, w_ref[:, columns], preferred_element_type=jnp.float32
        ).astype(jnp.bfloat16)


def qkv_ordered(kept, given, gain, w_qkv):
    width = kept.shape[1]
    rows = 2 * (kept.shape[0] - SUBLANES)
    return pl.pallas_call(
        qkv_kernel,
        out_shape=(
            jax.ShapeDtypeStruct((rows, w_qkv.shape[1]), jnp.bfloat16),
            jax.ShapeDtypeStruct((rows, width), jnp.bfloat16),
        ),
        in_specs=[VMEM] * 4,
        out_specs=(VMEM,) * 2,
        compiler_params=params(24),
        cost_estimate=cost(2 * rows * w_qkv.size, 2 * w_qkv.size),
        name="qkv",
    )(kept, given, in_hbm(gain), in_vmem(w_qkv))


def attend_kernel(kept_ref, given_ref, qkv_ref, *refs):
    attended_ref, sent_refs, sent = refs[0], refs[1:-1], refs[-1]
    rows = qkv_ref.shape[0]
    pairs = len(sent_refs)
    window_rows = rows // (2 * pairs)
    inner = attended_ref.shape[0]
    me = lax.axis_index("enc")
    core = me % 2
    key_row = iota((rows, rows), 0)
    key_window = key_row // window_rows
    live = jnp.zeros((rows, rows), jnp.float32)
    for ref, side in ((kept_ref, core), (given_ref, 1 - core)):
        lengths = ref[rows // 2 :, :rows].astype(jnp.float32)
        for b in range(pairs):
            live = jnp.where(key_window == 2 * b + side, lengths[b : b + 1], live)
    allowed = (key_window == iota((rows, rows), 1) // window_rows) & (
        (key_row % window_rows).astype(jnp.float32) < live
    )
    values_across = qkv_ref[:, 2 * inner :].astype(jnp.float32).T.astype(jnp.bfloat16)
    scale = 1.0 / math.sqrt(HD)
    for head in range(inner // HD):
        first = head * HD
        low = first // LANES * LANES
        high = -(-(first + HD) // LANES) * LANES
        lane = iota((rows, high - low), 1) + low
        own = (lane >= first) & (lane < first + HD)
        keys = qkv_ref[:, inner + low : inner + high]
        keys = jnp.where(own, keys, jnp.zeros((), jnp.bfloat16))
        scores = lax.dot_general(
            keys, qkv_ref[:, low:high], ROWS_WITH_ROWS, preferred_element_type=jnp.float32
        )
        scores = jnp.where(allowed, scores * scale, -1e30)
        raised = jnp.exp(scores - jnp.max(scores, axis=0, keepdims=True))
        weight = (raised / jnp.sum(raised, axis=0, keepdims=True)).astype(jnp.bfloat16)
        mixed = jnp.dot(
            values_across[first : first + HD, :], weight, preferred_element_type=jnp.float32
        ).astype(jnp.bfloat16)
        attended_ref[first : first + HD, :] = mixed
        relative = turn((head // 2) ^ (me // 2), core)
        sent[relative, head % 2 * HD : (head % 2 + 1) * HD, :] = mixed
    for b in range(pairs):
        sent_refs[b][...] = sent[b]


def attend_ordered(kept, given, qkv, pairs):
    rows = qkv.shape[0]
    inner = qkv.shape[1] // 3
    heads = inner // pairs
    return pl.pallas_call(
        attend_kernel,
        out_shape=(jax.ShapeDtypeStruct((inner, rows), jnp.bfloat16),)
        + (jax.ShapeDtypeStruct((heads, rows), jnp.bfloat16),) * pairs,
        in_specs=[VMEM] * 3,
        out_specs=(VMEM,) * (1 + pairs),
        scratch_shapes=[pltpu.VMEM((pairs, heads, rows), jnp.bfloat16)],
        compiler_params=params(24),
        cost_estimate=cost(4 * rows * rows * inner, 6 * rows * inner),
        name="attend",
    )(kept, given, qkv)


def project_kernel(attended_ref, ordered_ref, w_ref, *encoded_refs):
    added = lax.dot_general(
        attended_ref[...], w_ref[...], TRANSPOSED, preferred_element_type=jnp.float32
    )
    encoded = (ordered_ref[...].astype(jnp.float32) + added).astype(jnp.bfloat16)
    size = ordered_ref.shape[0] // len(encoded_refs)
    for b, ref in enumerate(encoded_refs):
        ref[...] = encoded[b * size : (b + 1) * size]


def project_ordered(attended, ordered, w_out, pairs):
    rows, width = ordered.shape
    return pl.pallas_call(
        project_kernel,
        out_shape=(jax.ShapeDtypeStruct((rows // pairs, width), jnp.bfloat16),) * pairs,
        in_specs=[VMEM] * 3,
        out_specs=(VMEM,) * pairs,
        compiler_params=params(16),
        cost_estimate=cost(2 * ordered.size * w_out.shape[0], 2 * w_out.size),
        name="project",
    )(attended, ordered, w_out)


def products(columns, blocks, places):
    left, right = [], []
    for b, o in places:
        size = columns[b].shape[1] // (1 << PAIR_BITS)
        r = b ^ o
        left.append(columns[b][:, r * size : (r + 1) * size])
        right.append(blocks[o][r * size : (r + 1) * size, :])
    return jnp.dot(
        jnp.concatenate(left, 1), jnp.concatenate(right, 0), preferred_element_type=jnp.float32
    )


def near_kernel(pairs, *refs):
    early = [b for b in range(pairs) if b != LATE]
    columns, blocks = dict(zip(early, refs)), refs[pairs - 1 : -1]
    refs[-1][...] = products(columns, blocks, [(b, o) for b in early for o in range(pairs - 1)])


def far_kernel(scale, pairs, *refs):
    columns, blocks, near_ref = refs[:pairs], refs[pairs : 2 * pairs], refs[2 * pairs]
    kept_ref, given_ref = refs[2 * pairs + 1 :]
    head = kept_ref.shape[0]
    last = pairs - 1
    places = [(LATE, o) for o in range(pairs)]
    places += [(b, last) for b in range(pairs) if b != LATE]
    total = (near_ref[...] + products(columns, blocks, places)) * scale
    first = lax.axis_index("enc") % 2 == 0
    kept_ref[...] = jnp.where(first, total[:head], total[head:])
    given_ref[...] = jnp.where(first, total[head:], total[:head]).astype(jnp.bfloat16)


def near_rows(columns, blocks):
    heads, rows = columns[0].shape
    width = blocks[0].shape[1]
    return pl.pallas_call(
        functools.partial(near_kernel, len(columns) + 1),
        out_shape=jax.ShapeDtypeStruct((heads, width), jnp.float32),
        in_specs=[VMEM] * (len(columns) + len(blocks)),
        out_specs=VMEM,
        compiler_params=params(24),
        cost_estimate=cost(NEAR * heads * rows * len(blocks) * width, 2 * len(blocks) * rows * width),
        name="near_rows",
    )(*columns, *blocks)


def far_rows(columns, blocks, near, scale):
    heads, rows = columns[0].shape
    width = near.shape[1]
    return pl.pallas_call(
        functools.partial(far_kernel, scale, len(columns)),
        out_shape=(
            jax.ShapeDtypeStruct((heads // 2, width), jnp.float32),
            jax.ShapeDtypeStruct((heads // 2, width), jnp.bfloat16),
        ),
        in_specs=[VMEM] * (2 * len(columns) + 1),
        out_specs=(VMEM, VMEM),
        compiler_params=params(24),
        cost_estimate=cost(2 * heads * rows * width, 2 * rows * width),
        name="far_rows",
    )(*columns, *blocks, near)


def place_kernel(slots_ref, *refs):
    embeddings_ref = refs[-1]
    arrived = jnp.concatenate([ref[...] for ref in refs[:-1]], 0)
    rows, width = arrived.shape
    tokens = embeddings_ref.shape[0]
    row = iota((rows, tokens), 0)
    window_rows = rows // (2 * (len(refs) - 1))
    holds = slots_ref[...] == slot_of_row(row, lax.axis_index("enc"), window_rows)
    for j in range(MERGE):
        put = jnp.where(holds & (row % MERGE == j), 1.0, 0.0).astype(jnp.bfloat16)
        part = lax.dot_general(put, arrived, TRANSPOSED, preferred_element_type=jnp.float32)
        embeddings_ref[:, j * width : (j + 1) * width] = part.astype(jnp.bfloat16)


def place_rows(slot_token, arrived):
    size, width = arrived[0].shape
    rows = size * len(arrived)
    tokens = slot_token.shape[0]
    return pl.pallas_call(
        place_kernel,
        out_shape=jax.ShapeDtypeStruct((tokens, MERGE * width), jnp.bfloat16),
        in_specs=[VMEM] * (1 + len(arrived)),
        out_specs=VMEM,
        compiler_params=params(16),
        cost_estimate=cost(PLACE * MERGE * rows * tokens * width, 2 * MERGE * tokens * width),
        name="place_rows",
    )(slot_token.reshape(1, tokens), *arrived)


def add_kernel(split, *refs):
    ins = len(refs) - (2 if split else 1)
    sums = [
        refs[i][...].astype(jnp.float32) + refs[i + 1][...].astype(jnp.float32)
        for i in range(0, ins, 2)
    ]
    outs = refs[ins:]
    whole = sums[0] if len(sums) == 1 else jnp.concatenate(sums, 1)
    width = outs[0].shape[1]
    for i, ref in enumerate(outs):
        ref[...] = whole[:, i * width : (i + 1) * width].astype(ref.dtype)


def add_halves(terms, kind, split):
    rows = terms[0][0].shape[0]
    width = sum(pair[0].shape[1] for pair in terms)
    count = 2 if split else 1
    return pl.pallas_call(
        functools.partial(add_kernel, split),
        out_shape=(jax.ShapeDtypeStruct((rows, width // count), kind),) * count,
        in_specs=[VMEM] * (2 * len(terms)),
        out_specs=(VMEM,) * count,
        compiler_params=params(8),
        cost_estimate=cost(rows * width, 8 * rows * width),
        name="add_halves",
    )(*[value for pair in terms for value in pair])


def after(value, other):
    return lax.optimization_barrier((value, other))[0]


def swap(value, axis, bits):
    size = lax.axis_size(axis)
    return lax.ppermute(value, axis, [(i, i ^ bits) for i in range(size)])


def chip_swap(value, relative):
    size = lax.axis_size("enc")
    return lax.ppermute(value, "enc", [(i, i ^ 2 * turn(relative, i % 2)) for i in range(size)])


def xor_slice(pixels, window_owner, window_len, slot_token, cotangent, w_qkv, w_out, gain):
    group = lax.axis_size("enc")
    replicas = lax.axis_size("rep")
    pairs = group // 2
    rows = pixels.shape[0]

    held, kept, given = pick_rows(window_owner, window_len, slot_token, pixels, cotangent)
    given = swap(given, "enc", 1)
    qkv, ordered = qkv_ordered(kept, given, gain, w_qkv)
    attended, *sent = attend_ordered(kept, given, qkv, pairs)
    blocks = [held, chip_swap(held, 1), chip_swap(after(held, qkv), 2)]
    blocks.append(chip_swap(after(blocks[1], attended), 2))
    columns = [sent[0]] + [chip_swap(sent[b], b) for b in range(1, pairs)]
    encoded = project_ordered(attended, ordered, w_out, pairs)
    scale = 1.0 / math.sqrt(rows * group * replicas)
    near = near_rows([columns[b] for b in range(pairs) if b != LATE], blocks[:-1])
    mine, other = far_rows(columns, blocks, near, scale)
    halves = add_halves([(mine, swap(other, "enc", 1))], jnp.bfloat16, split=True)
    arrived = [encoded[0]]
    for b in range(1, pairs):
        arrived.append(chip_swap(after(encoded[b], halves[0]), b))
    bits = [1 << i for i in range(replicas.bit_length() - 1)]
    for first, last in zip(bits, bits[::-1]):
        done = first == bits[-1]
        swapped = [swap(halves[0], "rep", first), swap(halves[1], "rep", last)]
        halves = add_halves(
            list(zip(halves, swapped)), jnp.float32 if done else jnp.bfloat16, split=not done
        )
    total = halves[0]
    embeddings = place_rows(slot_token, arrived)
    return (embeddings, total)


def solution(mesh):
    def shards(*args):
        group = mesh.shape["enc"]
        replicas = mesh.shape["rep"]
        square = group == 2 << PAIR_BITS and replicas & (replicas - 1) == 0 and replicas > 1
        whole = square and args[1].shape[0] == group
        return (xor_slice if whole else any_slice)(*args)

    return jax.shard_map(
        shards,
        mesh=mesh,
        in_specs=(
            P(("enc", "rep"), None),
            P(("enc", "rep")),
            P(("enc", "rep")),
            P(("enc", "rep")),
            P(("enc", "rep"), None),
            P(),
            P(),
            P(),
        ),
        out_specs=(P(("enc", "rep"), None), P("enc", None)),
        check_vma=False,
    )
```

```python
import functools
import math

import jax
import jax.numpy as jnp
from jax import lax
from jax.experimental import pallas as pl
from jax.experimental.pallas import tpu as pltpu
from jax.sharding import PartitionSpec as P

HD = 80
HEADS = 8
MERGE = 4


def normalize(inputs, gain):
    values = inputs.astype(jnp.float32)
    mean_square = jnp.mean(values * values, axis=-1, keepdims=True)
    return (values * lax.rsqrt(mean_square + 1e-06) * gain).astype(jnp.bfloat16)


def attend(windows, lengths, w_qkv, gain):
    number, window_size, feature_width = windows.shape
    inner_width = w_qkv.shape[1] // 3
    flat_rows = windows.reshape(number * window_size, feature_width)
    normed = normalize(flat_rows, gain)
    projected = jnp.dot(normed, w_qkv, preferred_element_type=jnp.float32).astype(jnp.bfloat16)
    queries = projected[:, :inner_width].reshape(number, window_size, HEADS, HD)
    keys_all = projected[:, inner_width : 2 * inner_width].reshape(number, window_size, HEADS, HD)
    values_all = projected[:, 2 * inner_width :].reshape(number, window_size, HEADS, HD)
    scores = jnp.einsum(
        "nqhd,nkhd->nhqk", queries, keys_all, preferred_element_type=jnp.float32
    ) / math.sqrt(HD)
    live_keys = jnp.arange(window_size, dtype=jnp.int32)[None, :] < lengths[:, None]
    scores = jnp.where(live_keys[:, None, None, :], scores, -1e30)
    weights = jax.nn.softmax(scores, axis=-1).astype(jnp.bfloat16)
    attended = jnp.einsum(
        "nhqk,nkhd->nqhd", weights, values_all, preferred_element_type=jnp.float32
    )
    return attended.astype(jnp.bfloat16).reshape(number * window_size, inner_width)


def project(flat_rows, attended, w_out):
    encoded = flat_rows.astype(jnp.float32) + jnp.dot(
        attended, w_out, preferred_element_type=jnp.float32
    )
    return encoded.astype(jnp.bfloat16)


def any_slice(pixels, window_owner, window_len, slot_token, cotangent, w_qkv, w_out, gain):
    group_size = lax.axis_size("enc")
    replica_count = lax.axis_size("rep")
    feature_width = pixels.shape[1]
    window_count = window_owner.shape[0]
    window_rows = pixels.shape[0] // window_count
    tokens_each = window_rows // MERGE
    merged_width = MERGE * feature_width
    owner_ids = jnp.arange(group_size, dtype=jnp.int32)
    route = (window_owner[None, :] == owner_ids[:, None]).astype(jnp.bfloat16)
    slot_ids = jnp.arange(group_size * tokens_each, dtype=jnp.int32)
    placing = (slot_token[:, None] == slot_ids[None, :]).astype(jnp.bfloat16)
    attended = attend(
        pixels.reshape(window_count, window_rows, feature_width), window_len, w_qkv, gain
    )
    encoded = project(pixels, attended, w_out)
    outgoing = jnp.dot(
        route,
        encoded.reshape(window_count, window_rows * feature_width),
        preferred_element_type=jnp.float32,
    )
    outgoing = outgoing.astype(jnp.bfloat16).reshape(group_size, tokens_each, merged_width)
    arrived = lax.all_to_all(outgoing, "enc", split_axis=0, concat_axis=0, tiled=True)
    embeddings = jnp.dot(
        placing,
        arrived.reshape(group_size * tokens_each, merged_width),
        preferred_element_type=jnp.float32,
    ).astype(jnp.bfloat16)
    returning = lax.dot_general(
        placing, cotangent, (((0,), (0,)), ((), ())), preferred_element_type=jnp.float32
    )
    returning = returning.astype(jnp.bfloat16).reshape(group_size, tokens_each, merged_width)
    answered = lax.all_to_all(returning, "enc", split_axis=0, concat_axis=0, tiled=True)
    d_encoded = lax.dot_general(
        route,
        answered.reshape(group_size, tokens_each * merged_width),
        (((0,), (0,)), ((), ())),
        preferred_element_type=jnp.float32,
    )
    d_encoded = d_encoded.astype(jnp.bfloat16).reshape(window_count * window_rows, feature_width)
    reduced = lax.psum_scatter(
        lax.dot_general(
            attended, d_encoded, (((0,), (0,)), ((), ())), preferred_element_type=jnp.float32
        ),
        "enc",
        scatter_dimension=0,
        tiled=True,
    )
    summed = lax.psum(reduced, "rep")
    patch_total = window_count * window_rows * group_size * replica_count
    gradient = summed / math.sqrt(patch_total)
    return (embeddings, gradient)


LANES = 128
SUBLANES = 16
PAIR_BITS = 2
NEAR = 40
PLACE = 200
VMEM = pl.BlockSpec(memory_space=pltpu.VMEM)
HBM = pl.BlockSpec(memory_space=pltpu.HBM)
SMEM = pl.BlockSpec(memory_space=pltpu.SMEM)
TRANSPOSED = (((0,), (0,)), ((), ()))
ROWS_WITH_ROWS = (((1,), (1,)), ((), ()))


def turn(relative, core):
    other = relative % 2 * 2 + relative // 2
    if isinstance(core, int):
        return other if core else relative
    return jnp.where(core == 1, other, relative)


def iota(shape, dim):
    return lax.broadcasted_iota(jnp.int32, shape, dim)


def cost(flops, moved):
    return pl.CostEstimate(flops=flops, bytes_accessed=moved, transcendentals=0)


def params(mib):
    return pltpu.CompilerParams(vmem_limit_bytes=mib * 1024 * 1024)


def in_hbm(value):
    return pltpu.with_memory_space_constraint(value, pltpu.HBM)


def in_vmem(value):
    return pltpu.with_memory_space_constraint(value, pltpu.VMEM)


def place(index, size):
    return pl.ds(pl.multiple_of(index * size, size), size)


def slot_of_row(row, me, window_rows):
    pair = turn(row // (2 * window_rows), me % 2) ^ (me // 2)
    source = pair * 2 + row // window_rows % 2
    return source * (window_rows // MERGE) + row % window_rows // MERGE


def pick_kernel(
    owner_hbm, len_hbm, slots_hbm, pixels_hbm, cotangent_hbm, held_ref, kept_ref, given_ref,
    owner_ref, len_ref, slots_ref, pixels_buf, parts, windows_buf, sems,
):
    rows, width = held_ref.shape
    tokens = cotangent_hbm.shape[0]
    windows = owner_ref.shape[0]
    window_rows = rows // windows
    me = lax.axis_index("enc")
    pairs_of_refs = [
        (owner_hbm, owner_ref),
        (len_hbm, len_ref),
        (slots_hbm, slots_ref),
        (pixels_hbm, pixels_buf),
    ]
    for j in range(MERGE):
        pairs_of_refs.append((cotangent_hbm.at[:, pl.ds(j * width, width)], parts.at[j]))
    copies = [
        pltpu.make_async_copy(source, target, sems.at[i])
        for i, (source, target) in enumerate(pairs_of_refs)
    ]
    for copy in copies:
        copy.start()
    for i in (0, 1, 3):
        copies[i].wait()
    which = iota((SUBLANES, width), 0)
    lengths = [jnp.zeros((SUBLANES, width), jnp.int32)] * 2
    for w in range(windows):
        owner = owner_ref[w]
        across = (owner + me) % 2
        relative = turn((owner // 2) ^ (me // 2), owner % 2)
        windows_buf[across, place(relative, window_rows), :] = pixels_buf[
            w * window_rows : (w + 1) * window_rows, :
        ]
        for side in range(2):
            here = jnp.where(across == side, relative, -1)
            lengths[side] = jnp.where(which == here, len_ref[w], lengths[side])
    for side, ref in enumerate((kept_ref, given_ref)):
        ref[: rows // 2, :] = windows_buf[side]
        ref[rows // 2 :, :] = lengths[side].astype(jnp.float32).astype(jnp.bfloat16)
    row = iota((rows, tokens), 0)
    copies[2].wait()
    holds = slots_ref[...] == slot_of_row(row, me, window_rows)
    picks = [
        jnp.where(holds & (row % MERGE == j), 1.0, 0.0).astype(jnp.bfloat16) for j in range(MERGE)
    ]
    held = None
    for j in range(MERGE):
        copies[4 + j].wait()
        term = jnp.dot(picks[j], parts[j], preferred_element_type=jnp.float32)
        held = term if held is None else held + term
    held_ref[...] = held.astype(jnp.bfloat16)

def pick_rows(window_owner, window_len, slot_token, pixels, cotangent):
    rows, width = pixels.shape
    tokens = cotangent.shape[0]
    half = jax.ShapeDtypeStruct((rows // 2 + SUBLANES, width), jnp.bfloat16)
    return pl.pallas_call(
        pick_kernel,
        out_shape=(jax.ShapeDtypeStruct((rows, width), jnp.bfloat16), half, half),
        in_specs=[HBM] * 5,
        out_specs=(VMEM, VMEM, VMEM),
        scratch_shapes=[
            pltpu.SMEM(window_owner.shape, jnp.int32),
            pltpu.SMEM(window_len.shape, jnp.int32),
            pltpu.VMEM((1, tokens), jnp.int32),
            pltpu.VMEM((rows, width), jnp.bfloat16),
            pltpu.VMEM((MERGE, tokens, width), jnp.bfloat16),
            pltpu.VMEM((2, rows // 2, width), jnp.bfloat16),
            pltpu.SemaphoreType.DMA((MERGE + 4,)),
        ],
        compiler_params=params(16),
        cost_estimate=cost(200 * MERGE * rows * tokens * width, 2 * cotangent.size),
        name="pick_rows",
    )(
        in_hbm(window_owner),
        in_hbm(window_len),
        in_hbm(slot_token.reshape(1, tokens)),
        in_hbm(pixels),
        in_hbm(cotangent),
    )


def qkv_kernel(kept_ref, given_ref, gain_ref, w_ref, qkv_ref, ordered_ref):
    rows = ordered_ref.shape[0]
    pairs = 1 << PAIR_BITS
    window_rows = rows // (2 * pairs)
    core = lax.axis_index("enc") % 2
    for ref, side in ((kept_ref, core), (given_ref, 1 - core)):
        for b in range(pairs):
            ordered_ref[place(2 * b + side, window_rows), :] = ref[
                b * window_rows : (b + 1) * window_rows, :
            ]
    values = ordered_ref[...].astype(jnp.float32)
    mean_square = jnp.mean(values * values, axis=-1, keepdims=True)
    normed = (values * lax.rsqrt(mean_square + 1e-06) * gain_ref[...][None, :]).astype(
        jnp.bfloat16
    )
    inner = w_ref.shape[1] // 3
    for part in range(3):
        columns = slice(part * inner, (part + 1) * inner)
        qkv_ref[:, columns] = jnp.dot(
            normed, w_ref[:, columns], preferred_element_type=jnp.float32
        ).astype(jnp.bfloat16)


def qkv_ordered(kept, given, gain, w_qkv):
    width = kept.shape[1]
    rows = 2 * (kept.shape[0] - SUBLANES)
    return pl.pallas_call(
        qkv_kernel,
        out_shape=(
            jax.ShapeDtypeStruct((rows, w_qkv.shape[1]), jnp.bfloat16),
            jax.ShapeDtypeStruct((rows, width), jnp.bfloat16),
        ),
        in_specs=[VMEM] * 4,
        out_specs=(VMEM,) * 2,
        compiler_params=params(24),
        cost_estimate=cost(2 * rows * w_qkv.size, 2 * w_qkv.size),
        name="qkv",
    )(kept, given, in_hbm(gain), in_vmem(w_qkv))


def attend_kernel(kept_ref, given_ref, qkv_ref, *refs):
    attended_ref, sent_refs, sent = refs[0], refs[1:-1], refs[-1]
    rows = qkv_ref.shape[0]
    pairs = len(sent_refs)
    window_rows = rows // (2 * pairs)
    inner = attended_ref.shape[0]
    me = lax.axis_index("enc")
    core = me % 2
    key_row = iota((rows, rows), 0)
    key_window = key_row // window_rows
    live = jnp.zeros((rows, rows), jnp.float32)
    for ref, side in ((kept_ref, core), (given_ref, 1 - core)):
        lengths = ref[rows // 2 :, :rows].astype(jnp.float32)
        for b in range(pairs):
            live = jnp.where(key_window == 2 * b + side, lengths[b : b + 1], live)
    allowed = (key_window == iota((rows, rows), 1) // window_rows) & (
        (key_row % window_rows).astype(jnp.float32) < live
    )
    values_across = qkv_ref[:, 2 * inner :].astype(jnp.float32).T.astype(jnp.bfloat16)
    scale = 1.0 / math.sqrt(HD)
    for head in range(inner // HD):
        first = head * HD
        low = first // LANES * LANES
        high = -(-(first + HD) // LANES) * LANES
        lane = iota((rows, high - low), 1) + low
        own = (lane >= first) & (lane < first + HD)
        keys = qkv_ref[:, inner + low : inner + high]
        keys = jnp.where(own, keys, jnp.zeros((), jnp.bfloat16))
        scores = lax.dot_general(
            keys, qkv_ref[:, low:high], ROWS_WITH_ROWS, preferred_element_type=jnp.float32
        )
        scores = jnp.where(allowed, scores * scale, -1e30)
        raised = jnp.exp(scores - jnp.max(scores, axis=0, keepdims=True))
        share = 1.0 / jnp.sum(raised, axis=0, keepdims=True)
        weight = (raised * share).astype(jnp.bfloat16)
        mixed = jnp.dot(
            values_across[first : first + HD, :], weight, preferred_element_type=jnp.float32
        ).astype(jnp.bfloat16)
        attended_ref[first : first + HD, :] = mixed
        relative = turn((head // 2) ^ (me // 2), core)
        sent[relative, head % 2 * HD : (head % 2 + 1) * HD, :] = mixed
    for b in range(pairs):
        sent_refs[b][...] = sent[b]


def attend_ordered(kept, given, qkv, pairs):
    rows = qkv.shape[0]
    inner = qkv.shape[1] // 3
    heads = inner // pairs
    return pl.pallas_call(
        attend_kernel,
        out_shape=(jax.ShapeDtypeStruct((inner, rows), jnp.bfloat16),)
        + (jax.ShapeDtypeStruct((heads, rows), jnp.bfloat16),) * pairs,
        in_specs=[VMEM] * 3,
        out_specs=(VMEM,) * (1 + pairs),
        scratch_shapes=[pltpu.VMEM((pairs, heads, rows), jnp.bfloat16)],
        compiler_params=params(24),
        cost_estimate=cost(4 * rows * rows * inner, 6 * rows * inner),
        name="attend",
    )(kept, given, qkv)


def project_kernel(attended_ref, ordered_ref, w_ref, *encoded_refs):
    added = lax.dot_general(
        attended_ref[...], w_ref[...], TRANSPOSED, preferred_element_type=jnp.float32
    )
    encoded = (ordered_ref[...].astype(jnp.float32) + added).astype(jnp.bfloat16)
    size = ordered_ref.shape[0] // len(encoded_refs)
    for b, ref in enumerate(encoded_refs):
        ref[...] = encoded[b * size : (b + 1) * size]


def project_ordered(attended, ordered, w_out, pairs):
    rows, width = ordered.shape
    return pl.pallas_call(
        project_kernel,
        out_shape=(jax.ShapeDtypeStruct((rows // pairs, width), jnp.bfloat16),) * pairs,
        in_specs=[VMEM] * 3,
        out_specs=(VMEM,) * pairs,
        compiler_params=params(16),
        cost_estimate=cost(2 * ordered.size * w_out.shape[0], 2 * w_out.size),
        name="project",
    )(attended, ordered, w_out)


def products(columns, blocks, places):
    left, right = [], []
    for b, o in places:
        size = columns[b].shape[1] // (1 << PAIR_BITS)
        r = b ^ o
        left.append(columns[b][:, r * size : (r + 1) * size])
        right.append(blocks[o][r * size : (r + 1) * size, :])
    return jnp.dot(
        jnp.concatenate(left, 1), jnp.concatenate(right, 0), preferred_element_type=jnp.float32
    )


def near_kernel(pairs, *refs):
    columns, blocks = refs[: pairs - 1], refs[pairs - 1 : -1]
    near = range(pairs - 1)
    refs[-1][...] = products(columns, blocks, [(b, o) for b in near for o in near])


def far_kernel(scale, pairs, *refs):
    columns, blocks, near_ref = refs[:pairs], refs[pairs : 2 * pairs], refs[2 * pairs]
    kept_ref, given_ref = refs[2 * pairs + 1 :]
    head = kept_ref.shape[0]
    last = pairs - 1
    places = [(last, o) for o in range(pairs)] + [(b, last) for b in range(last)]
    total = (near_ref[...] + products(columns, blocks, places)) * scale
    first = lax.axis_index("enc") % 2 == 0
    kept_ref[...] = jnp.where(first, total[:head], total[head:])
    given_ref[...] = jnp.where(first, total[head:], total[:head]).astype(jnp.bfloat16)


def near_rows(columns, blocks):
    heads, rows = columns[0].shape
    width = blocks[0].shape[1]
    return pl.pallas_call(
        functools.partial(near_kernel, len(columns) + 1),
        out_shape=jax.ShapeDtypeStruct((heads, width), jnp.float32),
        in_specs=[VMEM] * (len(columns) + len(blocks)),
        out_specs=VMEM,
        compiler_params=params(24),
        cost_estimate=cost(NEAR * heads * rows * len(blocks) * width, 2 * len(blocks) * rows * width),
        name="near_rows",
    )(*columns, *blocks)


def far_rows(columns, blocks, near, scale):
    heads, rows = columns[0].shape
    width = near.shape[1]
    return pl.pallas_call(
        functools.partial(far_kernel, scale, len(columns)),
        out_shape=(
            jax.ShapeDtypeStruct((heads // 2, width), jnp.float32),
            jax.ShapeDtypeStruct((heads // 2, width), jnp.bfloat16),
        ),
        in_specs=[VMEM] * (2 * len(columns) + 1),
        out_specs=(VMEM, VMEM),
        compiler_params=params(24),
        cost_estimate=cost(2 * heads * rows * width, 2 * rows * width),
        name="far_rows",
    )(*columns, *blocks, near)


def place_kernel(slots_ref, *refs):
    embeddings_ref = refs[-1]
    arrived = jnp.concatenate([ref[...] for ref in refs[:-1]], 0)
    rows, width = arrived.shape
    tokens = embeddings_ref.shape[0]
    row = iota((rows, tokens), 0)
    window_rows = rows // (2 * (len(refs) - 1))
    holds = slots_ref[...] == slot_of_row(row, lax.axis_index("enc"), window_rows)
    for j in range(MERGE):
        put = jnp.where(holds & (row % MERGE == j), 1.0, 0.0).astype(jnp.bfloat16)
        part = lax.dot_general(put, arrived, TRANSPOSED, preferred_element_type=jnp.float32)
        embeddings_ref[:, j * width : (j + 1) * width] = part.astype(jnp.bfloat16)


def place_rows(slot_token, arrived):
    size, width = arrived[0].shape
    rows = size * len(arrived)
    tokens = slot_token.shape[0]
    return pl.pallas_call(
        place_kernel,
        out_shape=jax.ShapeDtypeStruct((tokens, MERGE * width), jnp.bfloat16),
        in_specs=[VMEM] * (1 + len(arrived)),
        out_specs=VMEM,
        compiler_params=params(16),
        cost_estimate=cost(PLACE * MERGE * rows * tokens * width, 2 * MERGE * tokens * width),
        name="place_rows",
    )(slot_token.reshape(1, tokens), *arrived)


def add_kernel(split, *refs):
    ins = len(refs) - (2 if split else 1)
    sums = [
        refs[i][...].astype(jnp.float32) + refs[i + 1][...].astype(jnp.float32)
        for i in range(0, ins, 2)
    ]
    outs = refs[ins:]
    whole = sums[0] if len(sums) == 1 else jnp.concatenate(sums, 1)
    width = outs[0].shape[1]
    for i, ref in enumerate(outs):
        ref[...] = whole[:, i * width : (i + 1) * width].astype(ref.dtype)


def add_halves(terms, kind, split):
    rows = terms[0][0].shape[0]
    width = sum(pair[0].shape[1] for pair in terms)
    count = 2 if split else 1
    return pl.pallas_call(
        functools.partial(add_kernel, split),
        out_shape=(jax.ShapeDtypeStruct((rows, width // count), kind),) * count,
        in_specs=[VMEM] * (2 * len(terms)),
        out_specs=(VMEM,) * count,
        compiler_params=params(8),
        cost_estimate=cost(rows * width, 8 * rows * width),
        name="add_halves",
    )(*[value for pair in terms for value in pair])


def after(value, other):
    return lax.optimization_barrier((value, other))[0]


def swap(value, axis, bits):
    size = lax.axis_size(axis)
    return lax.ppermute(value, axis, [(i, i ^ bits) for i in range(size)])


def chip_swap(value, relative):
    size = lax.axis_size("enc")
    return lax.ppermute(value, "enc", [(i, i ^ 2 * turn(relative, i % 2)) for i in range(size)])


def xor_slice(pixels, window_owner, window_len, slot_token, cotangent, w_qkv, w_out, gain):
    group = lax.axis_size("enc")
    replicas = lax.axis_size("rep")
    pairs = group // 2
    rows = pixels.shape[0]

    held, kept, given = pick_rows(window_owner, window_len, slot_token, pixels, cotangent)
    given = swap(given, "enc", 1)
    qkv, ordered = qkv_ordered(kept, given, gain, w_qkv)
    attended, *sent = attend_ordered(kept, given, qkv, pairs)
    blocks = [held, chip_swap(held, 1), chip_swap(after(held, qkv), 2)]
    blocks.append(chip_swap(after(blocks[1], attended), 2))
    columns = [sent[0]] + [chip_swap(sent[b], b) for b in range(1, pairs)]
    encoded = project_ordered(attended, ordered, w_out, pairs)
    scale = 1.0 / math.sqrt(rows * group * replicas)
    near = near_rows(columns[:-1], blocks[:-1])
    mine, other = far_rows(columns, blocks, near, scale)
    halves = add_halves([(mine, swap(other, "enc", 1))], jnp.bfloat16, split=True)
    arrived = [encoded[0]]
    for b in range(1, pairs):
        arrived.append(chip_swap(after(encoded[b], halves[0]), b))
    bits = [1 << i for i in range(replicas.bit_length() - 1)]
    for first, last in zip(bits, bits[::-1]):
        done = first == bits[-1]
        swapped = [swap(halves[0], "rep", first), swap(halves[1], "rep", last)]
        halves = add_halves(
            list(zip(halves, swapped)), jnp.float32 if done else jnp.bfloat16, split=not done
        )
    total = halves[0]
    embeddings = place_rows(slot_token, arrived)
    return (embeddings, total)


def solution(mesh):
    def shards(*args):
        group = mesh.shape["enc"]
        replicas = mesh.shape["rep"]
        square = group == 2 << PAIR_BITS and replicas & (replicas - 1) == 0 and replicas > 1
        whole = square and args[1].shape[0] == group
        return (xor_slice if whole else any_slice)(*args)

    return jax.shard_map(
        shards,
        mesh=mesh,
        in_specs=(
            P(("enc", "rep"), None),
            P(("enc", "rep")),
            P(("enc", "rep")),
            P(("enc", "rep")),
            P(("enc", "rep"), None),
            P(),
            P(),
            P(),
        ),
        out_specs=(P(("enc", "rep"), None), P("enc", None)),
        check_vma=False,
    )
```

```python
import functools
import math

import jax
import jax.numpy as jnp
from jax import lax
from jax.experimental import pallas as pl
from jax.experimental.pallas import tpu as pltpu
from jax.sharding import PartitionSpec as P

HD = 80
HEADS = 8
MERGE = 4


def normalize(inputs, gain):
    values = inputs.astype(jnp.float32)
    mean_square = jnp.mean(values * values, axis=-1, keepdims=True)
    return (values * lax.rsqrt(mean_square + 1e-06) * gain).astype(jnp.bfloat16)


def attend(windows, lengths, w_qkv, gain):
    number, window_size, feature_width = windows.shape
    inner_width = w_qkv.shape[1] // 3
    flat_rows = windows.reshape(number * window_size, feature_width)
    normed = normalize(flat_rows, gain)
    projected = jnp.dot(normed, w_qkv, preferred_element_type=jnp.float32).astype(jnp.bfloat16)
    queries = projected[:, :inner_width].reshape(number, window_size, HEADS, HD)
    keys_all = projected[:, inner_width : 2 * inner_width].reshape(number, window_size, HEADS, HD)
    values_all = projected[:, 2 * inner_width :].reshape(number, window_size, HEADS, HD)
    scores = jnp.einsum(
        "nqhd,nkhd->nhqk", queries, keys_all, preferred_element_type=jnp.float32
    ) / math.sqrt(HD)
    live_keys = jnp.arange(window_size, dtype=jnp.int32)[None, :] < lengths[:, None]
    scores = jnp.where(live_keys[:, None, None, :], scores, -1e30)
    weights = jax.nn.softmax(scores, axis=-1).astype(jnp.bfloat16)
    attended = jnp.einsum(
        "nhqk,nkhd->nqhd", weights, values_all, preferred_element_type=jnp.float32
    )
    return attended.astype(jnp.bfloat16).reshape(number * window_size, inner_width)


def project(flat_rows, attended, w_out):
    encoded = flat_rows.astype(jnp.float32) + jnp.dot(
        attended, w_out, preferred_element_type=jnp.float32
    )
    return encoded.astype(jnp.bfloat16)


def any_slice(pixels, window_owner, window_len, slot_token, cotangent, w_qkv, w_out, gain):
    group_size = lax.axis_size("enc")
    replica_count = lax.axis_size("rep")
    feature_width = pixels.shape[1]
    window_count = window_owner.shape[0]
    window_rows = pixels.shape[0] // window_count
    tokens_each = window_rows // MERGE
    merged_width = MERGE * feature_width
    owner_ids = jnp.arange(group_size, dtype=jnp.int32)
    route = (window_owner[None, :] == owner_ids[:, None]).astype(jnp.bfloat16)
    slot_ids = jnp.arange(group_size * tokens_each, dtype=jnp.int32)
    placing = (slot_token[:, None] == slot_ids[None, :]).astype(jnp.bfloat16)
    attended = attend(
        pixels.reshape(window_count, window_rows, feature_width), window_len, w_qkv, gain
    )
    encoded = project(pixels, attended, w_out)
    outgoing = jnp.dot(
        route,
        encoded.reshape(window_count, window_rows * feature_width),
        preferred_element_type=jnp.float32,
    )
    outgoing = outgoing.astype(jnp.bfloat16).reshape(group_size, tokens_each, merged_width)
    arrived = lax.all_to_all(outgoing, "enc", split_axis=0, concat_axis=0, tiled=True)
    embeddings = jnp.dot(
        placing,
        arrived.reshape(group_size * tokens_each, merged_width),
        preferred_element_type=jnp.float32,
    ).astype(jnp.bfloat16)
    returning = lax.dot_general(
        placing, cotangent, (((0,), (0,)), ((), ())), preferred_element_type=jnp.float32
    )
    returning = returning.astype(jnp.bfloat16).reshape(group_size, tokens_each, merged_width)
    answered = lax.all_to_all(returning, "enc", split_axis=0, concat_axis=0, tiled=True)
    d_encoded = lax.dot_general(
        route,
        answered.reshape(group_size, tokens_each * merged_width),
        (((0,), (0,)), ((), ())),
        preferred_element_type=jnp.float32,
    )
    d_encoded = d_encoded.astype(jnp.bfloat16).reshape(window_count * window_rows, feature_width)
    reduced = lax.psum_scatter(
        lax.dot_general(
            attended, d_encoded, (((0,), (0,)), ((), ())), preferred_element_type=jnp.float32
        ),
        "enc",
        scatter_dimension=0,
        tiled=True,
    )
    summed = lax.psum(reduced, "rep")
    patch_total = window_count * window_rows * group_size * replica_count
    gradient = summed / math.sqrt(patch_total)
    return (embeddings, gradient)


LANES = 128
SUBLANES = 16
PAIR_BITS = 2
NEAR = 40
LATE = 2
PLACE = 200
VMEM = pl.BlockSpec(memory_space=pltpu.VMEM)
HBM = pl.BlockSpec(memory_space=pltpu.HBM)
SMEM = pl.BlockSpec(memory_space=pltpu.SMEM)
TRANSPOSED = (((0,), (0,)), ((), ()))
ROWS_WITH_ROWS = (((1,), (1,)), ((), ()))


def turn(relative, core):
    other = relative % 2 * 2 + relative // 2
    if isinstance(core, int):
        return other if core else relative
    return jnp.where(core == 1, other, relative)


def iota(shape, dim):
    return lax.broadcasted_iota(jnp.int32, shape, dim)


def cost(flops, moved):
    return pl.CostEstimate(flops=flops, bytes_accessed=moved, transcendentals=0)


def params(mib):
    return pltpu.CompilerParams(vmem_limit_bytes=mib * 1024 * 1024)


def in_hbm(value):
    return pltpu.with_memory_space_constraint(value, pltpu.HBM)


def in_vmem(value):
    return pltpu.with_memory_space_constraint(value, pltpu.VMEM)


def place(index, size):
    return pl.ds(pl.multiple_of(index * size, size), size)


def slot_of_row(row, me, window_rows):
    pair = turn(row // (2 * window_rows), me % 2) ^ (me // 2)
    source = pair * 2 + row // window_rows % 2
    return source * (window_rows // MERGE) + row % window_rows // MERGE


def pick_kernel(
    owner_hbm, len_hbm, slots_hbm, pixels_hbm, cotangent_hbm, held_ref, kept_ref, given_ref,
    owner_ref, len_ref, slots_ref, pixels_buf, parts, windows_buf, sems,
):
    rows, width = held_ref.shape
    tokens = cotangent_hbm.shape[0]
    windows = owner_ref.shape[0]
    window_rows = rows // windows
    me = lax.axis_index("enc")
    pairs_of_refs = [
        (owner_hbm, owner_ref),
        (len_hbm, len_ref),
        (slots_hbm, slots_ref),
        (pixels_hbm, pixels_buf),
    ]
    for j in range(MERGE):
        pairs_of_refs.append((cotangent_hbm.at[:, pl.ds(j * width, width)], parts.at[j]))
    copies = [
        pltpu.make_async_copy(source, target, sems.at[i])
        for i, (source, target) in enumerate(pairs_of_refs)
    ]
    for copy in copies:
        copy.start()
    for i in (0, 1, 3):
        copies[i].wait()
    which = iota((SUBLANES, width), 0)
    lengths = [jnp.zeros((SUBLANES, width), jnp.int32)] * 2
    for w in range(windows):
        owner = owner_ref[w]
        across = (owner + me) % 2
        relative = turn((owner // 2) ^ (me // 2), owner % 2)
        windows_buf[across, place(relative, window_rows), :] = pixels_buf[
            w * window_rows : (w + 1) * window_rows, :
        ]
        for side in range(2):
            here = jnp.where(across == side, relative, -1)
            lengths[side] = jnp.where(which == here, len_ref[w], lengths[side])
    for side, ref in enumerate((kept_ref, given_ref)):
        ref[: rows // 2, :] = windows_buf[side]
        ref[rows // 2 :, :] = lengths[side].astype(jnp.float32).astype(jnp.bfloat16)
    row = iota((rows, tokens), 0)
    copies[2].wait()
    holds = slots_ref[...] == slot_of_row(row, me, window_rows)
    picks = [
        jnp.where(holds & (row % MERGE == j), 1.0, 0.0).astype(jnp.bfloat16) for j in range(MERGE)
    ]
    held = None
    for j in range(MERGE):
        copies[4 + j].wait()
        term = jnp.dot(picks[j], parts[j], preferred_element_type=jnp.float32)
        held = term if held is None else held + term
    held_ref[...] = held.astype(jnp.bfloat16)

def pick_rows(window_owner, window_len, slot_token, pixels, cotangent):
    rows, width = pixels.shape
    tokens = cotangent.shape[0]
    half = jax.ShapeDtypeStruct((rows // 2 + SUBLANES, width), jnp.bfloat16)
    return pl.pallas_call(
        pick_kernel,
        out_shape=(jax.ShapeDtypeStruct((rows, width), jnp.bfloat16), half, half),
        in_specs=[HBM] * 5,
        out_specs=(VMEM, VMEM, VMEM),
        scratch_shapes=[
            pltpu.SMEM(window_owner.shape, jnp.int32),
            pltpu.SMEM(window_len.shape, jnp.int32),
            pltpu.VMEM((1, tokens), jnp.int32),
            pltpu.VMEM((rows, width), jnp.bfloat16),
            pltpu.VMEM((MERGE, tokens, width), jnp.bfloat16),
            pltpu.VMEM((2, rows // 2, width), jnp.bfloat16),
            pltpu.SemaphoreType.DMA((MERGE + 4,)),
        ],
        compiler_params=params(16),
        cost_estimate=cost(200 * MERGE * rows * tokens * width, 2 * cotangent.size),
        name="pick_rows",
    )(
        in_hbm(window_owner),
        in_hbm(window_len),
        in_hbm(slot_token.reshape(1, tokens)),
        in_hbm(pixels),
        in_hbm(cotangent),
    )


def qkv_kernel(kept_ref, given_ref, gain_ref, w_ref, qkv_ref, ordered_ref):
    rows = ordered_ref.shape[0]
    pairs = 1 << PAIR_BITS
    window_rows = rows // (2 * pairs)
    core = lax.axis_index("enc") % 2
    for ref, side in ((kept_ref, core), (given_ref, 1 - core)):
        for b in range(pairs):
            ordered_ref[place(2 * b + side, window_rows), :] = ref[
                b * window_rows : (b + 1) * window_rows, :
            ]
    values = ordered_ref[...].astype(jnp.float32)
    mean_square = jnp.mean(values * values, axis=-1, keepdims=True)
    normed = (values * lax.rsqrt(mean_square + 1e-06) * gain_ref[...][None, :]).astype(
        jnp.bfloat16
    )
    inner = w_ref.shape[1] // 3
    for part in range(3):
        columns = slice(part * inner, (part + 1) * inner)
        qkv_ref[:, columns] = jnp.dot(
            normed, w_ref[:, columns], preferred_element_type=jnp.float32
        ).astype(jnp.bfloat16)


def qkv_ordered(kept, given, gain, w_qkv):
    width = kept.shape[1]
    rows = 2 * (kept.shape[0] - SUBLANES)
    return pl.pallas_call(
        qkv_kernel,
        out_shape=(
            jax.ShapeDtypeStruct((rows, w_qkv.shape[1]), jnp.bfloat16),
            jax.ShapeDtypeStruct((rows, width), jnp.bfloat16),
        ),
        in_specs=[VMEM] * 4,
        out_specs=(VMEM,) * 2,
        compiler_params=params(24),
        cost_estimate=cost(2 * rows * w_qkv.size, 2 * w_qkv.size),
        name="qkv",
    )(kept, given, in_hbm(gain), in_vmem(w_qkv))


def attend_kernel(kept_ref, given_ref, qkv_ref, *refs):
    attended_ref, sent_refs, sent = refs[0], refs[1:-1], refs[-1]
    rows = qkv_ref.shape[0]
    pairs = len(sent_refs)
    window_rows = rows // (2 * pairs)
    inner = attended_ref.shape[0]
    me = lax.axis_index("enc")
    core = me % 2
    key_row = iota((rows, rows), 0)
    key_window = key_row // window_rows
    live = jnp.zeros((rows, rows), jnp.float32)
    for ref, side in ((kept_ref, core), (given_ref, 1 - core)):
        lengths = ref[rows // 2 :, :rows].astype(jnp.float32)
        for b in range(pairs):
            live = jnp.where(key_window == 2 * b + side, lengths[b : b + 1], live)
    allowed = (key_window == iota((rows, rows), 1) // window_rows) & (
        (key_row % window_rows).astype(jnp.float32) < live
    )
    values_across = qkv_ref[:, 2 * inner :].astype(jnp.float32).T.astype(jnp.bfloat16)
    scale = 1.0 / math.sqrt(HD)
    for head in range(inner // HD):
        first = head * HD
        low = first // LANES * LANES
        high = -(-(first + HD) // LANES) * LANES
        lane = iota((rows, high - low), 1) + low
        own = (lane >= first) & (lane < first + HD)
        keys = qkv_ref[:, inner + low : inner + high]
        keys = jnp.where(own, keys, jnp.zeros((), jnp.bfloat16))
        scores = lax.dot_general(
            keys, qkv_ref[:, low:high], ROWS_WITH_ROWS, preferred_element_type=jnp.float32
        )
        scores = jnp.where(allowed, scores * scale, -1e30)
        raised = jnp.exp(scores - jnp.max(scores, axis=0, keepdims=True))
        weight = (raised / jnp.sum(raised, axis=0, keepdims=True)).astype(jnp.bfloat16)
        mixed = jnp.dot(
            values_across[first : first + HD, :], weight, preferred_element_type=jnp.float32
        ).astype(jnp.bfloat16)
        attended_ref[first : first + HD, :] = mixed
        relative = turn((head // 2) ^ (me // 2), core)
        sent[relative, head % 2 * HD : (head % 2 + 1) * HD, :] = mixed
    for b in range(pairs):
        sent_refs[b][...] = sent[b]


def attend_ordered(kept, given, qkv, pairs):
    rows = qkv.shape[0]
    inner = qkv.shape[1] // 3
    heads = inner // pairs
    return pl.pallas_call(
        attend_kernel,
        out_shape=(jax.ShapeDtypeStruct((inner, rows), jnp.bfloat16),)
        + (jax.ShapeDtypeStruct((heads, rows), jnp.bfloat16),) * pairs,
        in_specs=[VMEM] * 3,
        out_specs=(VMEM,) * (1 + pairs),
        scratch_shapes=[pltpu.VMEM((pairs, heads, rows), jnp.bfloat16)],
        compiler_params=params(24),
        cost_estimate=cost(4 * rows * rows * inner, 6 * rows * inner),
        name="attend",
    )(kept, given, qkv)


def project_kernel(attended_ref, ordered_ref, w_ref, *encoded_refs):
    added = lax.dot_general(
        attended_ref[...], w_ref[...], TRANSPOSED, preferred_element_type=jnp.float32
    )
    encoded = (ordered_ref[...].astype(jnp.float32) + added).astype(jnp.bfloat16)
    size = ordered_ref.shape[0] // len(encoded_refs)
    for b, ref in enumerate(encoded_refs):
        ref[...] = encoded[b * size : (b + 1) * size]


def project_ordered(attended, ordered, w_out, pairs):
    rows, width = ordered.shape
    return pl.pallas_call(
        project_kernel,
        out_shape=(jax.ShapeDtypeStruct((rows // pairs, width), jnp.bfloat16),) * pairs,
        in_specs=[VMEM] * 3,
        out_specs=(VMEM,) * pairs,
        compiler_params=params(16),
        cost_estimate=cost(2 * ordered.size * w_out.shape[0], 2 * w_out.size),
        name="project",
    )(attended, ordered, w_out)


def products(columns, blocks, places):
    left, right = [], []
    for b, o in places:
        size = columns[b].shape[1] // (1 << PAIR_BITS)
        r = b ^ o
        left.append(columns[b][:, r * size : (r + 1) * size])
        right.append(blocks[o][r * size : (r + 1) * size, :])
    return jnp.dot(
        jnp.concatenate(left, 1), jnp.concatenate(right, 0), preferred_element_type=jnp.float32
    )


def near_kernel(pairs, *refs):
    early = [b for b in range(pairs) if b != LATE]
    columns, blocks = dict(zip(early, refs)), refs[pairs - 1 : -1]
    refs[-1][...] = products(columns, blocks, [(b, o) for b in early for o in range(pairs - 1)])


def far_kernel(scale, pairs, *refs):
    columns, blocks, near_ref = refs[:pairs], refs[pairs : 2 * pairs], refs[2 * pairs]
    kept_ref, given_ref = refs[2 * pairs + 1 :]
    head = kept_ref.shape[0]
    last = pairs - 1
    places = [(LATE, o) for o in range(pairs)]
    places += [(b, last) for b in range(pairs) if b != LATE]
    total = (near_ref[...] + products(columns, blocks, places)) * scale
    first = lax.axis_index("enc") % 2 == 0
    kept_ref[...] = jnp.where(first, total[:head], total[head:])
    given_ref[...] = jnp.where(first, total[head:], total[:head]).astype(jnp.bfloat16)


def near_rows(columns, blocks):
    heads, rows = columns[0].shape
    width = blocks[0].shape[1]
    return pl.pallas_call(
        functools.partial(near_kernel, len(columns) + 1),
        out_shape=jax.ShapeDtypeStruct((heads, width), jnp.float32),
        in_specs=[VMEM] * (len(columns) + len(blocks)),
        out_specs=VMEM,
        compiler_params=params(24),
        cost_estimate=cost(NEAR * heads * rows * len(blocks) * width, 2 * len(blocks) * rows * width),
        name="near_rows",
    )(*columns, *blocks)


def far_rows(columns, blocks, near, scale):
    heads, rows = columns[0].shape
    width = near.shape[1]
    return pl.pallas_call(
        functools.partial(far_kernel, scale, len(columns)),
        out_shape=(
            jax.ShapeDtypeStruct((heads // 2, width), jnp.float32),
            jax.ShapeDtypeStruct((heads // 2, width), jnp.bfloat16),
        ),
        in_specs=[VMEM] * (2 * len(columns) + 1),
        out_specs=(VMEM, VMEM),
        compiler_params=params(24),
        cost_estimate=cost(2 * heads * rows * width, 2 * rows * width),
        name="far_rows",
    )(*columns, *blocks, near)


def place_kernel(slots_ref, *refs):
    embeddings_ref = refs[-1]
    arrived = jnp.concatenate([ref[...] for ref in refs[:-1]], 0)
    rows, width = arrived.shape
    tokens = embeddings_ref.shape[0]
    row = iota((rows, tokens), 0)
    window_rows = rows // (2 * (len(refs) - 1))
    holds = slots_ref[...] == slot_of_row(row, lax.axis_index("enc"), window_rows)
    for j in range(MERGE):
        put = jnp.where(holds & (row % MERGE == j), 1.0, 0.0).astype(jnp.bfloat16)
        part = lax.dot_general(put, arrived, TRANSPOSED, preferred_element_type=jnp.float32)
        embeddings_ref[:, j * width : (j + 1) * width] = part.astype(jnp.bfloat16)


def place_rows(slot_token, arrived):
    size, width = arrived[0].shape
    rows = size * len(arrived)
    tokens = slot_token.shape[0]
    return pl.pallas_call(
        place_kernel,
        out_shape=jax.ShapeDtypeStruct((tokens, MERGE * width), jnp.bfloat16),
        in_specs=[VMEM] * (1 + len(arrived)),
        out_specs=VMEM,
        compiler_params=params(16),
        cost_estimate=cost(PLACE * MERGE * rows * tokens * width, 2 * MERGE * tokens * width),
        name="place_rows",
    )(slot_token.reshape(1, tokens), *arrived)


def add_kernel(split, *refs):
    ins = len(refs) - (2 if split else 1)
    sums = [
        refs[i][...].astype(jnp.float32) + refs[i + 1][...].astype(jnp.float32)
        for i in range(0, ins, 2)
    ]
    outs = refs[ins:]
    whole = sums[0] if len(sums) == 1 else jnp.concatenate(sums, 1)
    width = outs[0].shape[1]
    for i, ref in enumerate(outs):
        ref[...] = whole[:, i * width : (i + 1) * width].astype(ref.dtype)


def add_halves(terms, kind, split):
    rows = terms[0][0].shape[0]
    width = sum(pair[0].shape[1] for pair in terms)
    count = 2 if split else 1
    return pl.pallas_call(
        functools.partial(add_kernel, split),
        out_shape=(jax.ShapeDtypeStruct((rows, width // count), kind),) * count,
        in_specs=[VMEM] * (2 * len(terms)),
        out_specs=(VMEM,) * count,
        compiler_params=params(8),
        cost_estimate=cost(rows * width, 8 * rows * width),
        name="add_halves",
    )(*[value for pair in terms for value in pair])


def after(value, other):
    return lax.optimization_barrier((value, other))[0]


def swap(value, axis, bits):
    size = lax.axis_size(axis)
    return lax.ppermute(value, axis, [(i, i ^ bits) for i in range(size)])


def chip_swap(value, relative):
    size = lax.axis_size("enc")
    return lax.ppermute(value, "enc", [(i, i ^ 2 * turn(relative, i % 2)) for i in range(size)])


def xor_slice(pixels, window_owner, window_len, slot_token, cotangent, w_qkv, w_out, gain):
    group = lax.axis_size("enc")
    replicas = lax.axis_size("rep")
    pairs = group // 2
    rows = pixels.shape[0]

    held, kept, given = pick_rows(window_owner, window_len, slot_token, pixels, cotangent)
    given = swap(given, "enc", 1)
    qkv, ordered = qkv_ordered(kept, given, gain, w_qkv)
    attended, *sent = attend_ordered(kept, given, qkv, pairs)
    blocks = [held, chip_swap(held, 1), chip_swap(after(held, qkv), 2)]
    blocks.append(chip_swap(after(blocks[1], attended), 2))
    columns = [sent[0]] + [chip_swap(sent[b], b) for b in range(1, pairs)]
    encoded = project_ordered(attended, ordered, w_out, pairs)
    scale = 1.0 / math.sqrt(rows * group * replicas)
    near = near_rows([columns[b] for b in range(pairs) if b != LATE], blocks[:-1])
    mine, other = far_rows(columns, blocks, near, scale)
    halves = add_halves([(mine, swap(other, "enc", 1))], jnp.bfloat16, split=True)
    arrived = [encoded[0]]
    for b in range(1, pairs):
        arrived.append(chip_swap(after(encoded[b], halves[0]), b))
    bits = [1 << i for i in range(replicas.bit_length() - 1)]
    for first, last in zip(bits, bits[::-1]):
        done = first == bits[-1]
        swapped = [swap(halves[0], "rep", first), swap(halves[1], "rep", last)]
        halves = add_halves(
            list(zip(halves, swapped)), jnp.float32 if done else jnp.bfloat16, split=not done
        )
    total = halves[0]
    embeddings = place_rows(slot_token, arrived)
    return (embeddings, total)


def solution(mesh):
    def shards(*args):
        group = mesh.shape["enc"]
        replicas = mesh.shape["rep"]
        square = group == 2 << PAIR_BITS and replicas & (replicas - 1) == 0 and replicas > 1
        whole = square and args[1].shape[0] == group
        return (xor_slice if whole else any_slice)(*args)

    return jax.shard_map(
        shards,
        mesh=mesh,
        in_specs=(
            P(("enc", "rep"), None),
            P(("enc", "rep")),
            P(("enc", "rep")),
            P(("enc", "rep")),
            P(("enc", "rep"), None),
            P(),
            P(),
            P(),
        ),
        out_specs=(P(("enc", "rep"), None), P("enc", None)),
        check_vma=False,
    )
```
